32 devices in a mesh: dp: 8 (over y, x, core), mp: 4 (over z).
Axes of the slice: x: 2, y: 2, z: 4, core: 2. Of those that a mesh axis runs over, the one named last changes fastest.
Arguments:
- encoder_input: bfloat16 [4096, 768], P(('dp', 'mp')), may hold values from -6 to 6
- encoder_upstream: bfloat16 [4096, 768], P(('dp', 'mp')), may hold values from -6 to 6
- memory_index: int32 [64, 10], P('dp'), may hold values from 0 to 1023
- memory_table: bfloat16 [1024, 2, 768], replicated, may hold values from -6 to 6
- encoder_bucket: int32 [64, 64], replicated, may hold values from 0 to 31
- encoder_bias: float32 [32, 12], replicated, may hold values from -4 to 4
- encoder_gain: float32 [768], replicated, may hold values from 0.5 to 1.5
- encoder_query: bfloat16 [768, 768], P(None, 'mp'), may hold values from -0.0546875 to 0.0546875
- encoder_key: bfloat16 [768, 768], P(None, 'mp'), may hold values from -0.21875 to 0.21875
- encoder_value: bfloat16 [768, 768], P(None, 'mp'), may hold values from -0.21875 to 0.21875
- encoder_merge: bfloat16 [768, 768], P('mp'), may hold values from -0.4375 to 0.4375
- encoder_later_gain: float32 [768], replicated, may hold values from 0.5 to 1.5
- encoder_widen: bfloat16 [768, 3072], P(None, 'mp'), may hold values from -0.21875 to 0.21875
- encoder_narrow: bfloat16 [3072, 768], P('mp'), may hold values from -0.15625 to 0.15625
- decoder_input: bfloat16 [4096, 768], P(('dp', 'mp')), may hold values from -6 to 6
- decoder_upstream: bfloat16 [4096, 768], P(('dp', 'mp')), may hold values from -6 to 6
- encoder_states: bfloat16 [4096, 768], P(('dp', 'mp')), may hold values from -6 to 6
- decoder_bucket: int32 [64, 64], replicated, may hold values from 0 to 31
- decoder_bias: float32 [32, 12], replicated, may hold values from -4 to 4
- decoder_gain: float32 [768], replicated, may hold values from 0.5 to 1.5
- decoder_query: bfloat16 [768, 768], P(None, 'mp'), may hold values from -0.0546875 to 0.0546875
- decoder_key: bfloat16 [768, 768], P(None, 'mp'), may hold values from -0.21875 to 0.21875
- decoder_value: bfloat16 [768, 768], P(None, 'mp'), may hold values from -0.21875 to 0.21875
- decoder_merge: bfloat16 [768, 768], P('mp'), may hold values from -0.4375 to 0.4375
- cross_gain: float32 [768], replicated, may hold values from 0.5 to 1.5
- cross_query: bfloat16 [768, 768], P(None, 'mp'), may hold values from -0.0546875 to 0.0546875
- cross_key: bfloat16 [768, 768], P(None, 'mp'), may hold values from -0.21875 to 0.21875
- cross_value: bfloat16 [768, 768], P(None, 'mp'), may hold values from -0.21875 to 0.21875
- cross_merge: bfloat16 [768, 768], P('mp'), may hold values from -0.4375 to 0.4375
- decoder_later_gain: float32 [768], replicated, may hold values from 0.5 to 1.5
- decoder_widen: bfloat16 [768, 3072], P(None, 'mp'), may hold values from -0.21875 to 0.21875
- decoder_narrow: bfloat16 [3072, 768], P('mp'), may hold values from -0.15625 to 0.15625
Outputs:
- encoder_output: bfloat16 [4096, 768], P(('dp', 'mp'))
- encoder_input_grad: float32 [4096, 768], P(('dp', 'mp'))
- memory_table_grad: float32 [1024, 2, 768], P(('dp', 'mp'))
- encoder_bias_grad: float32 [32, 12], replicated
- encoder_gain_grad: float32 [768], replicated
- encoder_query_grad: float32 [768, 768], P('dp', 'mp')
- encoder_key_grad: float32 [768, 768], P('dp', 'mp')
- encoder_value_grad: float32 [768, 768], P('dp', 'mp')
- encoder_merge_grad: float32 [768, 768], P('mp', 'dp')
- encoder_later_gain_grad: float32 [768], replicated
- encoder_widen_grad: float32 [768, 3072], P('dp', 'mp')
- encoder_narrow_grad: float32 [3072, 768], P('mp', 'dp')
- decoder_output: bfloat16 [4096, 768], P(('dp', 'mp'))
- decoder_input_grad: float32 [4096, 768], P(('dp', 'mp'))
- encoder_states_grad: float32 [4096, 768], P(('dp', 'mp'))
- decoder_bias_grad: float32 [32, 12], replicated
- decoder_gain_grad: float32 [768], replicated
- decoder_query_grad: float32 [768, 768], P('dp', 'mp')
- decoder_key_grad: float32 [768, 768], P('dp', 'mp')
- decoder_value_grad: float32 [768, 768], P('dp', 'mp')
- decoder_merge_grad: float32 [768, 768], P('mp', 'dp')
- cross_gain_grad: float32 [768], replicated
- cross_query_grad: float32 [768, 768], P('dp', 'mp')
- cross_key_grad: float32 [768, 768], P('dp', 'mp')
- cross_value_grad: float32 [768, 768], P('dp', 'mp')
- cross_merge_grad: float32 [768, 768], P('mp', 'dp')
- decoder_later_gain_grad: float32 [768], replicated
- decoder_widen_grad: float32 [768, 3072], P('dp', 'mp')
- decoder_narrow_grad: float32 [3072, 768], P('mp', 'dp')
The draws below stay inside these ranges and needn't reach their ends.
All inputs are finite; a program needn't handle non-finite values.
Results may differ from the reference program's by a relative error of at most 0.024.
The reference program's roundings to bfloat16 on the way count: a program that leaves them out, or rounds other values in their place, can miss the bound.
Values may be sent and summed in bfloat16 or wider, within the bound.
No kernel may reach another device: no remote copies, remote signals or barrier semaphores. Data moves between devices by JAX's collectives and lax.ppermute only.
A program may use at most 192 MiB of HBM per device.

```python
import jax
import jax.numpy as jnp
from jax import lax

D = 768
H = 12
DH = 64
FF = 3072
BUCKETS = 32
SEQ = 64
MEMK = 10
PREFIX = 2
MEM = 1024
SEQS = 8
TOKENS = 4096
QUESTIONS = 64
N_DP = 8


def touch_ends(result, own_key, least, largest):
    index_at = [jax.random.randint(jax.random.fold_in(own_key, axis), (), 0, length) for axis, length in enumerate(result.shape)]
    main_axis = result.shape.index(max(result.shape))
    next_to = index_at[:main_axis] + [(index_at[main_axis] + 1) % result.shape[main_axis]] + index_at[main_axis + 1:]
    return result.at[tuple(index_at)].set(least).at[tuple(next_to)].set(largest)


def steps_of(stream_key, shape, split, smallest, largest):
    factor_of = 1.0
    for dim, parts in split:
        heights = jax.random.uniform(jax.random.fold_in(jax.random.fold_in(stream_key, 6), dim), (parts,), jnp.float32, smallest / len(split), largest / len(split))
        factor_of = factor_of * jnp.repeat(jnp.exp(heights), shape[dim] // parts).reshape((-1,) + (1,) * (len(shape) - 1 - dim))
    return factor_of


def gaussian(stream_key, shape, deviation, most, split=(), kind=jnp.bfloat16):
    loudness = steps_of(stream_key, shape, split, -0.22, 0.18) if split else 1.0
    values = jax.random.normal(stream_key, shape, jnp.float32) * deviation * loudness
    return jnp.minimum(jnp.maximum(values, -most), most).astype(kind)


def setup_inputs(seed: int = 0) -> dict:
    seeds = jax.random.split(jax.random.key(seed), 33)
    encoder_input = gaussian(seeds[0], (TOKENS, D), 1.0, 6.0, ((0, 32),))
    encoder_upstream = gaussian(seeds[1], (TOKENS, D), 1.0, 6.0, ((0, 32),))
    memory_index = touch_ends(jax.random.randint(seeds[2], (QUESTIONS, MEMK), 0, MEM), jax.random.fold_in(seeds[2], 1), 0, MEM - 1).astype(jnp.int32)
    memory_table = gaussian(seeds[3], (MEM, PREFIX, D), 1.0, 6.0)
    encoder_bucket = touch_ends(jax.random.randint(seeds[4], (SEQ, SEQ), 0, BUCKETS), jax.random.fold_in(seeds[4], 1), 0, BUCKETS - 1).astype(jnp.int32)
    encoder_bias = gaussian(seeds[5], (BUCKETS, H), 1.0, 4.0, (), jnp.float32)
    encoder_gain = jnp.clip(1.0 + 0.1 * jax.random.normal(seeds[6], (D,), jnp.float32), 0.5, 1.5)
    encoder_query = gaussian(seeds[7], (D, H * DH), (16 * D) ** -0.5, 0.0546875, ((1, 4),))
    encoder_key = gaussian(seeds[8], (D, H * DH), D ** -0.5, 0.21875, ((1, 4),))
    encoder_value = gaussian(seeds[9], (D, H * DH), D ** -0.5, 0.21875, ((1, 4),))
    encoder_merge = gaussian(seeds[10], (H * DH, D), (D // 4) ** -0.5, 0.4375, ((0, 4),))
    encoder_later_gain = jnp.clip(1.0 + 0.1 * jax.random.normal(seeds[11], (D,), jnp.float32), 0.5, 1.5)
    encoder_widen = gaussian(seeds[12], (D, FF), D ** -0.5, 0.21875, ((1, 4),))
    encoder_narrow = gaussian(seeds[13], (FF, D), (FF // 2) ** -0.5, 0.15625, ((0, 4),))
    decoder_input = gaussian(seeds[14], (TOKENS, D), 1.0, 6.0, ((0, 32),))
    decoder_upstream = gaussian(seeds[15], (TOKENS, D), 1.0, 6.0, ((0, 32),))
    encoder_states = gaussian(seeds[16], (TOKENS, D), 1.0, 6.0, ((0, 32),))
    decoder_bucket = touch_ends(jax.random.randint(seeds[17], (SEQ, SEQ), 0, BUCKETS), jax.random.fold_in(seeds[17], 1), 0, BUCKETS - 1).astype(jnp.int32)
    decoder_bias = gaussian(seeds[18], (BUCKETS, H), 1.0, 4.0, (), jnp.float32)
    decoder_gain = jnp.clip(1.0 + 0.1 * jax.random.normal(seeds[19], (D,), jnp.float32), 0.5, 1.5)
    decoder_query = gaussian(seeds[20], (D, H * DH), (16 * D) ** -0.5, 0.0546875, ((1, 4),))
    decoder_key = gaussian(seeds[21], (D, H * DH), D ** -0.5, 0.21875, ((1, 4),))
    decoder_value = gaussian(seeds[22], (D, H * DH), D ** -0.5, 0.21875, ((1, 4),))
    decoder_merge = gaussian(seeds[23], (H * DH, D), (D // 4) ** -0.5, 0.4375, ((0, 4),))
    cross_gain = jnp.clip(1.0 + 0.1 * jax.random.normal(seeds[24], (D,), jnp.float32), 0.5, 1.5)
    cross_query = gaussian(seeds[25], (D, H * DH), (16 * D) ** -0.5, 0.0546875, ((1, 4),))
    cross_key = gaussian(seeds[26], (D, H * DH), D ** -0.5, 0.21875, ((1, 4),))
    cross_value = gaussian(seeds[27], (D, H * DH), D ** -0.5, 0.21875, ((1, 4),))
    cross_merge = gaussian(seeds[28], (H * DH, D), (D // 4) ** -0.5, 0.4375, ((0, 4),))
    decoder_later_gain = jnp.clip(1.0 + 0.1 * jax.random.normal(seeds[29], (D,), jnp.float32), 0.5, 1.5)
    decoder_widen = gaussian(seeds[30], (D, FF), D ** -0.5, 0.21875, ((1, 4),))
    decoder_narrow = gaussian(seeds[31], (FF, D), (FF // 2) ** -0.5, 0.15625, ((0, 4),))
    return dict(encoder_input=encoder_input, encoder_upstream=encoder_upstream, memory_index=memory_index, memory_table=memory_table, encoder_bucket=encoder_bucket, encoder_bias=encoder_bias, encoder_gain=encoder_gain, encoder_query=encoder_query, encoder_key=encoder_key, encoder_value=encoder_value, encoder_merge=encoder_merge, encoder_later_gain=encoder_later_gain, encoder_widen=encoder_widen, encoder_narrow=encoder_narrow, decoder_input=decoder_input, decoder_upstream=decoder_upstream, encoder_states=encoder_states, decoder_bucket=decoder_bucket, decoder_bias=decoder_bias, decoder_gain=decoder_gain, decoder_query=decoder_query, decoder_key=decoder_key, decoder_value=decoder_value, decoder_merge=decoder_merge, cross_gain=cross_gain, cross_query=cross_query, cross_key=cross_key, cross_value=cross_value, cross_merge=cross_merge, decoder_later_gain=decoder_later_gain, decoder_widen=decoder_widen, decoder_narrow=decoder_narrow)


epsilon = 1e-06

@jax.custom_vjp
def low(v):
    return lax.optimization_barrier(v.astype(jnp.bfloat16)).astype(jnp.float32)

@jax.custom_vjp
def low_back(v):
    return v

def low_keep(v):
    return (low(v), None)

def low_pass(kept, grad):
    return (grad,)

def back_keep(v):
    return (v, None)

def back_low(kept, grad):
    return (low(grad),)
low.defvjp(low_keep, low_pass)
low_back.defvjp(back_keep, back_low)

def matmul_high(left, right):
    return jnp.dot(left, right, precision=lax.Precision.HIGHEST)

def rounded_both(value):
    return low(low_back(value))

def smooth_unit(value):
    return jax.nn.gelu(value, approximate=True)

def norm_apply(residual, norm_gain):
    return residual * lax.rsqrt(lax.optimization_barrier(jnp.mean(residual * residual, axis=-1, keepdims=True)) + epsilon) * norm_gain

def to_heads(rows, length):
    return rows.reshape(-1, length, H, DH)

def projected(rows, weight, length):
    return to_heads(rounded_both(matmul_high(rows, weight)), length)

def attend(queries, key_heads, value_heads, score_bias):
    scores = low_back(jnp.einsum('slhd,smhd->shlm', queries, key_heads, precision=lax.Precision.HIGHEST) + score_bias)
    chances = low(jax.nn.softmax(scores, axis=-1))
    mixture = jnp.einsum('shlm,smhd->slhd', chances, value_heads, precision=lax.Precision.HIGHEST)
    return rounded_both(mixture.reshape(-1, H * DH))

def relative(bias_table, bucket):
    return jnp.transpose(jnp.take(bias_table, bucket, axis=0), (2, 0, 1))

def feed_forward(residual, norm_gain, widen, narrow):
    normed = low(norm_apply(residual, norm_gain))
    hidden = low(smooth_unit(low_back(matmul_high(normed, widen))))
    return residual + low_back(matmul_high(hidden, narrow))

def encoder_block(weights_all, residual, index_rows, bucket):
    value_table, bias_table, norm_gain, w_query, w_key, w_value, w_merge, later_gain, widen, narrow = weights_all
    count = MEMK * PREFIX
    prefix = jnp.take(value_table, index_rows.reshape(-1), axis=0).reshape(-1, D)
    normed = low(norm_apply(residual, norm_gain))
    key_heads = jnp.concatenate([projected(prefix, w_key, count), projected(normed, w_key, SEQ)], axis=1)
    value_heads = jnp.concatenate([projected(prefix, w_value, count), projected(normed, w_value, SEQ)], axis=1)
    score_bias = jnp.concatenate([jnp.zeros((H, SEQ, count), jnp.float32), relative(bias_table, bucket)], axis=2)[None]
    mixture = attend(projected(normed, w_query, SEQ), key_heads, value_heads, score_bias)
    residual = residual + low_back(matmul_high(mixture, w_merge))
    return feed_forward(residual, later_gain, widen, narrow)

def decoder_block(weights_all, residual, states, bucket):
    bias_table, norm_gain, w_query, w_key, w_value, w_merge, cross_norm, c_query, c_key, c_value, c_merge, later_gain, widen, narrow = weights_all
    normed = low(norm_apply(residual, norm_gain))
    row_place = lax.broadcasted_iota(jnp.int32, (SEQ, SEQ), 0)
    col_place = lax.broadcasted_iota(jnp.int32, (SEQ, SEQ), 1)
    score_bias = jnp.where(col_place <= row_place, relative(bias_table, bucket), -1000000000.0)[None]
    mixture = attend(projected(normed, w_query, SEQ), projected(normed, w_key, SEQ), projected(normed, w_value, SEQ), score_bias)
    residual = residual + low_back(matmul_high(mixture, w_merge))
    normed = low(norm_apply(residual, cross_norm))
    mixture = attend(projected(normed, c_query, SEQ), projected(states, c_key, SEQ), projected(states, c_value, SEQ), jnp.zeros((1, 1, 1, 1), jnp.float32))
    residual = residual + low_back(matmul_high(mixture, c_merge))
    return feed_forward(residual, later_gain, widen, narrow)

def reference(encoder_input, encoder_upstream, memory_index, memory_table, encoder_bucket, encoder_bias, encoder_gain, encoder_query, encoder_key, encoder_value, encoder_merge, encoder_later_gain, encoder_widen, encoder_narrow, decoder_input, decoder_upstream, encoder_states, decoder_bucket, decoder_bias, decoder_gain, decoder_query, decoder_key, decoder_value, decoder_merge, cross_gain, cross_query, cross_key, cross_value, cross_merge, decoder_later_gain, decoder_widen, decoder_narrow):
    listed = (memory_table, encoder_bias, encoder_gain, encoder_query, encoder_key, encoder_value, encoder_merge, encoder_later_gain, encoder_widen, encoder_narrow, decoder_bias, decoder_gain, decoder_query, decoder_key, decoder_value, decoder_merge, cross_gain, cross_query, cross_key, cross_value, cross_merge, decoder_later_gain, decoder_widen, decoder_narrow)
    params = tuple((weight_item.astype(jnp.float32) for weight_item in listed))
    group_rows = SEQS * SEQ

    def grouped(array):
        return array.astype(jnp.float32).reshape(N_DP, group_rows, D)
    groups = (grouped(encoder_input), grouped(encoder_upstream), memory_index.reshape(N_DP, SEQS, MEMK), grouped(decoder_input), grouped(decoder_upstream), grouped(encoder_states))

    def one_group(carry, group):
        encoder_rows, encoder_grad_rows, index_rows, decoder_rows, decoder_grad_rows, state_rows = group

        def forward(weights_all, encoder_part, decoder_part, state_part):
            return (encoder_block(weights_all[:10], encoder_part, index_rows, encoder_bucket), decoder_block(weights_all[10:], decoder_part, state_part, decoder_bucket))
        outputs, pull = jax.vjp(forward, params, encoder_rows, decoder_rows, state_rows)
        grads = pull((encoder_grad_rows, decoder_grad_rows))
        carry = jax.tree.map(jnp.add, carry, grads[0])
        return (carry, (outputs[0], outputs[1], grads[1], grads[2], grads[3]))
    totals, stacked = lax.scan(one_group, jax.tree.map(jnp.zeros_like, params), groups)

    def whole(array):
        return array.reshape(TOKENS, D)
    return (whole(stacked[0]).astype(jnp.bfloat16), whole(stacked[2]), totals[0], totals[1], totals[2], totals[3], totals[4], totals[5], totals[6], totals[7], totals[8], totals[9], whole(stacked[1]).astype(jnp.bfloat16), whole(stacked[3]), whole(stacked[4]), totals[10], totals[11], totals[12], totals[13], totals[14], totals[15], totals[16], totals[17], totals[18], totals[19], totals[20], totals[21], totals[22], totals[23])
```

```python
import functools

import jax
import jax.numpy as jnp
from jax import lax
from jax.experimental import pallas as pl
from jax.experimental.pallas import tpu as pltpu
from jax.sharding import PartitionSpec as P

DH = 64
SEQ = 64
MEMK = 10
PREFIX = 2
EPS = 1e-06
NEG = -1e30
BLOCKS = 8
bf16 = jnp.bfloat16
f32 = jnp.float32
VMEM_LIMIT = 56 * 1024 * 1024


def nn(left, right):
    return lax.dot_general(left, right, (((1,), (0,)), ((), ())), preferred_element_type=f32)


def nt(left, right):
    return lax.dot_general(left, right, (((1,), (1,)), ((), ())), preferred_element_type=f32)


def tn(left, right):
    return lax.dot_general(left, right, (((0,), (0,)), ((), ())), preferred_element_type=f32)


def from_mp(array, step):
    size = lax.axis_size("mp")
    return lax.ppermute(array, "mp", [(i, (i - step) % size) for i in range(size)])


def to_mp(array, step):
    size = lax.axis_size("mp")
    return lax.ppermute(array, "mp", [(i, (i + step) % size) for i in range(size)])


def swap_mp(array, bit):
    return lax.ppermute(array, "mp", [(i, i ^ bit) for i in range(lax.axis_size("mp"))])


def swap_dp(array, bit):
    return lax.ppermute(array, "dp", [(i, i ^ bit) for i in range(lax.axis_size("dp"))])


def high_bits():
    low = lax.axis_size("dp") // BLOCKS
    return low, 2 * low, 4 * low


def gather_weights(block):
    core, along, across = high_bits()
    slots = [block] + [from_mp(block, step) for step in range(1, lax.axis_size("mp"))]
    first = jnp.stack(slots[:2])
    second = jnp.stack(slots[2:])
    first_x = swap_dp(first, along)
    first_y = swap_dp(first, across)
    second_y = swap_dp(second, across)
    second_x = swap_dp(second, along)
    first_xy = swap_dp(first_x, across)
    second_xy = swap_dp(second_y, along)
    own = jnp.stack(
        [
            jnp.concatenate([first, second]),
            jnp.concatenate([first_x, second_x]),
            jnp.concatenate([first_y, second_y]),
            jnp.concatenate([first_xy, second_xy]),
        ]
    )
    return own, swap_dp(own, core)


def rounded_sum(left, right):
    return (left.astype(f32) + right.astype(f32)).astype(bf16)


def reduce_dp(keep, send):
    core, along, across = high_bits()
    half = keep.shape[1] // 2
    got = swap_dp(send, core)

    def pick(places, first):
        part = slice(None, half) if first else slice(half, None)
        return jnp.stack([rounded_sum(keep[j, part], got[j, part]) for j in places])

    first_got = swap_dp(pick((1, 3), True), along)
    second_got = swap_dp(pick((2, 3), False), across)
    first_keep = pick((0, 2), True)
    second_keep = pick((0, 1), False)
    first_last = swap_dp(rounded_sum(first_keep[1], first_got[1]), across)
    second_last = swap_dp(rounded_sum(second_keep[1], second_got[1]), along)
    first_sum = first_keep[0].astype(f32) + first_got[0].astype(f32) + first_last.astype(f32)
    second_sum = second_keep[0].astype(f32) + second_got[0].astype(f32) + second_last.astype(f32)
    return jnp.concatenate([first_sum, second_sum])


def scatter_rest(rows):
    size = lax.axis_size("dp")
    low = size // BLOCKS
    if low == 1:
        return rows
    groups = [[high * low + i for i in range(low)] for high in range(BLOCKS)]
    return lax.psum_scatter(
        rows, "dp", scatter_dimension=0, axis_index_groups=groups, tiled=True
    )


def reduce_attention(keep, send):
    slots = reduce_dp(keep, send)
    total = slots[0]
    for step in range(1, lax.axis_size("mp")):
        total = total + to_mp(slots[step].astype(bf16), step).astype(f32)
    total = scatter_rest(total)
    width = total.shape[1] // 4
    parts = [total[:, i * width : (i + 1) * width] for i in range(4)]
    return parts[0], parts[1], parts[2], parts[3].T


def reduce_ffn(keep, send):
    both = reduce_dp(keep, send)
    return scatter_rest(both[0]), scatter_rest(both[1]).T


def sum_everywhere(array):
    bit = 1
    while bit < lax.axis_size("dp"):
        array = array + swap_dp(array, bit)
        bit *= 2
    bit = 1
    while bit < lax.axis_size("mp"):
        array = array + swap_mp(array, bit)
        bit *= 2
    return array


def fetch_weights(own_ref, rest_ref, held, sems, place):
    copies = []
    for slot in range(4):
        row = []
        for j in range(4):
            for side in range(2):
                source = (own_ref if side == 0 else rest_ref).at[j, slot]
                copy = pltpu.make_async_copy(
                    source, held.at[slot, place ^ (2 * j + side)], sems.at[slot, 2 * j + side]
                )
                copy.start()
                row.append(copy)
        copies.append(row)
    return copies


def slot_weights(copies, held, slot):
    for copy in copies[slot]:
        copy.wait()


def all_rows(held, slot, lanes):
    part = held[slot, :, :, lanes]
    return part.reshape(part.shape[0] * part.shape[1], part.shape[2])


def inverse_rms(rows):
    return lax.rsqrt(jnp.mean(rows * rows, axis=-1, keepdims=True) + EPS)


def column_head(shape):
    return lax.broadcasted_iota(jnp.int32, shape, 1) // DH


def softmax_rows(scores):
    shifted = jnp.exp(scores - jnp.max(scores, axis=-1, keepdims=True))
    return shifted / jnp.sum(shifted, axis=-1, keepdims=True)


def same_sequence(rows):
    row = lax.broadcasted_iota(jnp.int32, (rows, rows), 0)
    col = lax.broadcasted_iota(jnp.int32, (rows, rows), 1)
    return row // SEQ == col // SEQ, col <= row


def score_bias(kind, rel_ref, head, rows, keys):
    same, before = same_sequence(rows)
    if kind == "cross":
        return jnp.where(same, 0.0, NEG)
    wide = jnp.concatenate([rel_ref[head]] * (rows // SEQ), axis=0)
    if kind == "self":
        return jnp.where(jnp.logical_and(same, before), wide, NEG)
    row = lax.broadcasted_iota(jnp.int32, (rows, keys - rows), 0)
    col = lax.broadcasted_iota(jnp.int32, (rows, keys - rows), 1)
    first = (row // SEQ) * (MEMK * PREFIX)
    valid = jnp.logical_and(col >= first, col < first + MEMK * PREFIX)
    return jnp.concatenate([jnp.where(same, wide, NEG), jnp.where(valid, 0.0, NEG)], axis=1)


def attention_forward_kernel(kind, later, *refs):
    if kind == "encoder":
        place, x_ref, pre_ref, gain_ref, later_ref, rel_ref, own, rest = refs[:8]
        refs = refs[8:]
    elif kind == "self":
        place, x_ref, gain_ref, later_ref, rel_ref, own, rest = refs[:7]
        refs = refs[7:]
    else:
        place, x_ref, pre_ref, gain_ref, later_ref, own, rest = refs[:7]
        rel_ref = None
        refs = refs[7:]
    r1_ref, next_ref, a_ref, q_ref, kv_ref, o_ref, held, sems = refs
    copies = fetch_weights(own, rest, held, sems, place[0])
    r = x_ref[...].astype(f32)
    rows = r.shape[0]
    a = (r * inverse_rms(r) * gain_ref[...]).astype(bf16)
    if kind == "encoder":
        a_ref[0:rows, :] = a
        a_ref[rows:, :] = pre_ref[...]
        a_all = a_ref[...]
    else:
        a_ref[...] = a
        a_all = a
    acc = r
    for slot in range(4):
        slot_weights(copies, held, slot)
        w_in = all_rows(held, slot, slice(0, 576))
        if kind == "cross":
            q = nn(a, w_in[:, :192]).astype(bf16)
            kv = nn(pre_ref[...], w_in[:, 192:]).astype(bf16)
        else:
            qkv = nn(a_all, w_in).astype(bf16)
            q = qkv[:rows, :192]
            kv = qkv[:, 192:]
        q_ref[slot] = q
        kv_ref[slot] = kv
        k = kv[:, :192]
        v = kv[:, 192:]
        head_of = column_head(q.shape)
        o = jnp.zeros(q.shape, f32)
        for j in range(3):
            q_head = jnp.where(head_of == j, q, jnp.zeros_like(q))
            scores = nt(q_head, k) + score_bias(kind, rel_ref, 3 * slot + j, rows, k.shape[0])
            o = jnp.where(head_of == j, nn(softmax_rows(scores).astype(bf16), v), o)
        o = o.astype(bf16)
        o_ref[slot] = o
        acc = acc + nt(o, all_rows(held, slot, slice(576, 768)))
    r1_ref[...] = acc
    next_ref[...] = (acc * inverse_rms(acc) * later_ref[...]).astype(bf16)


def norm_back(dn, r, gain, dgain_ref):
    t = inverse_rms(r)
    dgain_ref[...] = jnp.sum(dn * r * t, axis=0, keepdims=True)
    scaled = dn * gain
    return t * (scaled - r * (t * t) * jnp.mean(scaled * r, axis=-1, keepdims=True))


def store_blocks(keep_ref, send_ref, place, part, value):
    size = value.shape[0] // BLOCKS
    side = place % 2
    for pair in range(BLOCKS // 2):
        where = pair ^ (place // 2)
        even = value[2 * pair * size : (2 * pair + 1) * size]
        odd = value[(2 * pair + 1) * size : (2 * pair + 2) * size]

        @pl.when(side == 0)
        def _():
            keep_ref[where, part] = even
            send_ref[where, part] = odd

        @pl.when(side == 1)
        def _():
            keep_ref[where, part] = odd
            send_ref[where, part] = even


def attention_backward_kernel(kind, after_ffn, *refs):
    refs = list(refs)
    place = refs.pop(0)[0]
    if after_ffn:
        dc_own, dc_rest, up_ref, r1_ref, later_ref = refs[:5]
        refs = refs[5:]
    else:
        up_ref = refs.pop(0)
    x_ref, gain_ref, a_ref = refs[:3]
    refs = refs[3:]
    source_ref = refs.pop(0) if kind == "cross" else None
    q_ref, kv_ref, o_ref, own, rest = refs[:5]
    refs = refs[5:]
    rel_ref, bucket_ref = (refs.pop(0), refs.pop(0)) if kind != "cross" else (None, None)
    dx_ref, dgain_ref, keep_ref, send_ref = refs[:4]
    refs = refs[4:]
    later_grad = refs.pop(0) if after_ffn else None
    if kind == "encoder":
        dpre_ref = refs.pop(0)
    elif kind == "cross":
        dsource_ref = refs.pop(0)
    bias_grad = refs.pop(0) if kind != "cross" else None
    held, sems, total, source_total, weight_grad = refs[:5]
    ds_sum = refs[5] if kind != "cross" else None

    copies = fetch_weights(own, rest, held, sems, place)
    d_out = up_ref[...].astype(f32)
    if after_ffn:
        dn = dc_own[...]
        for i in range(3):
            dn = dn + dc_rest[i].astype(f32)
        d_out = d_out + norm_back(dn, r1_ref[...], later_ref[...], later_grad)
    g = d_out.astype(bf16)
    rows = g.shape[0]
    a = a_ref[...]
    keys = kv_ref.shape[1]
    for slot in range(4):
        slot_weights(copies, held, slot)
        w_in = all_rows(held, slot, slice(0, 576))
        w_out = all_rows(held, slot, slice(576, 768))
        do = nn(g, w_out).astype(bf16)
        q = q_ref[slot]
        kv = kv_ref[slot]
        k = kv[:, :192]
        v = kv[:, 192:]
        head_q = column_head(q.shape)
        head_k = column_head(k.shape)
        dq = jnp.zeros(q.shape, f32)
        dk = jnp.zeros(k.shape, f32)
        dv = jnp.zeros(k.shape, f32)
        for j in range(3):
            q_head = jnp.where(head_q == j, q, jnp.zeros_like(q))
            do_head = jnp.where(head_q == j, do, jnp.zeros_like(do))
            scores = nt(q_head, k) + score_bias(kind, rel_ref, 3 * slot + j, rows, keys)
            p = softmax_rows(scores)
            dv = jnp.where(head_k == j, tn(p.astype(bf16), do), dv)
            dp = nt(do_head, v)
            ds = (p * (dp - jnp.sum(dp * p, axis=-1, keepdims=True))).astype(bf16)
            dq = jnp.where(head_q == j, nn(ds, k), dq)
            dk = jnp.where(head_k == j, tn(ds, q), dk)
            if kind != "cross":
                wide = ds[:, :rows].astype(f32)
                ds_sum[3 * slot + j] = wide[:SEQ] + wide[SEQ:]
        dq = dq.astype(bf16)
        dkv = jnp.concatenate([dk, dv], axis=1).astype(bf16)
        part_total = nt(dq, w_in[:, :192])
        part_source = nt(dkv, w_in[:, 192:])
        if kind == "cross":
            source = source_ref[...]
        else:
            source = a
        if slot == 0:
            total[...] = part_total
            source_total[...] = part_source
        else:
            total[...] += part_total
            source_total[...] += part_source
        weight_grad[:, 0:192] = tn(a[:rows], dq).astype(bf16)
        weight_grad[:, 192:576] = tn(source, dkv).astype(bf16)
        weight_grad[:, 576:768] = tn(g, o_ref[slot]).astype(bf16)
        store_blocks(keep_ref, send_ref, place, slot, weight_grad)
    da = total[...]
    if kind == "cross":
        dsource_ref[...] = source_total[...]
    else:
        da = da + source_total[0:rows]
    if kind == "encoder":
        dpre_ref[...] = source_total[rows:].astype(bf16)
    dx_ref[...] = d_out + norm_back(da, x_ref[...].astype(f32), gain_ref[...], dgain_ref)
    if kind != "cross":
        bucket = bucket_ref[...]
        for b in range(bias_grad.shape[1]):
            chosen = bucket == b
            for head in range(bias_grad.shape[0]):
                bias_grad[head, b : b + 1, :] = jnp.sum(
                    jnp.where(chosen, ds_sum[head], 0.0), axis=0, keepdims=True
                )


def ffn_first_kernel(c0, c1, c2, c3, g0, g1, g2, g3, widen, narrow, c_all, g_all, h_ref, du_ref, dc_own, dc_rest):
    tokens = c0.shape[0]
    for i, (c, g) in enumerate(((c0, g0), (c1, g1), (c2, g2), (c3, g3))):
        c_all[i * tokens : (i + 1) * tokens, :] = c[...]
        g_all[i * tokens : (i + 1) * tokens, :] = g[...]
    inner = 0.7978845608028654
    for n in range(widen.shape[1] // 256):
        at = slice(n * 256, (n + 1) * 256)
        u = nn(c_all[...], widen[:, at])
        u2 = u * u
        th = jnp.tanh(inner * (u + 0.044715 * u * u2))
        h_ref[:, at] = (0.5 * u * (1.0 + th)).astype(bf16)
        slope = 0.5 * (1.0 + th) + (0.5 * inner) * u * (1.0 - th * th) * (1.0 + 3 * 0.044715 * u2)
        dh = nt(g_all[...], narrow[at, :])
        du_ref[:, at] = (dh * slope).astype(bf16)
    for n in range(widen.shape[0] // 256):
        at = slice(n * 256, (n + 1) * 256)
        dc = nt(du_ref[...], widen[at, :])
        dc_own[:, at] = dc[:tokens]
        for i in range(3):
            dc_rest[i, :, at] = dc[(i + 1) * tokens : (i + 2) * tokens].astype(bf16)


def ffn_second_kernel(place, c_all, g_all, h_ref, du_ref, narrow, out_own, out_rest, keep_ref, send_ref, grad):
    tokens = out_own.shape[0]
    for n in range(narrow.shape[1] // 256):
        at = slice(n * 256, (n + 1) * 256)
        out = nn(h_ref[...], narrow[:, at])
        out_own[:, at] = out[:tokens]
        for i in range(3):
            out_rest[i, :, at] = out[(i + 1) * tokens : (i + 2) * tokens].astype(bf16)
    grad[...] = tn(c_all[...], du_ref[...]).astype(bf16)
    store_blocks(keep_ref, send_ref, place[0], 0, grad)
    grad[...] = tn(g_all[...], h_ref[...]).astype(bf16)
    store_blocks(keep_ref, send_ref, place[0], 1, grad)


def call(kernel, name, operands, smem, hbm, outs, scratch, flops):
    specs = []
    for i in range(len(operands)):
        if i in smem:
            specs.append(pl.BlockSpec(memory_space=pltpu.SMEM))
        elif i in hbm:
            specs.append(pl.BlockSpec(memory_space=pl.ANY))
        else:
            specs.append(pl.BlockSpec(memory_space=pltpu.VMEM))
    moved = sum(x.size * x.dtype.itemsize for x in operands)
    return pl.pallas_call(
        kernel,
        out_shape=[jax.ShapeDtypeStruct(shape, kind) for shape, kind in outs],
        in_specs=specs,
        out_specs=[pl.BlockSpec(memory_space=pltpu.VMEM)] * len(outs),
        scratch_shapes=scratch,
        compiler_params=pltpu.CompilerParams(vmem_limit_bytes=VMEM_LIMIT),
        cost_estimate=pl.CostEstimate(flops=flops, bytes_accessed=moved, transcendentals=0),
        name=name,
    )(*operands)


def attention_forward(kind, place, x, extra, gain, later, rel, weights):
    own, rest = weights
    rows, width = x.shape
    extra_rows = extra.shape[0] if kind == "encoder" else 0
    keys = rows + extra_rows
    operands = [place, x]
    if extra is not None:
        operands.append(extra)
    operands += [gain, later]
    if rel is not None:
        operands.append(rel)
    operands += [own, rest]
    count = len(operands)
    return call(
        functools.partial(attention_forward_kernel, kind, True),
        kind + "_forward",
        operands,
        (0,),
        (count - 2, count - 1),
        [
            ((rows, width), f32),
            ((rows, width), bf16),
            ((keys, width), bf16),
            ((4, rows, 192), bf16),
            ((4, keys, 384), bf16),
            ((4, rows, 192), bf16),
        ],
        [pltpu.VMEM((4, BLOCKS, own.shape[2], width), bf16), pltpu.SemaphoreType.DMA((4, 8))],
        8 * rows * width * width,
    )


def attention_backward(kind, place, ffn, upstream, x, gain, stored, source, weights, rel, bucket, buckets):
    own, rest = weights
    rows, width = upstream.shape
    a, q, kv, o = stored
    keys = kv.shape[1]
    operands = [place]
    if ffn is not None:
        dc_own, dc_rest, r1, later = ffn
        operands += [dc_own, dc_rest, upstream, r1, later]
    else:
        operands += [upstream]
    operands += [x, gain, a]
    if source is not None:
        operands.append(source)
    operands += [q, kv, o]
    hbm = (len(operands), len(operands) + 1)
    operands += [own, rest]
    if kind != "cross":
        operands += [rel, bucket]
    block = own.shape[2]
    outs = [
        ((rows, width), f32),
        ((1, width), f32),
        ((4, 4, block, width), bf16),
        ((4, 4, block, width), bf16),
    ]
    if ffn is not None:
        outs.append(((1, width), f32))
    if kind == "encoder":
        outs.append(((keys - rows, width), bf16))
    elif kind == "cross":
        outs.append(((rows, width), f32))
    if kind != "cross":
        outs.append(((rel.shape[0], buckets, 2 * SEQ), f32))
    scratch = [
        pltpu.VMEM((4, BLOCKS, block, width), bf16),
        pltpu.SemaphoreType.DMA((4, 8)),
        pltpu.VMEM((rows, width), f32),
        pltpu.VMEM((keys, width), f32),
        pltpu.VMEM((width, width), bf16),
    ]
    if kind != "cross":
        scratch.append(pltpu.VMEM((rel.shape[0], SEQ, 2 * SEQ), f32))
    return call(
        functools.partial(attention_backward_kernel, kind, ffn is not None),
        kind + "_backward",
        operands,
        (0,),
        hbm,
        outs,
        scratch,
        16 * rows * width * width,
    )


def ffn_both(name, place, c_parts, g_parts, widen, narrow):
    tokens, width = c_parts[0].shape
    hidden = widen.shape[1]
    every = 4 * tokens
    block = width // BLOCKS
    c_all, g_all, h, du, dc_own, dc_rest = call(
        ffn_first_kernel,
        name + "_first",
        [*c_parts, *g_parts, widen, narrow],
        (),
        (),
        [
            ((every, width), bf16),
            ((every, width), bf16),
            ((every, hidden), bf16),
            ((every, hidden), bf16),
            ((tokens, width), f32),
            ((3, tokens, width), bf16),
        ],
        [],
        6 * every * width * hidden,
    )
    out_own, out_rest, keep, send = call(
        ffn_second_kernel,
        name + "_second",
        [place, c_all, g_all, h, du, narrow],
        (0,),
        (),
        [
            ((tokens, width), f32),
            ((3, tokens, width), bf16),
            ((4, 2, block, hidden), bf16),
            ((4, 2, block, hidden), bf16),
        ],
        [pltpu.VMEM((width, hidden), bf16)],
        6 * every * width * hidden,
    )
    return dc_own, dc_rest, out_own, out_rest, keep, send


def gather_tokens(part):
    return [part] + [from_mp(part, step) for step in range(1, 4)]


def return_tokens(rest):
    return jnp.stack([to_mp(rest[step - 1], step) for step in range(1, 4)])


def weight_block(place, query, key, value, merge):
    size = query.shape[0] // BLOCKS
    start = place * size
    parts = [lax.dynamic_slice_in_dim(w, start, size, 0) for w in (query, key, value)]
    parts.append(lax.dynamic_slice_in_dim(merge, start, size, 1).T)
    return jnp.concatenate(parts, axis=1)


def relative_bias(bucket, table, heads_here):
    twice = jnp.concatenate([bucket, bucket], axis=1)
    onehot = (
        lax.broadcasted_iota(jnp.int32, (table.shape[0], 1), 0) == twice.reshape(1, -1)
    ).astype(f32)
    start = lax.axis_index("mp") * heads_here
    columns = jnp.concatenate([table.T, table.T], axis=0)
    ordered = lax.dynamic_slice_in_dim(columns, start, table.shape[1], 0)
    looked = jnp.dot(ordered, onehot, precision=lax.Precision.HIGHEST)
    return looked.reshape(table.shape[1], SEQ, 2 * SEQ), twice


def bias_sums(raw, heads_here):
    by_head = jnp.sum(raw, axis=-1)
    heads = by_head.shape[0]
    start = heads - lax.axis_index("mp") * heads_here
    twice = jnp.concatenate([by_head, by_head], axis=0)
    return lax.dynamic_slice_in_dim(twice, start, heads, 0)


def shards(
    encoder_input,
    encoder_upstream,
    memory_index,
    memory_table,
    encoder_bucket,
    encoder_bias,
    encoder_gain,
    encoder_query,
    encoder_key,
    encoder_value,
    encoder_merge,
    encoder_later_gain,
    encoder_widen,
    encoder_narrow,
    decoder_input,
    decoder_upstream,
    encoder_states,
    decoder_bucket,
    decoder_bias,
    decoder_gain,
    decoder_query,
    decoder_key,
    decoder_value,
    decoder_merge,
    cross_gain,
    cross_query,
    cross_key,
    cross_value,
    cross_merge,
    decoder_later_gain,
    decoder_widen,
    decoder_narrow,
):
    heads_here = encoder_query.shape[1] // DH
    width = encoder_input.shape[1]
    dp_at = lax.axis_index("dp")
    mp_at = lax.axis_index("mp")
    place = dp_at // (lax.axis_size("dp") // BLOCKS)
    place_in = place.reshape(1).astype(jnp.int32)

    def flat(gain):
        return gain.reshape(1, -1)

    encoder_weights = gather_weights(
        weight_block(place, encoder_query, encoder_key, encoder_value, encoder_merge)
    )
    self_weights = gather_weights(
        weight_block(place, decoder_query, decoder_key, decoder_value, decoder_merge)
    )
    cross_weights = gather_weights(
        weight_block(place, cross_query, cross_key, cross_value, cross_merge)
    )
    encoder_g = gather_tokens(encoder_upstream)
    decoder_g = gather_tokens(decoder_upstream)

    own_questions = memory_index.shape[0] // lax.axis_size("mp")
    entries = lax.dynamic_slice_in_dim(
        memory_index, mp_at * own_questions, own_questions, 0
    ).reshape(-1)
    prefix = jnp.take(memory_table, entries, axis=0).reshape(-1, width)
    prefix_rows = prefix.shape[0]
    prefix = jnp.pad(prefix, ((0, -prefix_rows % 64), (0, 0)))

    encoder_rel, encoder_twice = relative_bias(encoder_bucket, encoder_bias, heads_here)
    decoder_rel, decoder_twice = relative_bias(decoder_bucket, decoder_bias, heads_here)

    encoder_r1, encoder_c, *encoder_stored = attention_forward(
        "encoder",
        place_in,
        encoder_input,
        prefix,
        flat(encoder_gain),
        flat(encoder_later_gain),
        encoder_rel,
        encoder_weights,
    )
    dc_own, dc_rest, out_own, out_rest, keep, send = ffn_both(
        "encoder_ffn",
        place_in,
        gather_tokens(encoder_c),
        encoder_g,
        encoder_widen,
        encoder_narrow,
    )
    dc_rest = return_tokens(dc_rest)
    out_rest = return_tokens(out_rest)
    encoder_output = (
        encoder_r1 + out_own + jnp.sum(out_rest.astype(f32), axis=0)
    ).astype(bf16)
    encoder_widen_grad, encoder_narrow_grad = reduce_ffn(keep, send)
    (
        encoder_input_grad,
        encoder_gain_grad,
        keep,
        send,
        encoder_later_grad,
        prefix_grad,
        encoder_bias_raw,
    ) = attention_backward(
        "encoder",
        place_in,
        (dc_own, dc_rest, encoder_r1, flat(encoder_later_gain)),
        encoder_upstream,
        encoder_input,
        flat(encoder_gain),
        encoder_stored,
        None,
        encoder_weights,
        encoder_rel,
        encoder_twice,
        encoder_bias.shape[0],
    )
    encoder_mats = reduce_attention(keep, send)

    entry_rows = jnp.repeat(entries, PREFIX)
    numbers = jnp.stack([entry_rows // 32, entry_rows % 32], axis=1).astype(bf16)
    numbers = jnp.pad(numbers, ((0, 0), (0, 126)))
    packed = jnp.concatenate([prefix_grad[:prefix_rows], numbers], axis=1)
    used = lax.all_gather(packed, ("dp", "mp"), axis=0, tiled=True)
    used_entry = used[:, width].astype(jnp.int32) * 32 + used[:, width + 1].astype(jnp.int32)
    used_row = used_entry * PREFIX + jnp.arange(used.shape[0]) % PREFIX
    devices = lax.axis_size("dp") * lax.axis_size("mp")
    table_rows = memory_table.shape[0] * PREFIX // devices
    first_row = (dp_at * lax.axis_size("mp") + mp_at) * table_rows
    onehot = (
        first_row + lax.broadcasted_iota(jnp.int32, (table_rows, 1), 0) == used_row[None, :]
    ).astype(bf16)
    table_grad = nn(onehot, used[:, :width]).reshape(-1, PREFIX, width)

    self_r1, _, *self_stored = attention_forward(
        "self",
        place_in,
        decoder_input,
        None,
        flat(decoder_gain),
        flat(cross_gain),
        decoder_rel,
        self_weights,
    )
    cross_r2, decoder_c, *cross_stored = attention_forward(
        "cross",
        place_in,
        self_r1,
        encoder_states,
        flat(cross_gain),
        flat(decoder_later_gain),
        None,
        cross_weights,
    )
    dc_own, dc_rest, out_own, out_rest, keep, send = ffn_both(
        "decoder_ffn",
        place_in,
        gather_tokens(decoder_c),
        decoder_g,
        decoder_widen,
        decoder_narrow,
    )
    dc_rest = return_tokens(dc_rest)
    out_rest = return_tokens(out_rest)
    decoder_output = (cross_r2 + out_own + jnp.sum(out_rest.astype(f32), axis=0)).astype(bf16)
    decoder_widen_grad, decoder_narrow_grad = reduce_ffn(keep, send)
    cross_dx, cross_gain_grad, keep, send, decoder_later_grad, states_grad = attention_backward(
        "cross",
        place_in,
        (dc_own, dc_rest, cross_r2, flat(decoder_later_gain)),
        decoder_upstream,
        self_r1,
        flat(cross_gain),
        cross_stored,
        encoder_states,
        cross_weights,
        None,
        None,
        None,
    )
    cross_mats = reduce_attention(keep, send)
    decoder_input_grad, decoder_gain_grad, keep, send, decoder_bias_raw = attention_backward(
        "self",
        place_in,
        None,
        cross_dx,
        decoder_input,
        flat(decoder_gain),
        self_stored,
        None,
        self_weights,
        decoder_rel,
        decoder_twice,
        decoder_bias.shape[0],
    )
    self_mats = reduce_attention(keep, send)

    gains = [
        encoder_gain_grad,
        encoder_later_grad,
        decoder_gain_grad,
        cross_gain_grad,
        decoder_later_grad,
    ]
    tables = [bias_sums(encoder_bias_raw, heads_here), bias_sums(decoder_bias_raw, heads_here)]
    small = jnp.concatenate([x.reshape(-1) for x in gains + tables]).reshape(-1, 128)
    small = sum_everywhere(small).reshape(-1)
    gain_sums = [small[i * width : (i + 1) * width] for i in range(5)]
    heads, buckets = tables[0].shape
    table_at = 5 * width
    bias_grads = [
        small[table_at + i * heads * buckets : table_at + (i + 1) * heads * buckets]
        .reshape(heads, buckets)
        .T
        for i in range(2)
    ]
    return (
        encoder_output,
        encoder_input_grad,
        table_grad,
        bias_grads[0],
        gain_sums[0],
        *encoder_mats,
        gain_sums[1],
        encoder_widen_grad,
        encoder_narrow_grad,
        decoder_output,
        decoder_input_grad,
        states_grad,
        bias_grads[1],
        gain_sums[2],
        *self_mats,
        gain_sums[3],
        *cross_mats,
        gain_sums[4],
        decoder_widen_grad,
        decoder_narrow_grad,
    )


def solution(mesh):
    rows = P(("dp", "mp"), None)
    columns = P(None, "mp")
    lines = P("mp", None)
    attention = (columns, columns, columns, lines)
    in_specs = (
        (rows, rows, P("dp", None), P(), P(), P(), P())
        + attention
        + (P(), columns, lines, rows, rows, rows, P(), P(), P())
        + attention
        + (P(),)
        + attention
        + (P(), columns, lines)
    )
    both = P("dp", "mp")
    turned = P("mp", "dp")
    grads = (both, both, both, turned)
    out_specs = (
        (rows, rows, P(("dp", "mp"), None, None), P(), P())
        + grads
        + (P(), both, turned, rows, rows, rows, P(), P())
        + grads
        + (P(),)
        + grads
        + (P(), both, turned)
    )
    return jax.shard_map(shards, mesh=mesh, in_specs=in_specs, out_specs=out_specs, check_vma=False)
```

```python
import functools

import jax
import jax.numpy as jnp
from jax import lax
from jax.experimental import pallas as pl
from jax.experimental.pallas import tpu as pltpu
from jax.sharding import PartitionSpec as P

DH = 64
SEQ = 64
MEMK = 10
PREFIX = 2
EPS = 1e-06
NEG = -1e30
BLOCKS = 8
bf16 = jnp.bfloat16
f32 = jnp.float32


def nn(left, right):
    return lax.dot_general(left, right, (((1,), (0,)), ((), ())), preferred_element_type=f32)


def nt(left, right):
    return lax.dot_general(left, right, (((1,), (1,)), ((), ())), preferred_element_type=f32)


def tn(left, right):
    return lax.dot_general(left, right, (((0,), (0,)), ((), ())), preferred_element_type=f32)


def from_mp(array, step):
    size = lax.axis_size("mp")
    return lax.ppermute(array, "mp", [(i, (i - step) % size) for i in range(size)])


def to_mp(array, step):
    size = lax.axis_size("mp")
    return lax.ppermute(array, "mp", [(i, (i + step) % size) for i in range(size)])


def swap_mp(array, bit):
    return lax.ppermute(array, "mp", [(i, i ^ bit) for i in range(lax.axis_size("mp"))])


def swap_dp(array, bit):
    return lax.ppermute(array, "dp", [(i, i ^ bit) for i in range(lax.axis_size("dp"))])


def after(value, *earlier):
    leaves, shape = jax.tree.flatten(value)
    tied = lax.optimization_barrier((*leaves, *jax.tree.leaves(earlier)))
    return jax.tree.unflatten(shape, tied[: len(leaves)])


def high_bits():
    low = lax.axis_size("dp") // BLOCKS
    return low, 2 * low, 4 * low


def rounded_sum(left, right):
    return (left.astype(f32) + right.astype(f32)).astype(bf16)


def stack_slots(block, others):
    return jnp.stack([block, others[0]]), jnp.stack(others[1:])


def spread_once(first, second):
    core, along, across = high_bits()
    return swap_dp(first, along), swap_dp(second, across)


def spread_twice(first_two, second_two):
    core, along, across = high_bits()
    return swap_dp(first_two, across), swap_dp(second_two, along)


def join_places(first_two, second_two, first_far, second_far):
    return jnp.concatenate(
        [
            jnp.concatenate([first_two, first_far]),
            jnp.stack([second_two[0], second_far[0], second_two[1], second_far[1]]),
        ],
        axis=1,
    )


def swap_cores(array):
    return swap_dp(array, high_bits()[0])


def fold_cores(keep, got):
    return tuple(
        (rounded_sum(keep[i, :2], got[i, :2]), rounded_sum(keep[i, 2:], got[i, 2:])) for i in range(2)
    )


def send_once(halves):
    core, along, across = high_bits()
    return swap_dp(halves[0][1], along), swap_dp(halves[1][1], across)


def fold_once(halves, got):
    return tuple(rounded_sum(halves[i][0][1], got[i][1]) for i in range(2))


def send_twice(last):
    core, along, across = high_bits()
    return swap_dp(last[0], across), swap_dp(last[1], along)


def fold_twice(halves, got, last_got):
    sums = [
        halves[i][0][0].astype(f32) + got[i][0].astype(f32) + last_got[i].astype(f32) for i in range(2)
    ]
    return [sums[0][0], sums[0][1], sums[1][0], sums[1][1]]


def send_slots(slots):
    return [to_mp(slots[step].astype(bf16), step) for step in range(1, 4)]


def scatter_rest(rows):
    size = lax.axis_size("dp")
    low = size // BLOCKS
    if low == 1:
        return rows
    groups = [[high * low + i for i in range(low)] for high in range(BLOCKS)]
    return lax.psum_scatter(
        rows, "dp", scatter_dimension=0, axis_index_groups=groups, tiled=True
    )


def four_matrices(slots, got):
    total = slots[0]
    if lax.axis_size("dp") == BLOCKS:
        rows, width = total.shape
        part = width // 4
        return call(
            finish_kernel,
            "matrices",
            [total, *got],
            (),
            (),
            [((rows, part), f32)] * 3 + [((part, rows), f32)],
            [],
        )
    for other in got:
        total = total + other.astype(f32)
    total = scatter_rest(total)
    width = total.shape[1] // 4
    parts = [total[:, i * width : (i + 1) * width] for i in range(4)]
    return parts[0], parts[1], parts[2], parts[3].T


def reduce_ffn(grads):
    return lax.psum_scatter(grads, "dp", scatter_dimension=0, tiled=True)


def two_matrices(sums):
    rows, width = sums.shape
    if rows % 16:
        sums = sums.astype(f32)
        return sums[:, : width // 2], sums[:, width // 2 :].T
    return call(
        finish_ffn_kernel,
        "ffn_matrices",
        [sums],
        (),
        (),
        [((rows, width // 2), f32), ((width // 2, rows), f32)],
        [],
    )


def gather_blocks(blocks):
    low = lax.axis_size("dp") // BLOCKS
    if low == 1:
        every = lax.all_gather(blocks, ("dp", "mp"), axis=0, tiled=False)
        return every.reshape(BLOCKS, -1, *blocks.shape)
    groups = [[high * low + i for high in range(BLOCKS)] for i in range(low)]
    return lax.all_gather(
        lax.all_gather(blocks, "mp", axis=0, tiled=False),
        "dp",
        axis=0,
        axis_index_groups=groups,
        tiled=False,
    )


def sum_everywhere(array):
    bit = 1
    while bit < lax.axis_size("dp"):
        array = array + swap_dp(array, bit)
        bit *= 2
    bit = 1
    while bit < lax.axis_size("mp"):
        array = array + swap_mp(array, bit)
        bit *= 2
    return array


def fetch_weights(parts, group, held, sems, place, mp_at, order):
    copies = {(what, slot): [] for what in order for slot in range(4)}
    if len(parts) == 2:
        for slot in range(4):
            for j in range(4):
                for side in range(2):
                    held[slot, place ^ (2 * j + side)] = parts[side][j, slot]
        return copies
    for i, what in enumerate(order):
        blocks = pl.ds(6, 2) if what == "merge" else pl.ds(0, 6)
        for slot in range(4):
            copy = pltpu.make_async_copy(
                parts[0].at[blocks, (mp_at + slot) % 4, group],
                held.at[slot, blocks],
                sems.at[slot, i],
            )
            copy.start()
            copies[what, slot].append(copy)
    return copies


def wait_all(copies):
    for copy in copies:
        copy.wait()


def slot_rows(held, slot, first, last):
    part = held[slot, 2 * first : 2 * last]
    return part.reshape(part.shape[0] * part.shape[1], part.shape[2])


def blocks_kernel(groups, place_ref, *refs):
    inputs = refs[: 4 * groups]
    first, others, sems = refs[4 * groups :]
    outs = [first] + [others.at[i] for i in range(groups - 1)]
    size = first.shape[0]
    place = place_ref[0]
    start = pl.multiple_of((place % 2) * size, size)
    for j in range(4):

        @pl.when(place // 2 == j)
        def _():
            copies = [
                pltpu.make_async_copy(inputs[4 * i + j].at[pl.ds(start, size)], outs[i], sems.at[i])
                for i in range(groups)
            ]
            for copy in copies:
                copy.start()
            wait_all(copies)


def inverse_rms(rows):
    return lax.rsqrt(jnp.mean(rows * rows, axis=-1, keepdims=True) + EPS)


def gain_rows(kind, gains_ref):
    at = {"encoder": (0, 1), "self": (2, 3), "cross": (3, 4)}[kind]
    return tuple(gains_ref[i : i + 1, :] for i in at)


def column_head(shape):
    return lax.broadcasted_iota(jnp.int32, shape, 1) // DH


def softmax_rows(scores):
    shifted = jnp.exp(scores - jnp.max(scores, axis=-1, keepdims=True))
    return shifted / jnp.sum(shifted, axis=-1, keepdims=True)


def masks(kind, rows, keys):
    row = lax.broadcasted_iota(jnp.int32, (rows, rows), 0)
    col = lax.broadcasted_iota(jnp.int32, (rows, rows), 1)
    same = row // SEQ == col // SEQ
    if kind == "self":
        same = jnp.logical_and(same, col <= row)
    if kind != "encoder":
        return same, None
    row = lax.broadcasted_iota(jnp.int32, (rows, keys - rows), 0)
    col = lax.broadcasted_iota(jnp.int32, (rows, keys - rows), 1)
    first = (row // SEQ) * (MEMK * PREFIX)
    valid = jnp.logical_and(col >= first, col < first + MEMK * PREFIX)
    return same, jnp.where(valid, 0.0, NEG)


def add_bias(kind, scores, rel_ref, slot, same, before):
    rows = scores.shape[0] // 3
    parts = []
    for j in range(3):
        part = scores[j * rows : (j + 1) * rows]
        own = part[:, :rows]
        if kind != "cross":
            rel = rel_ref[3 * slot + j]
            own = own + jnp.concatenate([rel] * (rows // SEQ), axis=0)
        own = jnp.where(same, own, NEG)
        if before is not None:
            own = jnp.concatenate([own, part[:, rows:] + before], axis=1)
        parts.append(own)
    return jnp.concatenate(parts, axis=0)


def stack_heads(array):
    head = column_head(array.shape)
    return jnp.concatenate([jnp.where(head == j, array, jnp.zeros_like(array)) for j in range(3)], axis=0)


def join_heads(stacked):
    rows = stacked.shape[0] // 3
    head = column_head((rows, stacked.shape[1]))
    return jnp.where(
        head == 0,
        stacked[:rows],
        jnp.where(head == 1, stacked[rows : 2 * rows], stacked[2 * rows :]),
    )


def attention_forward_kernel(kind, parts, *refs):
    refs = list(refs)
    place_ref, x_ref = refs[:2]
    del refs[:2]
    pre_ref = refs.pop(0) if kind != "self" else None
    gains_ref = refs.pop(0)
    gain, later = gain_rows(kind, gains_ref)
    rel_ref = refs.pop(0) if kind != "cross" else None
    weights = refs[:parts]
    r1_ref, next_ref, a_ref, q_ref, kv_ref, o_ref, held, sems = refs[parts:]
    copies = fetch_weights(weights, int(kind == "cross"), held, sems, place_ref[0], place_ref[1], ("rest", "merge"))
    r = x_ref[...].astype(f32)
    rows = r.shape[0]
    a = (r * inverse_rms(r) * gain).astype(bf16)
    if kind == "encoder":
        a_ref[0:rows, :] = a
        a_ref[rows:, :] = pre_ref[...]
        a_all = a_ref[...]
    else:
        a_ref[...] = a
        a_all = a
    keys = kv_ref.shape[1]
    same, before = masks(kind, rows, keys)
    queries = []
    sources = []
    for slot in range(4):
        wait_all(copies["rest", slot])
        if kind == "cross":
            q = nt(a, slot_rows(held, slot, 0, 1)).astype(bf16)
            kv = nt(pre_ref[...], slot_rows(held, slot, 1, 3)).astype(bf16)
        else:
            qkv = nt(a_all, slot_rows(held, slot, 0, 3)).astype(bf16)
            q = qkv[:rows, :192]
            kv = qkv[:, 192:]
        q_ref[slot] = q
        kv_ref[slot] = kv
        queries.append(q)
        sources.append(kv)
    chances = []
    for slot in range(4):
        scores = nt(stack_heads(queries[slot]), sources[slot][:, :192])
        chances.append(softmax_rows(add_bias(kind, scores, rel_ref, slot, same, before)).astype(bf16))
    mixed = []
    for slot in range(4):
        o = join_heads(nn(chances[slot], sources[slot][:, 192:])).astype(bf16)
        o_ref[slot] = o
        mixed.append(o)
    acc = r
    for slot in range(4):
        wait_all(copies["merge", slot])
        acc = acc + nn(mixed[slot], slot_rows(held, slot, 3, 4))
    r1_ref[...] = acc
    next_ref[...] = (acc * inverse_rms(acc) * later).astype(bf16)


def norm_back(dn, r, gain, dgain_ref):
    t = inverse_rms(r)
    dgain_ref[...] = jnp.sum(dn * r * t, axis=0, keepdims=True)
    scaled = dn * gain
    return t * (scaled - r * (t * t) * jnp.mean(scaled * r, axis=-1, keepdims=True))


def store_blocks(keep_ref, send_ref, place, slot, value):
    size = value.shape[0] // BLOCKS
    side = place % 2
    for pair in range(BLOCKS // 2):
        where = pair ^ (place // 2)
        if slot // 2 == 0:
            where = (where % 2) * 2 + where // 2
        even = value[2 * pair * size : (2 * pair + 1) * size]
        odd = value[(2 * pair + 1) * size : (2 * pair + 2) * size]

        @pl.when(side == 0)
        def _():
            keep_ref[slot // 2, where, slot % 2] = even
            send_ref[slot // 2, where, slot % 2] = odd

        @pl.when(side == 1)
        def _():
            keep_ref[slot // 2, where, slot % 2] = odd
            send_ref[slot // 2, where, slot % 2] = even


def attention_backward_kernel(kind, parts, after_ffn, *refs):
    refs = list(refs)
    place_ref = refs.pop(0)
    place, mp_at = place_ref[0], place_ref[1]
    if after_ffn:
        dc_own, *dc_rest = refs[:4]
        up_ref, r1_ref = refs[4:6]
        refs = refs[6:]
    else:
        up_ref = refs.pop(0)
    x_ref, gains_ref, a_ref = refs[:3]
    gain, later = gain_rows(kind, gains_ref)
    refs = refs[3:]
    source_ref = refs.pop(0) if kind == "cross" else None
    q_ref, kv_ref, o_ref = refs[:3]
    weights = refs[3 : 3 + parts]
    refs = refs[3 + parts :]
    rel_ref, bucket_ref = (refs.pop(0), refs.pop(0)) if kind != "cross" else (None, None)
    dx_ref, dgain_ref = refs[:2]
    refs = refs[2:]
    keep_ref, send_ref = refs.pop(0), refs.pop(0)
    later_grad = refs.pop(0) if after_ffn else None
    if kind == "encoder":
        dpre_ref = refs.pop(0)
    elif kind == "cross":
        dsource_ref = refs.pop(0)
    bias_grad = refs.pop(0) if kind != "cross" else None
    held, sems, left, right = refs[:4]
    refs = refs[4:]
    ds_sum = refs.pop(0) if kind != "cross" else None
    weight_grad = refs.pop(0)

    copies = fetch_weights(weights, int(kind == "cross"), held, sems, place, mp_at, ("merge", "rest"))
    d_out = up_ref[...].astype(f32)
    if after_ffn:
        dn = dc_own[...]
        for part in dc_rest:
            dn = dn + part[...].astype(f32)
        d_out = d_out + norm_back(dn, r1_ref[...], later, later_grad)
    g = d_out.astype(bf16)
    rows, width = g.shape
    keys = kv_ref.shape[1]
    stacked = [a_ref[...]] + ([source_ref[...]] if kind == "cross" else []) + [g]
    left[...] = jnp.concatenate(stacked, axis=0).T
    source_at = rows if kind == "cross" else 0
    g_at = left.shape[1] - rows
    right[...] = jnp.zeros(right.shape, bf16)
    same, before = masks(kind, rows, keys)
    grads = []
    for slot in range(4):
        wait_all(copies["merge", slot])
        grads.append(nt(g, slot_rows(held, slot, 3, 4)).astype(bf16))
        right[slot, g_at:, 576:768] = o_ref[slot]
    chances = []
    for slot in range(4):
        scores = nt(stack_heads(q_ref[slot]), kv_ref[slot][:, :192])
        chances.append(softmax_rows(add_bias(kind, scores, rel_ref, slot, same, before)))
    d_scores = []
    for slot in range(4):
        p = chances[slot]
        do_heads = stack_heads(grads[slot])
        dv = tn(p.astype(bf16), do_heads).astype(bf16)
        right[slot, source_at : source_at + keys, 384:576] = dv
        dp = nt(do_heads, kv_ref[slot][:, 192:])
        ds = (p * (dp - jnp.sum(dp * p, axis=-1, keepdims=True))).astype(bf16)
        d_scores.append(ds)
    for slot in range(4):
        ds = d_scores[slot]
        right[slot, 0:rows, 0:192] = join_heads(nn(ds, kv_ref[slot][:, :192])).astype(bf16)
        right[slot, source_at : source_at + keys, 192:384] = tn(ds, stack_heads(q_ref[slot])).astype(bf16)
        if kind != "cross":
            for j in range(3):
                wide = ds[j * rows : (j + 1) * rows, :rows].astype(f32)
                ds_sum[3 * slot + j] = wide[:SEQ] + wide[SEQ:]
    for slot in range(4):
        grad = nn(left[...], right[slot]).astype(bf16)
        weight_grad[...] = grad
        store_blocks(keep_ref, send_ref, place, slot, weight_grad)
    total = None
    source_total = None
    for slot in range(4):
        wait_all(copies["rest", slot])
        if kind == "cross":
            part = nn(right[slot, 0:rows, 0:192], slot_rows(held, slot, 0, 1))
            other = nn(right[slot, rows : rows + keys, 192:576], slot_rows(held, slot, 1, 3))
            source_total = other if slot == 0 else source_total + other
        else:
            part = nn(right[slot, 0:keys, 0:576], slot_rows(held, slot, 0, 3))
        total = part if slot == 0 else total + part
    if kind == "cross":
        dsource_ref[...] = source_total
    if kind == "encoder":
        dpre_ref[...] = total[rows:].astype(bf16)
    dx_ref[...] = d_out + norm_back(total[:rows], x_ref[...].astype(f32), gain, dgain_ref)
    if kind != "cross":
        bucket = bucket_ref[...]
        heads, buckets = bias_grad.shape[:2]

        @pl.loop(0, buckets)
        def _(b):
            chosen = bucket == b
            for head in range(heads):
                part = jnp.where(chosen, ds_sum[head], 0.0)
                bias_grad[head, b] = jnp.sum(part.reshape(SEQ // 8, 8, 2 * SEQ), axis=0)


def ffn_first_kernel(c0, c1, c2, c3, g0, g1, g2, g3, widen, narrow, c_all, g_all, h_ref, du_ref, dc_own, dc_rest):
    tokens = c0.shape[0]
    for i, (c, g) in enumerate(((c0, g0), (c1, g1), (c2, g2), (c3, g3))):
        c_all[i * tokens : (i + 1) * tokens, :] = c[...]
        g_all[i * tokens : (i + 1) * tokens, :] = g[...]
    inner = 0.7978845608028654
    for n in range(widen.shape[1] // 256):
        at = slice(n * 256, (n + 1) * 256)
        u = nn(c_all[...], widen[:, at])
        u2 = u * u
        th = jnp.tanh(inner * (u + 0.044715 * u * u2))
        h_ref[:, at] = (0.5 * u * (1.0 + th)).astype(bf16)
        slope = 0.5 * (1.0 + th) + (0.5 * inner) * u * (1.0 - th * th) * (1.0 + 3 * 0.044715 * u2)
        dh = nt(g_all[...], narrow[at, :])
        du_ref[:, at] = (dh * slope).astype(bf16)
    for n in range(widen.shape[0] // 256):
        at = slice(n * 256, (n + 1) * 256)
        dc = nt(du_ref[...], widen[at, :])
        dc_own[:, at] = dc[:tokens]
        for i in range(3):
            dc_rest[i, :, at] = dc[(i + 1) * tokens : (i + 2) * tokens].astype(bf16)


def ffn_second_kernel(c_all, g_all, h_ref, du_ref, narrow, out_own, out_rest, grad_ref):
    tokens = out_own.shape[0]
    hidden = narrow.shape[0]
    for n in range(narrow.shape[1] // 256):
        at = slice(n * 256, (n + 1) * 256)
        out = nn(h_ref[...], narrow[:, at])
        out_own[:, at] = out[:tokens]
        for i in range(3):
            out_rest[i, :, at] = out[(i + 1) * tokens : (i + 2) * tokens].astype(bf16)
    grad_ref[:, :hidden] = tn(c_all[...], du_ref[...]).astype(bf16)
    grad_ref[:, hidden:] = tn(g_all[...], h_ref[...]).astype(bf16)


def finish_kernel(total_ref, got1, got2, got3, query, key, value, merge):
    total = total_ref[...]
    for got in (got1, got2, got3):
        total = total + got[...].astype(f32)
    width = query.shape[1]
    for i, out in enumerate((query, key, value)):
        out[...] = total[:, i * width : (i + 1) * width]
    merge[...] = total[:, 3 * width :].T


def finish_ffn_kernel(sums, widen, narrow):
    hidden = widen.shape[1]
    widen[...] = sums[:, :hidden].astype(f32)
    narrow[...] = sums[:, hidden:].astype(f32).T


def table_kernel(place_ref, used_ref, out_ref):
    width = out_ref.shape[2]
    rows, entries = used_ref.shape[0], out_ref.shape[0]
    number = used_ref[:, width : width + 128].astype(f32)
    entry = number[:, 0:1] * 32.0 + number[:, 1:2]
    first = (place_ref[2] * entries).astype(f32)
    column = lax.broadcasted_iota(jnp.int32, (rows, entries), 1).astype(f32) + first
    row = lax.broadcasted_iota(jnp.int32, (rows, entries), 0)
    values = used_ref[:, :width]
    for p in range(PREFIX):
        chosen = jnp.logical_and(entry == column, row % PREFIX == p)
        out_ref[:, p, :] = tn(jnp.where(chosen, 1.0, 0.0).astype(bf16), values)


def pack_kernel(place_ref, *refs):
    out = refs[7]
    out[...] = jnp.zeros(out.shape, f32)
    for i in range(2):
        raw = refs[5 + i]
        heads, buckets = raw.shape[:2]
        sums = jnp.sum(jnp.sum(raw[...], axis=2), axis=-1)
        here = lax.broadcasted_iota(jnp.int32, (heads, 128), 0)
        column = lax.broadcasted_iota(jnp.int32, (heads, 128), 1)
        target = (here + place_ref[1] * (heads // 4)) % heads + i * heads
        turn = jnp.where(column == target, 1.0, 0.0)
        out[0:buckets, :] += lax.dot_general(
            sums,
            turn,
            (((0,), (0,)), ((), ())),
            precision=lax.Precision.HIGHEST,
            preferred_element_type=f32,
        )
    for i in range(5):
        for j in range(6):
            out[32 + 6 * i + j : 33 + 6 * i + j, :] = refs[i][:, 128 * j : 128 * (j + 1)]


def call(kernel, name, operands, smem, hbm, outs, scratch, limit=28):
    specs = []
    for i in range(len(operands)):
        if i in smem:
            specs.append(pl.BlockSpec(memory_space=pltpu.SMEM))
        elif i in hbm:
            specs.append(pl.BlockSpec(memory_space=pl.ANY))
        else:
            specs.append(pl.BlockSpec(memory_space=pltpu.VMEM))
    return pl.pallas_call(
        kernel,
        out_shape=[jax.ShapeDtypeStruct(shape, kind) for shape, kind in outs],
        in_specs=specs,
        out_specs=[pl.BlockSpec(memory_space=pltpu.VMEM)] * len(outs),
        scratch_shapes=scratch,
        compiler_params=pltpu.CompilerParams(vmem_limit_bytes=limit * 1024 * 1024),
        cost_estimate=pl.CostEstimate(flops=0, bytes_accessed=1024, transcendentals=0),
        name=name,
    )(*operands)


def weight_blocks(place, groups):
    count = len(groups)
    operands = [place]
    for query, key, value, merge in groups:
        operands += [query.T, key.T, value.T, merge]
    columns, rows = operands[1].shape
    return call(
        functools.partial(blocks_kernel, count),
        "weight_blocks",
        operands,
        (0,),
        range(1, len(operands)),
        [
            ((4 * columns // BLOCKS, rows), bf16),
            ((count - 1, 4 * columns // BLOCKS, rows), bf16),
        ],
        [pltpu.SemaphoreType.DMA((count,))],
        60,
    )


def attention_forward(kind, place, x, extra, gains, rel, weights):
    rows, width = x.shape
    extra_rows = extra.shape[0] if kind == "encoder" else 0
    keys = rows + extra_rows
    operands = [place, x]
    if extra is not None:
        operands.append(extra)
    operands.append(gains)
    if rel is not None:
        operands.append(rel)
    hbm = (len(operands),) if len(weights) == 1 else ()
    operands += weights
    return call(
        functools.partial(attention_forward_kernel, kind, len(weights)),
        kind + "_forward",
        operands,
        (0,),
        hbm,
        [
            ((rows, width), f32),
            ((rows, width), bf16),
            ((keys, width), bf16),
            ((4, rows, 192), bf16),
            ((4, keys, 384), bf16),
            ((4, rows, 192), bf16),
        ],
        [pltpu.VMEM((4, BLOCKS, width // BLOCKS, width), bf16), pltpu.SemaphoreType.DMA((4, 2))],
        56 if len(weights) == 1 else 28,
    )


def attention_backward(kind, place, ffn, upstream, x, gains, stored, source, weights, rel, bucket, buckets):
    rows, width = upstream.shape
    a, q, kv, o = stored
    keys = kv.shape[1]
    operands = [place]
    if ffn is not None:
        dc_own, dc_rest, r1 = ffn
        operands += [dc_own, *dc_rest, upstream, r1]
    else:
        operands += [upstream]
    operands += [x, gains, a]
    if source is not None:
        operands.append(source)
    operands += [q, kv, o]
    hbm = (len(operands),) if len(weights) == 1 else ()
    operands += weights
    if kind != "cross":
        operands += [rel, bucket]
    block = width // BLOCKS
    outs = [
        ((rows, width), f32),
        ((1, width), f32),
    ]
    outs += [((2, 4, 2, block, width), bf16)] * 2
    if ffn is not None:
        outs.append(((1, width), f32))
    if kind == "encoder":
        outs.append(((keys - rows, width), bf16))
    elif kind == "cross":
        outs.append(((rows, width), f32))
    if kind != "cross":
        outs.append(((rel.shape[0], buckets, 8, 2 * SEQ), f32))
    depth = 2 * rows + (keys if kind == "cross" else keys - rows)
    scratch = [
        pltpu.VMEM((4, BLOCKS, block, width), bf16),
        pltpu.SemaphoreType.DMA((4, 2)),
        pltpu.VMEM((width, depth), bf16),
        pltpu.VMEM((4, depth, width), bf16),
    ]
    if kind != "cross":
        scratch.append(pltpu.VMEM((rel.shape[0], SEQ, 2 * SEQ), f32))
    scratch.append(pltpu.VMEM((width, width), bf16))
    return call(
        functools.partial(attention_backward_kernel, kind, len(weights), ffn is not None),
        kind + "_backward",
        operands,
        (0,),
        hbm,
        outs,
        scratch,
        56 if len(weights) == 1 else 28,
    )


def ffn_first(name, c_parts, g_parts, widen, narrow):
    tokens, width = c_parts[0].shape
    hidden = widen.shape[1]
    every = 4 * tokens
    return call(
        ffn_first_kernel,
        name + "_first",
        [*c_parts, *g_parts, widen, narrow],
        (),
        (),
        [
            ((every, width), bf16),
            ((every, width), bf16),
            ((every, hidden), bf16),
            ((every, hidden), bf16),
            ((tokens, width), f32),
            ((3, tokens, width), bf16),
        ],
        [],
    )


def ffn_second(name, c_all, g_all, h, du, narrow):
    every, width = c_all.shape
    hidden = h.shape[1]
    tokens = every // 4
    return call(
        ffn_second_kernel,
        name + "_second",
        [c_all, g_all, h, du, narrow],
        (),
        (),
        [((tokens, width), f32), ((3, tokens, width), bf16), ((width, 2 * hidden), bf16)],
        [],
    )


def gather_tokens(part):
    return [part] + [from_mp(part, step) for step in range(1, 4)]


def return_tokens(rest):
    return [to_mp(rest[step - 1], step) for step in range(1, 4)]


def relative_bias(bucket, table, heads_here):
    twice = jnp.concatenate([bucket, bucket], axis=1)
    onehot = (
        lax.broadcasted_iota(jnp.int32, (table.shape[0], 1), 0) == twice.reshape(1, -1)
    ).astype(f32)
    start = lax.axis_index("mp") * heads_here
    columns = jnp.concatenate([table.T, table.T], axis=0)
    ordered = lax.dynamic_slice_in_dim(columns, start, table.shape[1], 0)
    looked = jnp.dot(ordered, onehot, precision=lax.Precision.HIGHEST)
    return looked.reshape(table.shape[1], SEQ, 2 * SEQ), twice


def shards(
    encoder_input,
    encoder_upstream,
    memory_index,
    memory_table,
    encoder_bucket,
    encoder_bias,
    encoder_gain,
    encoder_query,
    encoder_key,
    encoder_value,
    encoder_merge,
    encoder_later_gain,
    encoder_widen,
    encoder_narrow,
    decoder_input,
    decoder_upstream,
    encoder_states,
    decoder_bucket,
    decoder_bias,
    decoder_gain,
    decoder_query,
    decoder_key,
    decoder_value,
    decoder_merge,
    cross_gain,
    cross_query,
    cross_key,
    cross_value,
    cross_merge,
    decoder_later_gain,
    decoder_widen,
    decoder_narrow,
):
    heads_here = encoder_query.shape[1] // DH
    width = encoder_input.shape[1]
    dp_at = lax.axis_index("dp")
    mp_at = lax.axis_index("mp")
    place = dp_at // (lax.axis_size("dp") // BLOCKS)
    place_in = jnp.stack([place, mp_at, dp_at * lax.axis_size("mp") + mp_at]).astype(jnp.int32)

    encoder_block, decoder_blocks = weight_blocks(
        place_in,
        [
            (encoder_query, encoder_key, encoder_value, encoder_merge),
            (decoder_query, decoder_key, decoder_value, decoder_merge),
            (cross_query, cross_key, cross_value, cross_merge),
        ],
    )
    encoder_others = gather_tokens(encoder_block)[1:]
    decoder_weights = (gather_blocks(decoder_blocks),)

    own_questions = memory_index.shape[0] // lax.axis_size("mp")
    entries = lax.dynamic_slice_in_dim(
        memory_index, mp_at * own_questions, own_questions, 0
    ).reshape(-1)
    prefix = jnp.take(memory_table, entries, axis=0).reshape(-1, width)
    prefix_rows = prefix.shape[0]
    prefix = jnp.pad(prefix, ((0, -prefix_rows % 64), (0, 0)))
    encoder_rel, encoder_twice = relative_bias(encoder_bucket, encoder_bias, heads_here)
    decoder_rel, decoder_twice = relative_bias(decoder_bucket, decoder_bias, heads_here)
    entry_rows = jnp.repeat(entries, PREFIX)
    numbers = jnp.stack([entry_rows // 32, entry_rows % 32], axis=1).astype(bf16)
    numbers = jnp.pad(numbers, ((0, 0), (0, 126)))
    gains = jnp.stack(
        [encoder_gain, encoder_later_gain, decoder_gain, cross_gain, decoder_later_gain]
    )
    small = (prefix, encoder_rel, encoder_twice, decoder_rel, decoder_twice, numbers, gains)
    small = after(small, encoder_block)
    prefix, encoder_rel, encoder_twice, decoder_rel, decoder_twice, numbers, gains = small

    first, second = stack_slots(after(encoder_block, small), encoder_others)
    first_got, second_got = spread_once(first, second)
    encoder_g = gather_tokens(after(encoder_upstream, encoder_others))
    pairs = after(
        (jnp.stack([first, first_got]), jnp.stack([second, second_got])), encoder_g
    )
    fars = spread_twice(*pairs)
    decoder_g = gather_tokens(after(decoder_upstream, encoder_g))
    encoder_own = after(join_places(*pairs, *fars), decoder_g)
    encoder_weights = (encoder_own, swap_cores(encoder_own))

    encoder_r1, encoder_c, *encoder_stored = attention_forward(
        "encoder", place_in, encoder_input, prefix, gains, encoder_rel, encoder_weights
    )
    encoder_c = gather_tokens(encoder_c)
    c_all, g_all, h, du, dc_own, dc_rest = ffn_first(
        "encoder_ffn", encoder_c, encoder_g, encoder_widen, encoder_narrow
    )
    encoder_dc = (dc_own, return_tokens(dc_rest))
    out_own, out_rest, grads = ffn_second("encoder_ffn", c_all, g_all, h, du, encoder_narrow)
    encoder_ffn_sums = reduce_ffn(grads)
    (
        encoder_input_grad,
        encoder_gain_grad,
        keep,
        send,
        encoder_later_grad,
        prefix_grad,
        encoder_bias_raw,
    ) = attention_backward(
        "encoder",
        after(place_in, out_own),
        (*encoder_dc, encoder_r1),
        encoder_upstream,
        encoder_input,
        gains,
        encoder_stored,
        None,
        encoder_weights,
        encoder_rel,
        encoder_twice,
        encoder_bias.shape[0],
    )
    encoder_got = swap_cores(send)
    packed = jnp.concatenate([prefix_grad[:prefix_rows], numbers], axis=1)
    used = lax.all_gather(packed, ("dp", "mp"), axis=0, tiled=True)
    encoder_halves = fold_cores(after(keep, packed), encoder_got)
    encoder_once = send_once(encoder_halves)

    self_r1, _, *self_stored = attention_forward(
        "self", after(place_in, encoder_halves), decoder_input, None, gains, decoder_rel, decoder_weights
    )
    cross_r2, decoder_c, *cross_stored = attention_forward(
        "cross", place_in, self_r1, encoder_states, gains, None, decoder_weights
    )
    decoder_c = gather_tokens(decoder_c)
    encoder_last = fold_once(after(encoder_halves, cross_r2), encoder_once)
    encoder_twice_got = send_twice(encoder_last)
    c_all, g_all, h, du, dc_own, dc_rest = ffn_first(
        "decoder_ffn",
        [after(decoder_c[0], encoder_last), *decoder_c[1:]],
        decoder_g,
        decoder_widen,
        decoder_narrow,
    )
    decoder_dc = (dc_own, return_tokens(after(dc_rest, encoder_twice_got)))
    out_own_d, out_rest_d, grads = ffn_second(
        "decoder_ffn", c_all, g_all, h, du, decoder_narrow
    )
    decoder_ffn_sums = reduce_ffn(grads)
    encoder_sums = fold_twice(
        after(encoder_halves, out_own_d), encoder_once, encoder_twice_got
    )
    encoder_widen_grad, encoder_narrow_grad = two_matrices(after(encoder_ffn_sums, encoder_sums))
    encoder_sent = send_slots(after(encoder_sums, decoder_dc))

    cross_dx, cross_gain_grad, keep, send, decoder_later_grad, states_grad = attention_backward(
        "cross",
        after(place_in, encoder_narrow_grad),
        (*decoder_dc, cross_r2),
        decoder_upstream,
        self_r1,
        gains,
        cross_stored,
        encoder_states,
        decoder_weights,
        None,
        None,
        None,
    )
    cross_got = swap_cores(after(send, encoder_sent))
    cross_halves = fold_cores(keep, cross_got)
    cross_once = send_once(cross_halves)
    encoder_out = return_tokens(after(out_rest, encoder_sent))
    decoder_input_grad, decoder_gain_grad, keep, send, decoder_bias_raw = attention_backward(
        "self",
        after(place_in, cross_halves),
        None,
        cross_dx,
        decoder_input,
        gains,
        self_stored,
        None,
        decoder_weights,
        decoder_rel,
        decoder_twice,
        decoder_bias.shape[0],
    )
    self_got = swap_cores(after(send, cross_once, encoder_out))
    cross_last = fold_once(after(cross_halves, decoder_input_grad), cross_once)
    cross_twice_got = send_twice(cross_last)
    sums = call(
        pack_kernel,
        "pack",
        [
            after(place_in, cross_last),
            encoder_gain_grad,
            encoder_later_grad,
            decoder_gain_grad,
            cross_gain_grad,
            decoder_later_grad,
            encoder_bias_raw,
            decoder_bias_raw,
        ],
        (0,),
        (),
        [((64, 128), f32)],
        [],
    )[0]
    self_halves = fold_cores(keep, after(self_got, sums))
    self_once = send_once(self_halves)
    decoder_out = return_tokens(after(out_rest_d, encoder_out))

    encoder_mats = four_matrices(after(encoder_sums, self_halves), encoder_sent)
    encoder_output = (
        after(encoder_r1, self_halves) + out_own + sum(part.astype(f32) for part in encoder_out)
    ).astype(bf16)
    sums = sum_everywhere(after(sums, self_halves))
    cross_sums = fold_twice(after(cross_halves, encoder_mats), cross_once, cross_twice_got)
    self_last = fold_once(self_halves, after(self_once, cross_sums))
    self_twice_got = send_twice(self_last)
    cross_sent = send_slots(after(cross_sums, self_last, decoder_out))

    table_rows = memory_table.shape[0] // (lax.axis_size("dp") * lax.axis_size("mp"))
    table_grad = call(
        table_kernel,
        "table",
        [after(place_in, self_last), used],
        (0,),
        (),
        [((table_rows, PREFIX, width), f32)],
        [],
    )[0]
    decoder_widen_grad, decoder_narrow_grad = two_matrices(after(decoder_ffn_sums, self_last))
    decoder_output = (
        after(cross_r2, self_last) + out_own_d + sum(part.astype(f32) for part in decoder_out)
    ).astype(bf16)
    self_sums = fold_twice(
        after(self_halves, table_grad, decoder_narrow_grad), self_once, self_twice_got
    )
    self_sent = send_slots(after(self_sums, cross_sent))
    cross_mats = four_matrices(after(cross_sums, self_sums), cross_sent)
    self_mats = four_matrices(self_sums, self_sent)

    gain_sums = [sums[32 + 6 * i : 38 + 6 * i].reshape(-1) for i in range(5)]
    buckets, heads = encoder_bias.shape
    bias_grads = [sums[:buckets, i * heads : (i + 1) * heads] for i in range(2)]
    return (
        encoder_output,
        encoder_input_grad,
        table_grad,
        bias_grads[0],
        gain_sums[0],
        *encoder_mats,
        gain_sums[1],
        encoder_widen_grad,
        encoder_narrow_grad,
        decoder_output,
        decoder_input_grad,
        states_grad,
        bias_grads[1],
        gain_sums[2],
        *self_mats,
        gain_sums[3],
        *cross_mats,
        gain_sums[4],
        decoder_widen_grad,
        decoder_narrow_grad,
    )


def solution(mesh):
    rows = P(("dp", "mp"), None)
    columns = P(None, "mp")
    lines = P("mp", None)
    attention = (columns, columns, columns, lines)
    in_specs = (
        (rows, rows, P("dp", None), P(), P(), P(), P())
        + attention
        + (P(), columns, lines, rows, rows, rows, P(), P(), P())
        + attention
        + (P(),)
        + attention
        + (P(), columns, lines)
    )
    both = P("dp", "mp")
    turned = P("mp", "dp")
    grads = (both, both, both, turned)
    out_specs = (
        (rows, rows, P(("dp", "mp"), None, None), P(), P())
        + grads
        + (P(), both, turned, rows, rows, rows, P(), P())
        + grads
        + (P(),)
        + grads
        + (P(), both, turned)
    )
    return jax.shard_map(shards, mesh=mesh, in_specs=in_specs, out_specs=out_specs, check_vma=False)
```

```python
import functools

import jax
import jax.numpy as jnp
from jax import lax
from jax.experimental import pallas as pl
from jax.experimental.pallas import tpu as pltpu
from jax.sharding import PartitionSpec as P

DH = 64
SEQ = 64
MEMK = 10
PREFIX = 2
EPS = 1e-06
NEG = -1e30
BLOCKS = 8
bf16 = jnp.bfloat16
f32 = jnp.float32


def nn(left, right):
    return lax.dot_general(left, right, (((1,), (0,)), ((), ())), preferred_element_type=f32)


def nt(left, right):
    return lax.dot_general(left, right, (((1,), (1,)), ((), ())), preferred_element_type=f32)


def tn(left, right):
    return lax.dot_general(left, right, (((0,), (0,)), ((), ())), preferred_element_type=f32)


def from_mp(array, step):
    size = lax.axis_size("mp")
    return lax.ppermute(array, "mp", [(i, (i - step) % size) for i in range(size)])


def to_mp(array, step):
    size = lax.axis_size("mp")
    return lax.ppermute(array, "mp", [(i, (i + step) % size) for i in range(size)])


def swap_dp(array, bit):
    return lax.ppermute(array, "dp", [(i, i ^ bit) for i in range(lax.axis_size("dp"))])


def after(value, *earlier):
    leaves, shape = jax.tree.flatten(value)
    tied = lax.optimization_barrier((*leaves, *jax.tree.leaves(earlier)))
    return jax.tree.unflatten(shape, tied[: len(leaves)])


def high_bits():
    low = lax.axis_size("dp") // BLOCKS
    return low, 2 * low, 4 * low


def rounded_sum(left, right):
    return (left.astype(f32) + right.astype(f32)).astype(bf16)


def swap_cores(array):
    return swap_dp(array, high_bits()[0])


def fold_cores(keep, got):
    return tuple(
        (rounded_sum(keep[i, :2], got[i, :2]), rounded_sum(keep[i, 2:], got[i, 2:])) for i in range(2)
    )


def send_once(halves):
    core, along, across = high_bits()
    return swap_dp(halves[0][1], along), swap_dp(halves[1][1], across)


def fold_once(halves, got):
    return tuple(rounded_sum(halves[i][0][1], got[i][1]) for i in range(2))


def send_twice(last):
    core, along, across = high_bits()
    return swap_dp(last[0], across), swap_dp(last[1], along)


def fold_twice(halves, got, last_got):
    sums = [
        halves[i][0][0].astype(f32) + got[i][0].astype(f32) + last_got[i].astype(f32) for i in range(2)
    ]
    return [sums[0][0], sums[0][1], sums[1][0], sums[1][1]] + [part[i] for i in range(2, sums[0].shape[0]) for part in sums]


def send_slots(slots):
    return [to_mp(slots[step].astype(bf16), step) for step in range(1, 4)]


def scatter_rest(rows):
    size = lax.axis_size("dp")
    low = size // BLOCKS
    if low == 1:
        return rows
    groups = [[high * low + i for i in range(low)] for high in range(BLOCKS)]
    return lax.psum_scatter(
        rows, "dp", scatter_dimension=0, axis_index_groups=groups, tiled=True
    )


def four_matrices(slots, got):
    total = slots[0]
    if lax.axis_size("dp") == BLOCKS:
        rows, width = total.shape
        part = width // 4
        return call(
            finish_kernel,
            "matrices",
            [total, *got],
            (),
            (),
            [((rows, part), f32)] * 3 + [((part, rows), f32)],
            [],
        )
    for other in got:
        total = total + other.astype(f32)
    total = scatter_rest(total)
    width = total.shape[1] // 4
    parts = [total[:, i * width : (i + 1) * width] for i in range(4)]
    return parts[0], parts[1], parts[2], parts[3].T


def two_matrices(widen, narrow):
    return scatter_rest(widen), scatter_rest(narrow).T


def gather_blocks(slots):
    low = lax.axis_size("dp") // BLOCKS
    groups = [[high * low + i for high in range(BLOCKS)] for i in range(low)]
    if low == 1:
        groups = None
    return lax.all_gather(slots, "dp", axis=0, axis_index_groups=groups, tiled=False)


def sum_over(axis, array):
    size = lax.axis_size(axis)
    bit = 1
    while bit < size:
        array = array + lax.ppermute(array, axis, [(i, i ^ bit) for i in range(size)])
        bit *= 2
    return array


def fetch_weights(weights, group, held, sems, order):
    copies = {}
    for i, what in enumerate(order):
        blocks = pl.ds(6, 2) if what == "merge" else pl.ds(0, 6)
        for slot in range(4):
            copies[what, slot] = pltpu.make_async_copy(
                weights.at[blocks, slot, group], held.at[slot, blocks], sems.at[slot, i]
            )
            copies[what, slot].start()
    return copies


def slot_rows(held, slot, first, last):
    part = held[slot, 2 * first : 2 * last]
    return part.reshape(part.shape[0] * part.shape[1], part.shape[2])


def wait_all(copies):
    for copy in copies:
        copy.wait()


def blocks_kernel(groups, place_ref, *refs):
    inputs = refs[: 4 * groups]
    first, others, sems = refs[4 * groups :]
    outs = [first] + [others.at[i] for i in range(groups - 1)]
    size = first.shape[0]
    place = place_ref[0]
    start = pl.multiple_of((place % 2) * size, size)
    for j in range(4):

        @pl.when(place // 2 == j)
        def _():
            copies = [
                pltpu.make_async_copy(inputs[4 * i + j].at[pl.ds(start, size)], outs[i], sems.at[i])
                for i in range(groups)
            ]
            for copy in copies:
                copy.start()
            wait_all(copies)


def inverse_rms(rows):
    return lax.rsqrt(jnp.mean(rows * rows, axis=-1, keepdims=True) + EPS)


def gain_rows(kind, gains_ref):
    at = {"encoder": (0, 1), "self": (2, 3), "cross": (3, 4)}[kind]
    return tuple(gains_ref[i : i + 1, :] for i in at)


def column_head(shape):
    return lax.broadcasted_iota(jnp.int32, shape, 1) // DH


def softmax_rows(scores):
    shifted = jnp.exp(scores - jnp.max(scores, axis=-1, keepdims=True))
    return shifted / jnp.sum(shifted, axis=-1, keepdims=True)


def masks(kind, rows, keys):
    row = lax.broadcasted_iota(jnp.int32, (rows, rows), 0)
    col = lax.broadcasted_iota(jnp.int32, (rows, rows), 1)
    same = row // SEQ == col // SEQ
    if kind == "self":
        same = jnp.logical_and(same, col <= row)
    if kind != "encoder":
        return same, None
    row = lax.broadcasted_iota(jnp.int32, (rows, keys - rows), 0)
    col = lax.broadcasted_iota(jnp.int32, (rows, keys - rows), 1)
    first = (row // SEQ) * (MEMK * PREFIX)
    valid = jnp.logical_and(col >= first, col < first + MEMK * PREFIX)
    return same, jnp.where(valid, 0.0, NEG)


def add_bias(kind, scores, rel_ref, slot, same, before):
    rows = scores.shape[0] // 3
    parts = []
    for j in range(3):
        part = scores[j * rows : (j + 1) * rows]
        own = part[:, :rows]
        if kind != "cross":
            rel = rel_ref[3 * slot + j]
            own = own + jnp.concatenate([rel] * (rows // SEQ), axis=0)
        own = jnp.where(same, own, NEG)
        if before is not None:
            own = jnp.concatenate([own, part[:, rows:] + before], axis=1)
        parts.append(own)
    return jnp.concatenate(parts, axis=0)


def stack_heads(array):
    head = column_head(array.shape)
    return jnp.concatenate([jnp.where(head == j, array, jnp.zeros_like(array)) for j in range(3)], axis=0)


def join_heads(stacked):
    rows = stacked.shape[0] // 3
    head = column_head((rows, stacked.shape[1]))
    return jnp.where(
        head == 0,
        stacked[:rows],
        jnp.where(head == 1, stacked[rows : 2 * rows], stacked[2 * rows :]),
    )


def attention_forward_kernel(kind, *refs):
    refs = list(refs)
    place_ref, x_ref = refs[:2]
    del refs[:2]
    pre_ref = refs.pop(0) if kind != "self" else None
    gains_ref = refs.pop(0)
    gain, later = gain_rows(kind, gains_ref)
    rel_ref = refs.pop(0) if kind != "cross" else None
    weights, r1_ref, next_ref, a_ref, q_ref, kv_ref, o_ref, held, sems = refs
    copies = fetch_weights(weights, int(kind == "cross"), held, sems, ("rest", "merge"))
    r = x_ref[...].astype(f32)
    rows = r.shape[0]
    a = (r * inverse_rms(r) * gain).astype(bf16)
    if kind == "encoder":
        a_ref[0:rows, :] = a
        a_ref[rows:, :] = pre_ref[...]
        a_all = a_ref[...]
    else:
        a_ref[...] = a
        a_all = a
    keys = kv_ref.shape[1]
    same, before = masks(kind, rows, keys)
    queries = []
    sources = []
    for slot in range(4):
        copies["rest", slot].wait()
        if kind == "cross":
            q = nt(a, slot_rows(held, slot, 0, 1)).astype(bf16)
            kv = nt(pre_ref[...], slot_rows(held, slot, 1, 3)).astype(bf16)
        else:
            qkv = nt(a_all, slot_rows(held, slot, 0, 3)).astype(bf16)
            q = qkv[:rows, :192]
            kv = qkv[:, 192:]
        q_ref[slot] = q
        kv_ref[slot] = kv
        queries.append(q)
        sources.append(kv)
    chances = []
    for slot in range(4):
        scores = nt(stack_heads(queries[slot]), sources[slot][:, :192])
        chances.append(softmax_rows(add_bias(kind, scores, rel_ref, slot, same, before)).astype(bf16))
    mixed = []
    for slot in range(4):
        o = join_heads(nn(chances[slot], sources[slot][:, 192:])).astype(bf16)
        o_ref[slot] = o
        mixed.append(o)
    acc = r
    for slot in range(4):
        copies["merge", slot].wait()
        acc = acc + nn(mixed[slot], slot_rows(held, slot, 3, 4))
    r1_ref[...] = acc
    next_ref[...] = (acc * inverse_rms(acc) * later).astype(bf16)


def norm_back(dn, r, gain, dgain_ref):
    t = inverse_rms(r)
    dgain_ref[...] = jnp.sum(dn * r * t, axis=0, keepdims=True)
    scaled = dn * gain
    return t * (scaled - r * (t * t) * jnp.mean(scaled * r, axis=-1, keepdims=True))


def attention_backward_kernel(kind, after_ffn, *refs):
    refs = list(refs)
    place_ref = refs.pop(0)
    place = place_ref[0]
    if after_ffn:
        dc_own, *dc_rest = refs[:4]
        up_ref, r1_ref = refs[4:6]
        refs = refs[6:]
    else:
        up_ref = refs.pop(0)
    x_ref, gains_ref, a_ref = refs[:3]
    gain, later = gain_rows(kind, gains_ref)
    refs = refs[3:]
    source_ref = refs.pop(0) if kind == "cross" else None
    q_ref, kv_ref, o_ref = refs[:3]
    weights = refs[3]
    refs = refs[4:]
    rel_ref, bucket_ref = (refs.pop(0), refs.pop(0)) if kind != "cross" else (None, None)
    if kind != "self":
        refs = refs[2:]
    dx_ref, dgain_ref = refs[:2]
    refs = refs[2:]
    keep_ref, send_ref = refs.pop(0), refs.pop(0)
    later_grad = refs.pop(0) if after_ffn else None
    if kind == "encoder":
        dpre_ref = refs.pop(0)
    elif kind == "cross":
        dsource_ref = refs.pop(0)
    bias_grad = refs.pop(0) if kind != "cross" else None
    held, sems, left, right = refs[:4]
    refs = refs[4:]
    ds_sum = refs.pop(0) if kind != "cross" else None
    stage, out_sems = refs
    copies = fetch_weights(weights, int(kind == "cross"), held, sems, ("merge", "rest"))

    d_out = up_ref[...].astype(f32)
    if after_ffn:
        dn = dc_own[...]
        for part in dc_rest:
            dn = dn + part[...].astype(f32)
        d_out = d_out + norm_back(dn, r1_ref[...], later, later_grad)
    g = d_out.astype(bf16)
    rows, width = g.shape
    keys = kv_ref.shape[1]
    stacked = [a_ref[...]] + ([source_ref[...]] if kind == "cross" else []) + [g]
    turned = jnp.concatenate(stacked, axis=0).T
    size = width // BLOCKS
    for d in range(BLOCKS):
        away = place ^ d
        at = pl.multiple_of(((away % 2) * 4 + away // 2) * size, size)
        left[pl.ds(at, size), :] = turned[d * size : (d + 1) * size]
    source_at = rows if kind == "cross" else 0
    g_at = left.shape[1] - rows
    right[...] = jnp.zeros(right.shape, bf16)
    same, before = masks(kind, rows, keys)
    grads = []
    for slot in range(4):
        copies["merge", slot].wait()
        grads.append(nt(g, slot_rows(held, slot, 3, 4)).astype(bf16))
        right[slot, g_at:, 576:768] = o_ref[slot]
    chances = []
    for slot in range(4):
        scores = nt(stack_heads(q_ref[slot]), kv_ref[slot][:, :192])
        chances.append(softmax_rows(add_bias(kind, scores, rel_ref, slot, same, before)))
    d_scores = []
    for slot in range(4):
        p = chances[slot]
        do_heads = stack_heads(grads[slot])
        dv = tn(p.astype(bf16), do_heads).astype(bf16)
        right[slot, source_at : source_at + keys, 384:576] = dv
        dp = nt(do_heads, kv_ref[slot][:, 192:])
        ds = (p * (dp - jnp.sum(dp * p, axis=-1, keepdims=True))).astype(bf16)
        d_scores.append(ds)
    for slot in range(4):
        ds = d_scores[slot]
        right[slot, 0:rows, 0:192] = join_heads(nn(ds, kv_ref[slot][:, :192])).astype(bf16)
        right[slot, source_at : source_at + keys, 192:384] = tn(ds, stack_heads(q_ref[slot])).astype(bf16)
        if kind != "cross":
            for j in range(3):
                wide = ds[j * rows : (j + 1) * rows, :rows].astype(f32)
                ds_sum[3 * slot + j] = wide[:SEQ] + wide[SEQ:]
    outgoing = []
    for slot in range(4):
        grad = nn(left[...], right[slot]).astype(bf16)
        for j in range(BLOCKS):
            to = (j // 4) * 4 + ((j % 2) * 2 + (j % 4) // 2 if slot // 2 == 0 else j % 4)
            stage[slot, to] = grad[j * size : (j + 1) * size]
        for i, out in enumerate((keep_ref, send_ref)):
            copy = pltpu.make_async_copy(
                stage.at[slot, pl.ds(4 * i, 4)], out.at[slot // 2, :, slot % 2], out_sems.at[slot, i]
            )
            copy.start()
            outgoing.append(copy)
    total = None
    source_total = None
    for slot in range(4):
        copies["rest", slot].wait()
        if kind == "cross":
            part = nn(right[slot, 0:rows, 0:192], slot_rows(held, slot, 0, 1))
            other = nn(right[slot, rows : rows + keys, 192:576], slot_rows(held, slot, 1, 3))
            source_total = other if slot == 0 else source_total + other
        else:
            part = nn(right[slot, 0:keys, 0:576], slot_rows(held, slot, 0, 3))
        total = part if slot == 0 else total + part
    if kind == "cross":
        dsource_ref[...] = source_total
    if kind == "encoder":
        dpre_ref[...] = total[rows:].astype(bf16)
    dx_ref[...] = d_out + norm_back(total[:rows], x_ref[...].astype(f32), gain, dgain_ref)
    if kind != "cross":
        bucket = bucket_ref[...]
        heads, buckets = bias_grad.shape[:2]

        @pl.loop(0, buckets)
        def _(b):
            chosen = bucket == b
            for head in range(heads):
                part = jnp.where(chosen, ds_sum[head], 0.0)
                bias_grad[head, b] = jnp.sum(part.reshape(SEQ // 8, 8, 2 * SEQ), axis=0)

    wait_all(outgoing)


def ffn_first_kernel(c0, c1, c2, c3, g0, g1, g2, g3, widen, narrow, c_all, g_all, h_ref, du_ref, dc_own, dc_rest):
    tokens = c0.shape[0]
    for i, (c, g) in enumerate(((c0, g0), (c1, g1), (c2, g2), (c3, g3))):
        c_all[i * tokens : (i + 1) * tokens, :] = c[...]
        g_all[i * tokens : (i + 1) * tokens, :] = g[...]
    inner = 0.7978845608028654
    for n in range(widen.shape[1] // 256):
        at = slice(n * 256, (n + 1) * 256)
        u = nn(c_all[...], widen[:, at])
        u2 = u * u
        th = jnp.tanh(inner * (u + 0.044715 * u * u2))
        h_ref[:, at] = (0.5 * u * (1.0 + th)).astype(bf16)
        slope = 0.5 * (1.0 + th) + (0.5 * inner) * u * (1.0 - th * th) * (1.0 + 3 * 0.044715 * u2)
        dh = nt(g_all[...], narrow[at, :])
        du_ref[:, at] = (dh * slope).astype(bf16)
    for n in range(widen.shape[0] // 256):
        at = slice(n * 256, (n + 1) * 256)
        dc = nt(du_ref[...], widen[at, :])
        dc_own[:, at] = dc[:tokens]
        for i in range(3):
            dc_rest[i, :, at] = dc[(i + 1) * tokens : (i + 2) * tokens].astype(bf16)


def ffn_second_kernel(across, place_ref, c_all, g_all, h_ref, du_ref, narrow, *refs):
    outs = refs[:-4]
    keep_ref, send_ref, stage, sems = refs[-4:]
    tokens = c_all.shape[0] // 4
    place = place_ref[0]
    copies = []
    for half, (left, right) in enumerate(((c_all, du_ref), (g_all, h_ref))):
        grad = tn(left[...], right[...]).astype(bf16)
        size = grad.shape[0] // BLOCKS
        for d in range(BLOCKS):
            away = place ^ d
            where = away // 2
            if half == 0:
                where = (where % 2) * 2 + where // 2
            stage[half, (away % 2) * 4 + where] = grad[d * size : (d + 1) * size]
        for i, ref in enumerate((keep_ref, send_ref)):
            copy = pltpu.make_async_copy(
                stage.at[half, pl.ds(4 * i, 4)], ref.at[half, :, 2], sems.at[half, i]
            )
            copy.start()
            copies.append(copy)
    for n in range(narrow.shape[1] // 256):
        at = slice(n * 256, (n + 1) * 256)
        out = nn(h_ref[...], narrow[:, at])
        for i in range(4):
            part = out[i * tokens : (i + 1) * tokens]
            if across:
                row = pl.multiple_of((place_ref[1] + i) % 4 * tokens, tokens)
                outs[0][pl.ds(row, tokens), at] = part.astype(bf16)
            else:
                outs[i][:, at] = part.astype(outs[i].dtype)
    wait_all(copies)


def gains_kernel(*refs):
    for i in range(5):
        refs[5][i : i + 1, :] = refs[i][...].reshape(1, -1)


def finish_kernel(total_ref, got1, got2, got3, query, key, value, merge):
    total = total_ref[...]
    for got in (got1, got2, got3):
        total = total + got[...].astype(f32)
    width = query.shape[1]
    for i, out in enumerate((query, key, value)):
        out[...] = total[:, i * width : (i + 1) * width]
    merge[...] = total[:, 3 * width :].T


def table_kernel(place_ref, used_ref, out_ref):
    width = out_ref.shape[2]
    rows, entries = used_ref.shape[0], out_ref.shape[0]
    number = used_ref[:, width : width + 128].astype(f32)
    entry = number[:, 0:1] * 32.0 + number[:, 1:2]
    first = (place_ref[2] * entries).astype(f32)
    column = lax.broadcasted_iota(jnp.int32, (rows, entries), 1).astype(f32) + first
    row = lax.broadcasted_iota(jnp.int32, (rows, entries), 0)
    values = used_ref[:, :width]
    for p in range(PREFIX):
        chosen = jnp.logical_and(entry == column, row % PREFIX == p)
        out_ref[:, p, :] = tn(jnp.where(chosen, 1.0, 0.0).astype(bf16), values)


def pack_kernel(place_ref, *refs):
    out = refs[7]
    out[...] = jnp.zeros(out.shape, f32)
    for i in range(2):
        raw = refs[5 + i]
        heads, buckets = raw.shape[:2]
        sums = jnp.sum(jnp.sum(raw[...], axis=2), axis=-1)
        here = lax.broadcasted_iota(jnp.int32, (heads, 128), 0)
        column = lax.broadcasted_iota(jnp.int32, (heads, 128), 1)
        target = (here + place_ref[1] * (heads // 4)) % heads + i * heads
        turn = jnp.where(column == target, 1.0, 0.0)
        out[0:buckets, :] += lax.dot_general(
            sums,
            turn,
            (((0,), (0,)), ((), ())),
            precision=lax.Precision.HIGHEST,
            preferred_element_type=f32,
        )
    for i in range(5):
        for j in range(6):
            out[32 + 6 * i + j : 33 + 6 * i + j, :] = refs[i][:, 128 * j : 128 * (j + 1)]


def call(kernel, name, operands, smem, hbm, outs, scratch, limit=28, hbm_outs=(), aliases=None):
    specs = []
    for i in range(len(operands)):
        if i in smem:
            specs.append(pl.BlockSpec(memory_space=pltpu.SMEM))
        elif i in hbm:
            specs.append(pl.BlockSpec(memory_space=pl.ANY))
        else:
            specs.append(pl.BlockSpec(memory_space=pltpu.VMEM))
    return pl.pallas_call(
        kernel,
        out_shape=[jax.ShapeDtypeStruct(shape, kind) for shape, kind in outs],
        in_specs=specs,
        out_specs=[
            pl.BlockSpec(memory_space=pl.ANY if i in hbm_outs else pltpu.VMEM)
            for i in range(len(outs))
        ],
        scratch_shapes=scratch,
        input_output_aliases=aliases or {},
        compiler_params=pltpu.CompilerParams(vmem_limit_bytes=limit * 1024 * 1024),
        cost_estimate=pl.CostEstimate(flops=0, bytes_accessed=1024, transcendentals=0),
        name=name,
    )(*operands)


def weight_blocks(place, groups):
    count = len(groups)
    operands = [place]
    for query, key, value, merge in groups:
        operands += [query.T, key.T, value.T, merge]
    columns, rows = operands[1].shape
    return call(
        functools.partial(blocks_kernel, count),
        "weight_blocks",
        operands,
        (0,),
        range(1, len(operands)),
        [
            ((4 * columns // BLOCKS, rows), bf16),
            ((count - 1, 4 * columns // BLOCKS, rows), bf16),
        ],
        [pltpu.SemaphoreType.DMA((count,))],
        60,
    )


def attention_forward(kind, place, x, extra, gains, rel, weights):
    rows, width = x.shape
    extra_rows = extra.shape[0] if kind == "encoder" else 0
    keys = rows + extra_rows
    operands = [place, x]
    if extra is not None:
        operands.append(extra)
    operands.append(gains)
    if rel is not None:
        operands.append(rel)
    hbm = (len(operands),)
    operands.append(weights)
    return call(
        functools.partial(attention_forward_kernel, kind),
        kind + "_forward",
        operands,
        (0,),
        hbm,
        [
            ((rows, width), f32),
            ((rows, width), bf16),
            ((keys, width), bf16),
            ((4, rows, 192), bf16),
            ((4, keys, 384), bf16),
            ((4, rows, 192), bf16),
        ],
        [pltpu.VMEM((4, BLOCKS, width // BLOCKS, width), bf16), pltpu.SemaphoreType.DMA((4, 2))],
        56,
    )


def attention_backward(
    kind, place, ffn, upstream, x, gains, stored, source, weights, rel, bucket, buckets, grads
):
    rows, width = upstream.shape
    a, q, kv, o = stored
    keys = kv.shape[1]
    operands = [place]
    if ffn is not None:
        dc_own, dc_rest, r1 = ffn
        operands += [dc_own, *dc_rest, upstream, r1]
    else:
        operands += [upstream]
    operands += [x, gains, a]
    if source is not None:
        operands.append(source)
    operands += [q, kv, o]
    hbm = (len(operands),)
    operands.append(weights)
    if kind != "cross":
        operands += [rel, bucket]
    aliases = None
    if grads is not None:
        hbm += (len(operands), len(operands) + 1)
        aliases = {len(operands): 2, len(operands) + 1: 3}
        operands += grads
    block = width // BLOCKS
    outs = [
        ((rows, width), f32),
        ((1, width), f32),
    ]
    outs += [((2, 4, 2 if grads is None else 3, block, width), bf16)] * 2
    if ffn is not None:
        outs.append(((1, width), f32))
    if kind == "encoder":
        outs.append(((keys - rows, width), bf16))
    elif kind == "cross":
        outs.append(((rows, width), f32))
    if kind != "cross":
        outs.append(((rel.shape[0], buckets, 8, 2 * SEQ), f32))
    depth = 2 * rows + (keys if kind == "cross" else keys - rows)
    scratch = [
        pltpu.VMEM((4, BLOCKS, block, width), bf16),
        pltpu.SemaphoreType.DMA((4, 2)),
        pltpu.VMEM((width, depth), bf16),
        pltpu.VMEM((4, depth, width), bf16),
    ]
    if kind != "cross":
        scratch.append(pltpu.VMEM((rel.shape[0], SEQ, 2 * SEQ), f32))
    scratch += [pltpu.VMEM((4, BLOCKS, block, width), bf16), pltpu.SemaphoreType.DMA((4, 2))]
    return call(
        functools.partial(attention_backward_kernel, kind, ffn is not None),
        kind + "_backward",
        operands,
        (0,),
        hbm,
        outs,
        scratch,
        56,
        (2, 3),
        aliases,
    )


def ffn_first(name, c_parts, g_parts, widen, narrow):
    tokens, width = c_parts[0].shape
    hidden = widen.shape[1]
    every = 4 * tokens
    return call(
        ffn_first_kernel,
        name + "_first",
        [*c_parts, *g_parts, widen, narrow],
        (),
        (),
        [
            ((every, width), bf16),
            ((every, width), bf16),
            ((every, hidden), bf16),
            ((every, hidden), bf16),
            ((tokens, width), f32),
            ((3, tokens, width), bf16),
        ],
        [],
    )


def ffn_second(name, across, place, c_all, g_all, h, du, narrow):
    every, width = c_all.shape
    hidden = h.shape[1]
    tokens = every // 4
    block = width // BLOCKS
    if across:
        outs = [((every, width), bf16)]
    else:
        outs = [((tokens, width), f32)] + [((tokens, width), bf16)] * 3
    count = len(outs)
    return call(
        functools.partial(ffn_second_kernel, across),
        name + "_second",
        [place, c_all, g_all, h, du, narrow],
        (0,),
        (),
        outs + [((2, 4, 3, block, hidden), bf16)] * 2,
        [pltpu.VMEM((2, BLOCKS, block, hidden), bf16), pltpu.SemaphoreType.DMA((2, 2))],
        28,
        (count, count + 1),
    )


def gather_tokens(part):
    return [part] + [from_mp(part, step) for step in range(1, 4)]


def return_tokens(rest):
    return [to_mp(rest[step - 1], step) for step in range(1, 4)]


def relative_bias(bucket, table, heads_here):
    twice = jnp.concatenate([bucket, bucket], axis=1)
    onehot = (
        lax.broadcasted_iota(jnp.int32, (table.shape[0], 1), 0) == twice.reshape(1, -1)
    ).astype(f32)
    start = lax.axis_index("mp") * heads_here
    columns = jnp.concatenate([table.T, table.T], axis=0)
    ordered = lax.dynamic_slice_in_dim(columns, start, table.shape[1], 0)
    looked = jnp.dot(ordered, onehot, precision=lax.Precision.HIGHEST)
    return looked.reshape(table.shape[1], SEQ, 2 * SEQ), twice


def shards(
    encoder_input,
    encoder_upstream,
    memory_index,
    memory_table,
    encoder_bucket,
    encoder_bias,
    encoder_gain,
    encoder_query,
    encoder_key,
    encoder_value,
    encoder_merge,
    encoder_later_gain,
    encoder_widen,
    encoder_narrow,
    decoder_input,
    decoder_upstream,
    encoder_states,
    decoder_bucket,
    decoder_bias,
    decoder_gain,
    decoder_query,
    decoder_key,
    decoder_value,
    decoder_merge,
    cross_gain,
    cross_query,
    cross_key,
    cross_value,
    cross_merge,
    decoder_later_gain,
    decoder_widen,
    decoder_narrow,
):
    heads_here = encoder_query.shape[1] // DH
    width = encoder_input.shape[1]
    dp_at = lax.axis_index("dp")
    mp_at = lax.axis_index("mp")
    place = dp_at // (lax.axis_size("dp") // BLOCKS)
    place_in = jnp.stack([place, mp_at, dp_at * lax.axis_size("mp") + mp_at]).astype(jnp.int32)

    encoder_block, decoder_blocks = weight_blocks(
        place_in,
        [
            (encoder_query, encoder_key, encoder_value, encoder_merge),
            (decoder_query, decoder_key, decoder_value, decoder_merge),
            (cross_query, cross_key, cross_value, cross_merge),
        ],
    )
    encoder_slots = jnp.stack(gather_tokens(encoder_block))[:, None]
    encoder_weights = gather_blocks(encoder_slots)
    encoder_g = gather_tokens(after(encoder_upstream, encoder_slots))

    own_questions = memory_index.shape[0] // lax.axis_size("mp")
    entries = lax.dynamic_slice_in_dim(
        memory_index, mp_at * own_questions, own_questions, 0
    ).reshape(-1)
    prefix = jnp.take(memory_table, entries, axis=0).reshape(-1, width)
    prefix_rows = prefix.shape[0]
    prefix = jnp.pad(prefix, ((0, -prefix_rows % 64), (0, 0)))
    encoder_rel, encoder_twice = relative_bias(encoder_bucket, encoder_bias, heads_here)
    decoder_rel, decoder_twice = relative_bias(decoder_bucket, decoder_bias, heads_here)
    entry_rows = jnp.repeat(entries, PREFIX)
    numbers = jnp.stack([entry_rows // 32, entry_rows % 32], axis=1).astype(bf16)
    numbers = jnp.pad(numbers, ((0, 0), (0, 126)))
    gains = call(
        gains_kernel,
        "gains",
        [encoder_gain, encoder_later_gain, decoder_gain, cross_gain, decoder_later_gain],
        (),
        (),
        [((5, width), f32)],
        [],
    )[0]
    small = (prefix, encoder_rel, encoder_twice, decoder_rel, decoder_twice, numbers, gains)
    small = after(small, encoder_block)
    prefix, encoder_rel, encoder_twice, decoder_rel, decoder_twice, numbers, gains = small
    decoder_slots = jnp.stack(gather_tokens(after(decoder_blocks, encoder_g, small)))
    decoder_weights = gather_blocks(decoder_slots)


    encoder_r1, encoder_c, *encoder_stored = attention_forward(
        "encoder",
        after(place_in, encoder_g),
        encoder_input,
        prefix,
        gains,
        encoder_rel,
        encoder_weights,
    )
    encoder_c = gather_tokens(encoder_c)
    c_all, g_all, h, du, dc_own, dc_rest = ffn_first(
        "encoder_ffn", encoder_c, encoder_g, encoder_widen, encoder_narrow
    )
    encoder_dc = (dc_own, return_tokens(dc_rest))
    out, *grads = ffn_second(
        "encoder_ffn", True, place_in, c_all, g_all, h, du, encoder_narrow
    )
    encoder_out = lax.psum_scatter(out, "mp", scatter_dimension=0, tiled=True)
    decoder_g = gather_tokens(after(decoder_upstream, encoder_dc))
    (
        encoder_input_grad,
        encoder_gain_grad,
        keep,
        send,
        encoder_later_grad,
        prefix_grad,
        encoder_bias_raw,
    ) = attention_backward(
        "encoder",
        after(place_in, out),
        (*encoder_dc, encoder_r1),
        encoder_upstream,
        encoder_input,
        gains,
        encoder_stored,
        None,
        encoder_weights,
        encoder_rel,
        encoder_twice,
        encoder_bias.shape[0],
        grads,
    )
    encoder_got = swap_cores(after(send, decoder_g))
    packed = jnp.concatenate([prefix_grad[:prefix_rows], numbers], axis=1)
    used = lax.all_gather(packed, ("dp", "mp"), axis=0, tiled=True)
    encoder_halves = fold_cores(keep, encoder_got)
    encoder_once = send_once(encoder_halves)

    self_r1, _, *self_stored = attention_forward(
        "self", after(place_in, encoder_halves), decoder_input, None, gains, decoder_rel, decoder_weights
    )
    cross_r2, decoder_c, *cross_stored = attention_forward(
        "cross", place_in, self_r1, encoder_states, gains, None, decoder_weights
    )
    decoder_c = gather_tokens(decoder_c)
    c_all, g_all, h, du, dc_own, dc_rest = ffn_first(
        "decoder_ffn",
        [after(decoder_c[0], encoder_once, encoder_out), *decoder_c[1:]],
        decoder_g,
        decoder_widen,
        decoder_narrow,
    )
    decoder_dc = (dc_own, return_tokens(dc_rest))
    encoder_last = fold_once(after(encoder_halves, dc_own), encoder_once)
    encoder_twice_got = send_twice(encoder_last)
    out, *rest, keep, send = ffn_second(
        "decoder_ffn", False, place_in, c_all, g_all, h, du, decoder_narrow
    )
    grads = [keep, send]
    encoder_sums = fold_twice(
        after(encoder_halves, out), encoder_once, encoder_twice_got
    )
    encoder_sent = send_slots(after(encoder_sums, decoder_dc))

    cross_dx, cross_gain_grad, keep, send, decoder_later_grad, states_grad = attention_backward(
        "cross",
        after(place_in, encoder_sums),
        (*decoder_dc, cross_r2),
        decoder_upstream,
        self_r1,
        gains,
        cross_stored,
        encoder_states,
        decoder_weights,
        None,
        None,
        None,
        grads,
    )
    cross_got = swap_cores(after(send, encoder_sent))
    cross_halves = fold_cores(keep, cross_got)
    cross_once = send_once(cross_halves)
    decoder_out = [to_mp(part, i + 1) for i, part in enumerate(after(rest, cross_halves))]
    decoder_input_grad, decoder_gain_grad, keep, send, decoder_bias_raw = attention_backward(
        "self",
        after(place_in, cross_halves),
        None,
        cross_dx,
        decoder_input,
        gains,
        self_stored,
        None,
        decoder_weights,
        decoder_rel,
        decoder_twice,
        decoder_bias.shape[0],
        None,
    )
    self_got = swap_cores(after(send, cross_once, decoder_out))
    cross_last = fold_once(after(cross_halves, decoder_input_grad), cross_once)
    cross_twice_got = send_twice(cross_last)
    sums = call(
        pack_kernel,
        "pack",
        [
            after(place_in, cross_last),
            encoder_gain_grad,
            encoder_later_grad,
            decoder_gain_grad,
            cross_gain_grad,
            decoder_later_grad,
            encoder_bias_raw,
            decoder_bias_raw,
        ],
        (0,),
        (),
        [((64, 128), f32)],
        [],
    )[0]
    self_halves = fold_cores(keep, after(self_got, sums))
    self_once = send_once(self_halves)
    cross_sums = fold_twice(after(cross_halves, self_halves), cross_once, cross_twice_got)
    cross_sent = send_slots(cross_sums)
    self_last = fold_once(after(self_halves, cross_sent, used), self_once)
    self_twice_got = send_twice(self_last)
    sums = sum_over("dp", after(sums, self_halves))
    self_sums = fold_twice(after(self_halves, sums), self_once, self_twice_got)
    self_sent = send_slots(self_sums)
    sums = sum_over("mp", after(sums, self_sums))

    def last(value):
        return after(value, self_sums)

    cross_mats = four_matrices(last(cross_sums), cross_sent)
    encoder_mats = four_matrices(last(encoder_sums), encoder_sent)
    encoder_output = (last(encoder_r1) + encoder_out.astype(f32)).astype(bf16)
    encoder_widen_grad, encoder_narrow_grad = two_matrices(*last(encoder_sums[4:]))
    table_rows = memory_table.shape[0] // (lax.axis_size("dp") * lax.axis_size("mp"))
    table_grad = call(
        table_kernel,
        "table",
        [last(place_in), last(used)],
        (0,),
        (),
        [((table_rows, PREFIX, width), f32)],
        [],
    )[0]
    decoder_output = (
        last(cross_r2) + out + sum(part.astype(f32) for part in decoder_out)
    ).astype(bf16)
    decoder_widen_grad, decoder_narrow_grad = two_matrices(*last(cross_sums[4:]))
    self_mats = four_matrices(self_sums, self_sent)

    gain_sums = [sums[32 + 6 * i : 38 + 6 * i].reshape(-1) for i in range(5)]
    buckets, heads = encoder_bias.shape
    bias_grads = [sums[:buckets, i * heads : (i + 1) * heads] for i in range(2)]
    return (
        encoder_output,
        encoder_input_grad,
        table_grad,
        bias_grads[0],
        gain_sums[0],
        *encoder_mats,
        gain_sums[1],
        encoder_widen_grad,
        encoder_narrow_grad,
        decoder_output,
        decoder_input_grad,
        states_grad,
        bias_grads[1],
        gain_sums[2],
        *self_mats,
        gain_sums[3],
        *cross_mats,
        gain_sums[4],
        decoder_widen_grad,
        decoder_narrow_grad,
    )


def solution(mesh):
    rows = P(("dp", "mp"), None)
    columns = P(None, "mp")
    lines = P("mp", None)
    attention = (columns, columns, columns, lines)
    in_specs = (
        (rows, rows, P("dp", None), P(), P(), P(), P())
        + attention
        + (P(), columns, lines, rows, rows, rows, P(), P(), P())
        + attention
        + (P(),)
        + attention
        + (P(), columns, lines)
    )
    both = P("dp", "mp")
    turned = P("mp", "dp")
    grads = (both, both, both, turned)
    out_specs = (
        (rows, rows, P(("dp", "mp"), None, None), P(), P())
        + grads
        + (P(), both, turned, rows, rows, rows, P(), P())
        + grads
        + (P(),)
        + grads
        + (P(), both, turned)
    )
    return jax.shard_map(shards, mesh=mesh, in_specs=in_specs, out_specs=out_specs, check_vma=False)
```

```python
import functools

import jax
import jax.numpy as jnp
from jax import lax
from jax.experimental import pallas as pl
from jax.experimental.pallas import tpu as pltpu
from jax.sharding import PartitionSpec as P

DH = 64
SEQ = 64
MEMK = 10
PREFIX = 2
EPS = 1e-06
NEG = -1e30
BLOCKS = 8
bf16 = jnp.bfloat16
f32 = jnp.float32


def nn(left, right):
    return lax.dot_general(left, right, (((1,), (0,)), ((), ())), preferred_element_type=f32)


def nt(left, right):
    return lax.dot_general(left, right, (((1,), (1,)), ((), ())), preferred_element_type=f32)


def tn(left, right):
    return lax.dot_general(left, right, (((0,), (0,)), ((), ())), preferred_element_type=f32)


def from_mp(array, step):
    size = lax.axis_size("mp")
    return lax.ppermute(array, "mp", [(i, (i - step) % size) for i in range(size)])


def to_mp(array, step):
    size = lax.axis_size("mp")
    return lax.ppermute(array, "mp", [(i, (i + step) % size) for i in range(size)])


def swap_dp(array, bit):
    return lax.ppermute(array, "dp", [(i, i ^ bit) for i in range(lax.axis_size("dp"))])


def after(value, *earlier):
    leaves, shape = jax.tree.flatten(value)
    tied = lax.optimization_barrier((*leaves, *jax.tree.leaves(earlier)))
    return jax.tree.unflatten(shape, tied[: len(leaves)])


def high_bits():
    low = lax.axis_size("dp") // BLOCKS
    return low, 2 * low, 4 * low


def rounded_sum(left, right):
    return (left.astype(f32) + right.astype(f32)).astype(bf16)


def swap_cores(array):
    return swap_dp(array, high_bits()[0])


def fold_cores(keep, got):
    return tuple(
        (rounded_sum(keep[i, :2], got[i, :2]), rounded_sum(keep[i, 2:], got[i, 2:])) for i in range(2)
    )


def send_once(halves):
    core, along, across = high_bits()
    return swap_dp(halves[0][1], along), swap_dp(halves[1][1], across)


def fold_once(halves, got):
    return tuple(rounded_sum(halves[i][0][1], got[i][1]) for i in range(2))


def send_twice(last):
    core, along, across = high_bits()
    return swap_dp(last[0], across), swap_dp(last[1], along)


def fold_twice(halves, got, last_got):
    sums = [
        halves[i][0][0].astype(f32) + got[i][0].astype(f32) + last_got[i].astype(f32) for i in range(2)
    ]
    return [sums[0][0], sums[0][1], sums[1][0], sums[1][1]] + [part[i] for i in range(2, sums[0].shape[0]) for part in sums]


def send_slots(slots):
    return [to_mp(slots[step].astype(bf16), step) for step in range(1, 4)]


def scatter_rest(rows):
    size = lax.axis_size("dp")
    low = size // BLOCKS
    if low == 1:
        return rows
    groups = [[high * low + i for i in range(low)] for high in range(BLOCKS)]
    return lax.psum_scatter(
        rows, "dp", scatter_dimension=0, axis_index_groups=groups, tiled=True
    )


def four_matrices(slots, got):
    total = slots[0]
    if lax.axis_size("dp") == BLOCKS:
        rows, width = total.shape
        part = width // 4
        return call(
            finish_kernel,
            "matrices",
            [total, *got],
            (),
            (),
            [((rows, part), f32)] * 3 + [((part, rows), f32)],
            [],
        )
    for other in got:
        total = total + other.astype(f32)
    total = scatter_rest(total)
    width = total.shape[1] // 4
    parts = [total[:, i * width : (i + 1) * width] for i in range(4)]
    return parts[0], parts[1], parts[2], parts[3].T


def two_matrices(widen, narrow):
    return scatter_rest(widen), scatter_rest(narrow).T


def gather_blocks(slots):
    low = lax.axis_size("dp") // BLOCKS
    groups = [[high * low + i for high in range(BLOCKS)] for i in range(low)]
    if low == 1:
        groups = None
    return lax.all_gather(slots, "dp", axis=0, axis_index_groups=groups, tiled=False)


def sum_bits(axis, array, bit, end):
    size = lax.axis_size(axis)
    while bit < end:
        array = array + lax.ppermute(array, axis, [(i, i ^ bit) for i in range(size)])
        bit *= 2
    return array


def fetch_weights(weights, group, held, sems, order):
    copies = {}
    for i, what in enumerate(order):
        blocks = pl.ds(6, 2) if what == "merge" else pl.ds(0, 6)
        for slot in range(4):
            copies[what, slot] = pltpu.make_async_copy(
                weights.at[blocks, slot, group], held.at[slot, blocks], sems.at[slot, i]
            )
            copies[what, slot].start()
    return copies


def slot_rows(held, slot, first, last):
    part = held[slot, 2 * first : 2 * last]
    return part.reshape(part.shape[0] * part.shape[1], part.shape[2])


def wait_all(copies):
    for copy in copies:
        copy.wait()


def blocks_kernel(groups, place_ref, *refs):
    inputs = refs[: 4 * groups]
    first, others, sems = refs[4 * groups :]
    outs = [first] + [others.at[i] for i in range(groups - 1)]
    size = first.shape[0]
    place = place_ref[0]
    start = pl.multiple_of((place % 2) * size, size)
    for j in range(4):

        @pl.when(place // 2 == j)
        def _():
            copies = [
                pltpu.make_async_copy(inputs[4 * i + j].at[pl.ds(start, size)], outs[i], sems.at[i])
                for i in range(groups)
            ]
            for copy in copies:
                copy.start()
            wait_all(copies)


def inverse_rms(rows):
    return lax.rsqrt(jnp.mean(rows * rows, axis=-1, keepdims=True) + EPS)


def gain_rows(kind, gains_ref):
    at = {"encoder": (0, 1), "self": (2, 3), "cross": (3, 4)}[kind]
    return tuple(gains_ref[i : i + 1, :] for i in at)


def column_head(shape):
    return lax.broadcasted_iota(jnp.int32, shape, 1) // DH


def softmax_rows(scores):
    shifted = jnp.exp(scores - jnp.max(scores, axis=-1, keepdims=True))
    return shifted / jnp.sum(shifted, axis=-1, keepdims=True)


def masks(kind, rows, keys):
    row = lax.broadcasted_iota(jnp.int32, (rows, rows), 0)
    col = lax.broadcasted_iota(jnp.int32, (rows, rows), 1)
    same = row // SEQ == col // SEQ
    if kind == "self":
        same = jnp.logical_and(same, col <= row)
    if kind != "encoder":
        return same, None
    row = lax.broadcasted_iota(jnp.int32, (rows, keys - rows), 0)
    col = lax.broadcasted_iota(jnp.int32, (rows, keys - rows), 1)
    first = (row // SEQ) * (MEMK * PREFIX)
    valid = jnp.logical_and(col >= first, col < first + MEMK * PREFIX)
    return same, jnp.where(valid, 0.0, NEG)


def add_bias(kind, scores, rel_ref, slot, same, before):
    rows = scores.shape[0] // 3
    parts = []
    for j in range(3):
        part = scores[j * rows : (j + 1) * rows]
        own = part[:, :rows]
        if kind != "cross":
            rel = rel_ref[3 * slot + j]
            own = own + jnp.concatenate([rel] * (rows // SEQ), axis=0)
        own = jnp.where(same, own, NEG)
        if before is not None:
            own = jnp.concatenate([own, part[:, rows:] + before], axis=1)
        parts.append(own)
    return jnp.concatenate(parts, axis=0)


def stack_heads(array):
    head = column_head(array.shape)
    return jnp.concatenate([jnp.where(head == j, array, jnp.zeros_like(array)) for j in range(3)], axis=0)


def join_heads(stacked):
    rows = stacked.shape[0] // 3
    head = column_head((rows, stacked.shape[1]))
    return jnp.where(
        head == 0,
        stacked[:rows],
        jnp.where(head == 1, stacked[rows : 2 * rows], stacked[2 * rows :]),
    )


def attention_forward_kernel(kind, *refs):
    refs = list(refs)
    place_ref, x_ref = refs[:2]
    del refs[:2]
    pre_ref = refs.pop(0) if kind != "self" else None
    gains_ref = refs.pop(0)
    gain, later = gain_rows(kind, gains_ref)
    rel_ref = refs.pop(0) if kind != "cross" else None
    weights, r1_ref, next_ref, a_ref, q_ref, kv_ref, o_ref, held, sems = refs
    copies = fetch_weights(weights, int(kind == "cross"), held, sems, ("rest", "merge"))
    r = x_ref[...].astype(f32)
    rows = r.shape[0]
    a = (r * inverse_rms(r) * gain).astype(bf16)
    if kind == "encoder":
        a_ref[0:rows, :] = a
        a_ref[rows:, :] = pre_ref[...]
        a_all = a_ref[...]
    else:
        a_ref[...] = a
        a_all = a
    keys = kv_ref.shape[1]
    same, before = masks(kind, rows, keys)
    queries = []
    sources = []
    for slot in range(4):
        copies["rest", slot].wait()
        if kind == "cross":
            q = nt(a, slot_rows(held, slot, 0, 1)).astype(bf16)
            kv = nt(pre_ref[...], slot_rows(held, slot, 1, 3)).astype(bf16)
        else:
            qkv = nt(a_all, slot_rows(held, slot, 0, 3)).astype(bf16)
            q = qkv[:rows, :192]
            kv = qkv[:, 192:]
        q_ref[slot] = q
        kv_ref[slot] = kv
        queries.append(q)
        sources.append(kv)
    chances = []
    for slot in range(4):
        scores = nt(stack_heads(queries[slot]), sources[slot][:, :192])
        chances.append(softmax_rows(add_bias(kind, scores, rel_ref, slot, same, before)).astype(bf16))
    mixed = []
    for slot in range(4):
        o = join_heads(nn(chances[slot], sources[slot][:, 192:])).astype(bf16)
        o_ref[slot] = o
        mixed.append(o)
    acc = r
    for slot in range(4):
        copies["merge", slot].wait()
        acc = acc + nn(mixed[slot], slot_rows(held, slot, 3, 4))
    r1_ref[...] = acc
    next_ref[...] = (acc * inverse_rms(acc) * later).astype(bf16)


def norm_back(dn, r, gain, dgain_ref):
    t = inverse_rms(r)
    dgain_ref[...] = jnp.sum(dn * r * t, axis=0, keepdims=True)
    scaled = dn * gain
    return t * (scaled - r * (t * t) * jnp.mean(scaled * r, axis=-1, keepdims=True))


def attention_backward_kernel(kind, after_ffn, *refs):
    refs = list(refs)
    place_ref = refs.pop(0)
    place = place_ref[0]
    if after_ffn:
        dc_own, *dc_rest = refs[:4]
        up_ref, r1_ref = refs[4:6]
        refs = refs[6:]
    else:
        up_ref = refs.pop(0)
    x_ref, gains_ref, a_ref = refs[:3]
    gain, later = gain_rows(kind, gains_ref)
    refs = refs[3:]
    source_ref = refs.pop(0) if kind == "cross" else None
    q_ref, kv_ref, o_ref = refs[:3]
    weights = refs[3]
    refs = refs[4:]
    rel_ref, bucket_ref = (refs.pop(0), refs.pop(0)) if kind != "cross" else (None, None)
    if kind != "self":
        refs = refs[2:]
    dx_ref, dgain_ref = refs[:2]
    refs = refs[2:]
    keep_ref, send_ref = refs.pop(0), refs.pop(0)
    later_grad = refs.pop(0) if after_ffn else None
    if kind == "encoder":
        dpre_ref = refs.pop(0)
    elif kind == "cross":
        dsource_ref = refs.pop(0)
    bias_grad = refs.pop(0) if kind != "cross" else None
    held, sems, left, right = refs[:4]
    refs = refs[4:]
    ds_sum = refs.pop(0) if kind != "cross" else None
    stage, out_sems = refs
    copies = fetch_weights(weights, int(kind == "cross"), held, sems, ("merge", "rest"))

    d_out = up_ref[...].astype(f32)
    if after_ffn:
        dn = dc_own[...]
        for part in dc_rest:
            dn = dn + part[...].astype(f32)
        d_out = d_out + norm_back(dn, r1_ref[...], later, later_grad)
    g = d_out.astype(bf16)
    rows, width = g.shape
    keys = kv_ref.shape[1]
    stacked = [a_ref[...]] + ([source_ref[...]] if kind == "cross" else []) + [g]
    turned = jnp.concatenate(stacked, axis=0).T
    size = width // BLOCKS
    for d in range(BLOCKS):
        away = place ^ d
        at = pl.multiple_of(((away % 2) * 4 + away // 2) * size, size)
        left[pl.ds(at, size), :] = turned[d * size : (d + 1) * size]
    source_at = rows if kind == "cross" else 0
    g_at = left.shape[1] - rows
    right[...] = jnp.zeros(right.shape, bf16)
    same, before = masks(kind, rows, keys)
    grads = []
    for slot in range(4):
        copies["merge", slot].wait()
        grads.append(nt(g, slot_rows(held, slot, 3, 4)).astype(bf16))
        right[slot, g_at:, 576:768] = o_ref[slot]
    chances = []
    for slot in range(4):
        scores = nt(stack_heads(q_ref[slot]), kv_ref[slot][:, :192])
        chances.append(softmax_rows(add_bias(kind, scores, rel_ref, slot, same, before)))
    d_scores = []
    for slot in range(4):
        p = chances[slot]
        do_heads = stack_heads(grads[slot])
        dv = tn(p.astype(bf16), do_heads).astype(bf16)
        right[slot, source_at : source_at + keys, 384:576] = dv
        dp = nt(do_heads, kv_ref[slot][:, 192:])
        ds = (p * (dp - jnp.sum(dp * p, axis=-1, keepdims=True))).astype(bf16)
        d_scores.append(ds)
    for slot in range(4):
        ds = d_scores[slot]
        right[slot, 0:rows, 0:192] = join_heads(nn(ds, kv_ref[slot][:, :192])).astype(bf16)
        right[slot, source_at : source_at + keys, 192:384] = tn(ds, stack_heads(q_ref[slot])).astype(bf16)
        if kind != "cross":
            for j in range(3):
                wide = ds[j * rows : (j + 1) * rows, :rows].astype(f32)
                ds_sum[3 * slot + j] = wide[:SEQ] + wide[SEQ:]
    outgoing = []
    for slot in range(4):
        grad = nn(left[...], right[slot]).astype(bf16)
        for j in range(BLOCKS):
            to = (j // 4) * 4 + ((j % 2) * 2 + (j % 4) // 2 if slot // 2 == 0 else j % 4)
            stage[slot, to] = grad[j * size : (j + 1) * size]
        for i, out in enumerate((keep_ref, send_ref)):
            copy = pltpu.make_async_copy(
                stage.at[slot, pl.ds(4 * i, 4)], out.at[slot // 2, :, slot % 2], out_sems.at[slot, i]
            )
            copy.start()
            outgoing.append(copy)
    total = None
    source_total = None
    for slot in range(4):
        copies["rest", slot].wait()
        if kind == "cross":
            part = nn(right[slot, 0:rows, 0:192], slot_rows(held, slot, 0, 1))
            other = nn(right[slot, rows : rows + keys, 192:576], slot_rows(held, slot, 1, 3))
            source_total = other if slot == 0 else source_total + other
        else:
            part = nn(right[slot, 0:keys, 0:576], slot_rows(held, slot, 0, 3))
        total = part if slot == 0 else total + part
    if kind == "cross":
        dsource_ref[...] = source_total
    if kind == "encoder":
        dpre_ref[...] = total[rows:].astype(bf16)
    dx_ref[...] = d_out + norm_back(total[:rows], x_ref[...].astype(f32), gain, dgain_ref)
    if kind != "cross":
        bucket = bucket_ref[...]
        heads, buckets = bias_grad.shape[:2]

        @pl.loop(0, buckets)
        def _(b):
            chosen = bucket == b
            for head in range(heads):
                part = jnp.where(chosen, ds_sum[head], 0.0)
                bias_grad[head, b] = jnp.sum(part.reshape(SEQ // 8, 8, 2 * SEQ), axis=0)

    wait_all(outgoing)


def ffn_first_kernel(c0, c1, c2, c3, g0, g1, g2, g3, widen, narrow, c_all, g_all, h_ref, du_ref, dc_own, dc_rest):
    tokens = c0.shape[0]
    for i, (c, g) in enumerate(((c0, g0), (c1, g1), (c2, g2), (c3, g3))):
        c_all[i * tokens : (i + 1) * tokens, :] = c[...]
        g_all[i * tokens : (i + 1) * tokens, :] = g[...]
    inner = 0.7978845608028654
    for n in range(widen.shape[1] // 256):
        at = slice(n * 256, (n + 1) * 256)
        u = nn(c_all[...], widen[:, at])
        u2 = u * u
        th = jnp.tanh(inner * (u + 0.044715 * u * u2))
        h_ref[:, at] = (0.5 * u * (1.0 + th)).astype(bf16)
        slope = 0.5 * (1.0 + th) + (0.5 * inner) * u * (1.0 - th * th) * (1.0 + 3 * 0.044715 * u2)
        dh = nt(g_all[...], narrow[at, :])
        du_ref[:, at] = (dh * slope).astype(bf16)
    for n in range(widen.shape[0] // 256):
        at = slice(n * 256, (n + 1) * 256)
        dc = nt(du_ref[...], widen[at, :])
        dc_own[:, at] = dc[:tokens]
        for i in range(3):
            dc_rest[i, :, at] = dc[(i + 1) * tokens : (i + 2) * tokens].astype(bf16)


def ffn_second_kernel(across, place_ref, c_all, g_all, h_ref, du_ref, narrow, *refs):
    outs = refs[:-4]
    keep_ref, send_ref, stage, sems = refs[-4:]
    tokens = c_all.shape[0] // 4
    if not across:
        packed, *outs = outs
        for out in outs[1:]:
            out[tokens:, :] = packed[...]
    place = place_ref[0]
    copies = []
    for half, (left, right) in enumerate(((c_all, du_ref), (g_all, h_ref))):
        grad = tn(left[...], right[...]).astype(bf16)
        size = grad.shape[0] // BLOCKS
        for d in range(BLOCKS):
            away = place ^ d
            where = away // 2
            if half == 0:
                where = (where % 2) * 2 + where // 2
            stage[half, (away % 2) * 4 + where] = grad[d * size : (d + 1) * size]
        for i, ref in enumerate((keep_ref, send_ref)):
            copy = pltpu.make_async_copy(
                stage.at[half, pl.ds(4 * i, 4)], ref.at[half, :, 2], sems.at[half, i]
            )
            copy.start()
            copies.append(copy)
    for n in range(narrow.shape[1] // 256):
        at = slice(n * 256, (n + 1) * 256)
        out = nn(h_ref[...], narrow[:, at])
        for i in range(4):
            part = out[i * tokens : (i + 1) * tokens]
            if across:
                row = pl.multiple_of((place_ref[1] + i) % 4 * tokens, tokens)
                outs[0][pl.ds(row, tokens), at] = part.astype(bf16)
            else:
                outs[i][0:tokens, at] = part.astype(outs[i].dtype)
    wait_all(copies)


def gains_kernel(*refs):
    for i in range(5):
        refs[5][i : i + 1, :] = refs[i][...].reshape(1, -1)


def finish_kernel(total_ref, got1, got2, got3, query, key, value, merge):
    total = total_ref[...]
    for got in (got1, got2, got3):
        total = total + got[...].astype(f32)
    width = query.shape[1]
    for i, out in enumerate((query, key, value)):
        out[...] = total[:, i * width : (i + 1) * width]
    merge[...] = total[:, 3 * width :].T


def table_kernel(rows, place_ref, used_ref, out_ref):
    entries = out_ref.shape[0]
    size = used_ref.shape[1]
    first = (place_ref[2] * entries).astype(f32)
    row = lax.broadcasted_iota(jnp.int32, (PREFIX * entries, size), 0)
    column = lax.broadcasted_iota(jnp.int32, (PREFIX * entries, size), 1)
    wanted = (row % entries).astype(f32) + first
    fits = jnp.logical_and(column % PREFIX == row // entries, column < rows)
    total = jnp.zeros((PREFIX * entries, used_ref.shape[2]), f32)
    for i in range(used_ref.shape[0]):
        number = used_ref[i, :, 0:128].astype(f32)
        entry = number[rows : rows + 1, :size] * 32.0 + number[rows + 1 : rows + 2, :size]
        chosen = jnp.logical_and(entry == wanted, fits)
        total = total + nn(jnp.where(chosen, 1.0, 0.0).astype(bf16), used_ref[i])
    for p in range(PREFIX):
        out_ref[:, p, :] = total[p * entries : (p + 1) * entries]


def pack_kernel(place_ref, *refs):
    out = refs[7]
    out[...] = jnp.zeros(out.shape, f32)
    for i in range(2):
        raw = refs[5 + i]
        heads, buckets = raw.shape[:2]
        sums = jnp.sum(jnp.sum(raw[...], axis=2), axis=-1)
        here = lax.broadcasted_iota(jnp.int32, (heads, 128), 0)
        column = lax.broadcasted_iota(jnp.int32, (heads, 128), 1)
        target = (here + place_ref[1] * (heads // 4)) % heads + i * heads
        turn = jnp.where(column == target, 1.0, 0.0)
        out[0:buckets, :] += lax.dot_general(
            sums,
            turn,
            (((0,), (0,)), ((), ())),
            precision=lax.Precision.HIGHEST,
            preferred_element_type=f32,
        )
    for i in range(5):
        for j in range(6):
            out[32 + 6 * i + j : 33 + 6 * i + j, :] = refs[i][:, 128 * j : 128 * (j + 1)]


def call(kernel, name, operands, smem, hbm, outs, scratch, limit=28, hbm_outs=(), aliases=None):
    specs = []
    for i in range(len(operands)):
        if i in smem:
            specs.append(pl.BlockSpec(memory_space=pltpu.SMEM))
        elif i in hbm:
            specs.append(pl.BlockSpec(memory_space=pl.ANY))
        else:
            specs.append(pl.BlockSpec(memory_space=pltpu.VMEM))
    return pl.pallas_call(
        kernel,
        out_shape=[jax.ShapeDtypeStruct(shape, kind) for shape, kind in outs],
        in_specs=specs,
        out_specs=[
            pl.BlockSpec(memory_space=pl.ANY if i in hbm_outs else pltpu.VMEM)
            for i in range(len(outs))
        ],
        scratch_shapes=scratch,
        input_output_aliases=aliases or {},
        compiler_params=pltpu.CompilerParams(vmem_limit_bytes=limit * 1024 * 1024),
        cost_estimate=pl.CostEstimate(flops=0, bytes_accessed=1024, transcendentals=0),
        name=name,
    )(*operands)


def weight_blocks(place, groups):
    count = len(groups)
    operands = [place]
    for query, key, value, merge in groups:
        operands += [query.T, key.T, value.T, merge]
    columns, rows = operands[1].shape
    return call(
        functools.partial(blocks_kernel, count),
        "weight_blocks",
        operands,
        (0,),
        range(1, len(operands)),
        [
            ((4 * columns // BLOCKS, rows), bf16),
            ((count - 1, 4 * columns // BLOCKS, rows), bf16),
        ],
        [pltpu.SemaphoreType.DMA((count,))],
        60,
    )


def attention_forward(kind, place, x, extra, gains, rel, weights):
    rows, width = x.shape
    extra_rows = extra.shape[0] if kind == "encoder" else 0
    keys = rows + extra_rows
    operands = [place, x]
    if extra is not None:
        operands.append(extra)
    operands.append(gains)
    if rel is not None:
        operands.append(rel)
    hbm = (len(operands),)
    operands.append(weights)
    return call(
        functools.partial(attention_forward_kernel, kind),
        kind + "_forward",
        operands,
        (0,),
        hbm,
        [
            ((rows, width), f32),
            ((rows, width), bf16),
            ((keys, width), bf16),
            ((4, rows, 192), bf16),
            ((4, keys, 384), bf16),
            ((4, rows, 192), bf16),
        ],
        [pltpu.VMEM((4, BLOCKS, width // BLOCKS, width), bf16), pltpu.SemaphoreType.DMA((4, 2))],
        56,
    )


def attention_backward(
    kind, place, ffn, upstream, x, gains, stored, source, weights, rel, bucket, buckets, grads
):
    rows, width = upstream.shape
    a, q, kv, o = stored
    keys = kv.shape[1]
    operands = [place]
    if ffn is not None:
        dc_own, dc_rest, r1 = ffn
        operands += [dc_own, *dc_rest, upstream, r1]
    else:
        operands += [upstream]
    operands += [x, gains, a]
    if source is not None:
        operands.append(source)
    operands += [q, kv, o]
    hbm = (len(operands),)
    operands.append(weights)
    if kind != "cross":
        operands += [rel, bucket]
    aliases = None
    if grads is not None:
        hbm += (len(operands), len(operands) + 1)
        aliases = {len(operands): 2, len(operands) + 1: 3}
        operands += grads
    block = width // BLOCKS
    outs = [
        ((rows, width), f32),
        ((1, width), f32),
    ]
    outs += [((2, 4, 2 if grads is None else 3, block, width), bf16)] * 2
    if ffn is not None:
        outs.append(((1, width), f32))
    if kind == "encoder":
        outs.append(((keys - rows, width), bf16))
    elif kind == "cross":
        outs.append(((rows, width), f32))
    if kind != "cross":
        outs.append(((rel.shape[0], buckets, 8, 2 * SEQ), f32))
    depth = 2 * rows + (keys if kind == "cross" else keys - rows)
    scratch = [
        pltpu.VMEM((4, BLOCKS, block, width), bf16),
        pltpu.SemaphoreType.DMA((4, 2)),
        pltpu.VMEM((width, depth), bf16),
        pltpu.VMEM((4, depth, width), bf16),
    ]
    if kind != "cross":
        scratch.append(pltpu.VMEM((rel.shape[0], SEQ, 2 * SEQ), f32))
    scratch += [pltpu.VMEM((4, BLOCKS, block, width), bf16), pltpu.SemaphoreType.DMA((4, 2))]
    return call(
        functools.partial(attention_backward_kernel, kind, ffn is not None),
        kind + "_backward",
        operands,
        (0,),
        hbm,
        outs,
        scratch,
        56,
        (2, 3),
        aliases,
    )


def ffn_first(name, c_parts, g_parts, widen, narrow):
    tokens, width = c_parts[0].shape
    hidden = widen.shape[1]
    every = 4 * tokens
    return call(
        ffn_first_kernel,
        name + "_first",
        [*c_parts, *g_parts, widen, narrow],
        (),
        (),
        [
            ((every, width), bf16),
            ((every, width), bf16),
            ((every, hidden), bf16),
            ((every, hidden), bf16),
            ((tokens, width), f32),
            ((3, tokens, width), bf16),
        ],
        [],
    )


def ffn_second(name, packed, place, c_all, g_all, h, du, narrow):
    every, width = c_all.shape
    hidden = h.shape[1]
    tokens = every // 4
    block = width // BLOCKS
    across = packed is None
    operands = [place, c_all, g_all, h, du, narrow]
    if across:
        outs = [((every, width), bf16)]
    else:
        operands.append(packed)
        outs = [((tokens, width), f32)] + [((tokens + packed.shape[0], width), bf16)] * 3
    count = len(outs)
    return call(
        functools.partial(ffn_second_kernel, across),
        name + "_second",
        operands,
        (0,),
        (),
        outs + [((2, 4, 3, block, hidden), bf16)] * 2,
        [pltpu.VMEM((2, BLOCKS, block, hidden), bf16), pltpu.SemaphoreType.DMA((2, 2))],
        28,
        (count, count + 1),
    )


def gather_tokens(part):
    return [part] + [from_mp(part, step) for step in range(1, 4)]


def return_tokens(rest):
    return [to_mp(rest[step - 1], step) for step in range(1, 4)]


def relative_bias(bucket, table, heads_here):
    twice = jnp.concatenate([bucket, bucket], axis=1)
    onehot = (
        lax.broadcasted_iota(jnp.int32, (table.shape[0], 1), 0) == twice.reshape(1, -1)
    ).astype(f32)
    start = lax.axis_index("mp") * heads_here
    columns = jnp.concatenate([table.T, table.T], axis=0)
    ordered = lax.dynamic_slice_in_dim(columns, start, table.shape[1], 0)
    looked = jnp.dot(ordered, onehot, precision=lax.Precision.HIGHEST)
    return looked.reshape(table.shape[1], SEQ, 2 * SEQ), twice


def shards(
    encoder_input,
    encoder_upstream,
    memory_index,
    memory_table,
    encoder_bucket,
    encoder_bias,
    encoder_gain,
    encoder_query,
    encoder_key,
    encoder_value,
    encoder_merge,
    encoder_later_gain,
    encoder_widen,
    encoder_narrow,
    decoder_input,
    decoder_upstream,
    encoder_states,
    decoder_bucket,
    decoder_bias,
    decoder_gain,
    decoder_query,
    decoder_key,
    decoder_value,
    decoder_merge,
    cross_gain,
    cross_query,
    cross_key,
    cross_value,
    cross_merge,
    decoder_later_gain,
    decoder_widen,
    decoder_narrow,
):
    heads_here = encoder_query.shape[1] // DH
    width = encoder_input.shape[1]
    dp_at = lax.axis_index("dp")
    mp_at = lax.axis_index("mp")
    place = dp_at // (lax.axis_size("dp") // BLOCKS)
    place_in = jnp.stack([place, mp_at, dp_at * lax.axis_size("mp") + mp_at]).astype(jnp.int32)

    encoder_block, decoder_blocks = weight_blocks(
        place_in,
        [
            (encoder_query, encoder_key, encoder_value, encoder_merge),
            (decoder_query, decoder_key, decoder_value, decoder_merge),
            (cross_query, cross_key, cross_value, cross_merge),
        ],
    )
    encoder_slots = jnp.stack(gather_tokens(encoder_block))[:, None]
    encoder_weights = gather_blocks(encoder_slots)
    encoder_g = gather_tokens(after(encoder_upstream, encoder_slots))

    own_questions = memory_index.shape[0] // lax.axis_size("mp")
    entries = lax.dynamic_slice_in_dim(
        memory_index, mp_at * own_questions, own_questions, 0
    ).reshape(-1)
    prefix = jnp.take(memory_table, entries, axis=0).reshape(-1, width)
    prefix_rows = prefix.shape[0]
    prefix = jnp.pad(prefix, ((0, -prefix_rows % 64), (0, 0)))
    encoder_rel, encoder_twice = relative_bias(encoder_bucket, encoder_bias, heads_here)
    decoder_rel, decoder_twice = relative_bias(decoder_bucket, decoder_bias, heads_here)
    entry_rows = jnp.repeat(entries, PREFIX)
    numbers = jnp.stack([entry_rows // 32, entry_rows % 32]).astype(bf16)
    numbers = jnp.pad(numbers, ((0, -(prefix_rows + 2) % 16), (0, width - prefix_rows)))
    gains = call(
        gains_kernel,
        "gains",
        [encoder_gain, encoder_later_gain, decoder_gain, cross_gain, decoder_later_gain],
        (),
        (),
        [((5, width), f32)],
        [],
    )[0]
    small = (prefix, encoder_rel, encoder_twice, decoder_rel, decoder_twice, numbers, gains)
    small = after(small, encoder_block)
    prefix, encoder_rel, encoder_twice, decoder_rel, decoder_twice, numbers, gains = small
    decoder_slots = jnp.stack(gather_tokens(after(decoder_blocks, encoder_g, small)))
    decoder_weights = gather_blocks(decoder_slots)


    encoder_r1, encoder_c, *encoder_stored = attention_forward(
        "encoder",
        after(place_in, encoder_g),
        encoder_input,
        prefix,
        gains,
        encoder_rel,
        encoder_weights,
    )
    encoder_c = gather_tokens(encoder_c)
    c_all, g_all, h, du, dc_own, dc_rest = ffn_first(
        "encoder_ffn", encoder_c, encoder_g, encoder_widen, encoder_narrow
    )
    encoder_dc = (dc_own, return_tokens(dc_rest))
    out, *grads = ffn_second(
        "encoder_ffn", None, after(place_in, encoder_dc[1][0]), c_all, g_all, h, du, encoder_narrow
    )
    encoder_out = lax.psum_scatter(out, "mp", scatter_dimension=0, tiled=True)
    decoder_g = gather_tokens(after(decoder_upstream, encoder_dc))
    (
        encoder_input_grad,
        encoder_gain_grad,
        keep,
        send,
        encoder_later_grad,
        prefix_grad,
        encoder_bias_raw,
    ) = attention_backward(
        "encoder",
        after(place_in, out),
        (*encoder_dc, encoder_r1),
        encoder_upstream,
        encoder_input,
        gains,
        encoder_stored,
        None,
        encoder_weights,
        encoder_rel,
        encoder_twice,
        encoder_bias.shape[0],
        grads,
    )
    encoder_got = swap_cores(after(send, decoder_g))
    packed = jnp.concatenate([prefix_grad[:prefix_rows], numbers])

    self_r1, _, *self_stored = attention_forward(
        "self", after(place_in, encoder_input_grad), decoder_input, None, gains, decoder_rel, decoder_weights
    )
    encoder_halves = fold_cores(after(keep, self_r1), encoder_got)
    encoder_once = send_once(encoder_halves)
    cross_r2, decoder_c, *cross_stored = attention_forward(
        "cross", after(place_in, encoder_halves), self_r1, encoder_states, gains, None, decoder_weights
    )
    decoder_c = gather_tokens(decoder_c)
    c_all, g_all, h, du, dc_own, dc_rest = ffn_first(
        "decoder_ffn",
        [after(decoder_c[0], encoder_out), *decoder_c[1:]],
        decoder_g,
        decoder_widen,
        decoder_narrow,
    )
    decoder_dc = (dc_own, return_tokens(dc_rest))
    encoder_last = fold_once(after(encoder_halves, decoder_dc[1][0]), encoder_once)
    encoder_twice_got = send_twice(encoder_last)
    out, *rest, keep, send = ffn_second(
        "decoder_ffn", packed, after(place_in, encoder_last), c_all, g_all, h, du, decoder_narrow
    )
    grads = [keep, send]

    encoder_sums = fold_twice(
        after(encoder_halves, out), encoder_once, encoder_twice_got
    )
    encoder_sent = send_slots(after(encoder_sums, decoder_dc))

    cross_dx, cross_gain_grad, keep, send, decoder_later_grad, states_grad = attention_backward(
        "cross",
        after(place_in, encoder_sums),
        (*decoder_dc, cross_r2),
        decoder_upstream,
        self_r1,
        gains,
        cross_stored,
        encoder_states,
        decoder_weights,
        None,
        None,
        None,
        grads,
    )
    cross_got = swap_cores(after(send, encoder_sent))
    cross_halves = fold_cores(keep, cross_got)
    cross_once = send_once(cross_halves)
    decoder_out = [to_mp(part, i + 1) for i, part in enumerate(after(rest, cross_halves))]
    tokens = cross_r2.shape[0]
    used = jnp.stack([packed] + [part[tokens:] for part in decoder_out])
    used = lax.all_gather(used, "dp", axis=0, tiled=False).reshape(-1, *packed.shape)
    decoder_input_grad, decoder_gain_grad, keep, send, decoder_bias_raw = attention_backward(
        "self",
        after(place_in, cross_halves),
        None,
        cross_dx,
        decoder_input,
        gains,
        self_stored,
        None,
        decoder_weights,
        decoder_rel,
        decoder_twice,
        decoder_bias.shape[0],
        None,
    )
    self_got = swap_cores(after(send, cross_once, decoder_out))
    cross_last = fold_once(after(cross_halves, decoder_input_grad), cross_once)
    cross_twice_got = send_twice(cross_last)
    sums = call(
        pack_kernel,
        "pack",
        [
            place_in,
            encoder_gain_grad,
            encoder_later_grad,
            decoder_gain_grad,
            cross_gain_grad,
            decoder_later_grad,
            encoder_bias_raw,
            decoder_bias_raw,
        ],
        (0,),
        (),
        [((64, 128), f32)],
        [],
    )[0]
    sums = sum_bits("mp", sums, 1, lax.axis_size("mp"))
    self_halves = fold_cores(keep, after(self_got, sums, cross_last))
    self_once = send_once(self_halves)
    cross_sums = fold_twice(after(cross_halves, self_halves), cross_once, cross_twice_got)
    cross_sent = send_slots(cross_sums)
    sums = sum_bits("dp", after(sums, self_halves), 1, 2)
    self_last = fold_once(after(self_halves, cross_sums), self_once)
    self_twice_got = send_twice(self_last)
    self_sums = fold_twice(after(self_halves, sums, cross_sent), self_once, self_twice_got)
    self_sent = send_slots(self_sums)
    sums = sum_bits("dp", after(sums, self_sums), 2, lax.axis_size("dp"))

    def last(value):
        return after(value, self_sums)

    cross_mats = four_matrices(last(cross_sums), cross_sent)
    encoder_mats = four_matrices(last(encoder_sums), encoder_sent)
    encoder_output = (last(encoder_r1) + encoder_out.astype(f32)).astype(bf16)
    encoder_widen_grad, encoder_narrow_grad = two_matrices(*last(encoder_sums[4:]))
    table_rows = memory_table.shape[0] // (lax.axis_size("dp") * lax.axis_size("mp"))
    table_grad = call(
        functools.partial(table_kernel, prefix_rows),
        "table",
        [last(place_in), last(used)],
        (0,),
        (),
        [((table_rows, PREFIX, width), f32)],
        [],
    )[0]
    decoder_output = (
        last(cross_r2) + out + sum(part[:tokens].astype(f32) for part in decoder_out)
    ).astype(bf16)
    decoder_widen_grad, decoder_narrow_grad = two_matrices(*last(cross_sums[4:]))
    self_mats = four_matrices(self_sums, self_sent)

    gain_sums = [sums[32 + 6 * i : 38 + 6 * i].reshape(-1) for i in range(5)]
    buckets, heads = encoder_bias.shape
    bias_grads = [sums[:buckets, i * heads : (i + 1) * heads] for i in range(2)]
    return (
        encoder_output,
        encoder_input_grad,
        table_grad,
        bias_grads[0],
        gain_sums[0],
        *encoder_mats,
        gain_sums[1],
        encoder_widen_grad,
        encoder_narrow_grad,
        decoder_output,
        decoder_input_grad,
        states_grad,
        bias_grads[1],
        gain_sums[2],
        *self_mats,
        gain_sums[3],
        *cross_mats,
        gain_sums[4],
        decoder_widen_grad,
        decoder_narrow_grad,
    )


def solution(mesh):
    rows = P(("dp", "mp"), None)
    columns = P(None, "mp")
    lines = P("mp", None)
    attention = (columns, columns, columns, lines)
    in_specs = (
        (rows, rows, P("dp", None), P(), P(), P(), P())
        + attention
        + (P(), columns, lines, rows, rows, rows, P(), P(), P())
        + attention
        + (P(),)
        + attention
        + (P(), columns, lines)
    )
    both = P("dp", "mp")
    turned = P("mp", "dp")
    grads = (both, both, both, turned)
    out_specs = (
        (rows, rows, P(("dp", "mp"), None, None), P(), P())
        + grads
        + (P(), both, turned, rows, rows, rows, P(), P())
        + grads
        + (P(),)
        + grads
        + (P(), both, turned)
    )
    return jax.shard_map(shards, mesh=mesh, in_specs=in_specs, out_specs=out_specs, check_vma=False)
```

```python
import functools

import jax
import jax.numpy as jnp
from jax import lax
from jax.experimental import pallas as pl
from jax.experimental.pallas import tpu as pltpu
from jax.sharding import PartitionSpec as P

DH = 64
SEQ = 64
MEMK = 10
PREFIX = 2
EPS = 1e-06
NEG = -1e30
BLOCKS = 8
bf16 = jnp.bfloat16
f32 = jnp.float32


def nn(left, right):
    return lax.dot_general(left, right, (((1,), (0,)), ((), ())), preferred_element_type=f32)


def nt(left, right):
    return lax.dot_general(left, right, (((1,), (1,)), ((), ())), preferred_element_type=f32)


def tn(left, right):
    return lax.dot_general(left, right, (((0,), (0,)), ((), ())), preferred_element_type=f32)


def from_mp(array, step):
    size = lax.axis_size("mp")
    return lax.ppermute(array, "mp", [(i, (i - step) % size) for i in range(size)])


def to_mp(array, step):
    size = lax.axis_size("mp")
    return lax.ppermute(array, "mp", [(i, (i + step) % size) for i in range(size)])


def swap_dp(array, bit):
    return lax.ppermute(array, "dp", [(i, i ^ bit) for i in range(lax.axis_size("dp"))])


def after(value, *earlier):
    leaves, shape = jax.tree.flatten(value)
    tied = lax.optimization_barrier((*leaves, *jax.tree.leaves(earlier)))
    return jax.tree.unflatten(shape, tied[: len(leaves)])


def high_bits():
    low = lax.axis_size("dp") // BLOCKS
    return low, 2 * low, 4 * low


def rounded_sum(left, right):
    return (left.astype(f32) + right.astype(f32)).astype(bf16)


def swap_cores(array):
    return swap_dp(array, high_bits()[0])


def fold_cores(keep, got):
    return tuple(
        (rounded_sum(keep[i, :2], got[i, :2]), rounded_sum(keep[i, 2:], got[i, 2:])) for i in range(2)
    )


def send_once(halves):
    core, along, across = high_bits()
    return swap_dp(halves[0][1], along), swap_dp(halves[1][1], across)


def fold_once(halves, got):
    return tuple(rounded_sum(halves[i][0][1], got[i][1]) for i in range(2))


def send_twice(last):
    core, along, across = high_bits()
    return swap_dp(last[0], across), swap_dp(last[1], along)


def fold_twice(halves, got, last_got):
    sums = [
        halves[i][0][0].astype(f32) + got[i][0].astype(f32) + last_got[i].astype(f32) for i in range(2)
    ]
    return [sums[0][0], sums[0][1], sums[1][0], sums[1][1]] + [part[i] for i in range(2, sums[0].shape[0]) for part in sums]


def send_slots(slots):
    return [to_mp(slots[step].astype(bf16), step) for step in range(1, 4)]


def scatter_rest(rows):
    size = lax.axis_size("dp")
    low = size // BLOCKS
    if low == 1:
        return rows
    groups = [[high * low + i for i in range(low)] for high in range(BLOCKS)]
    return lax.psum_scatter(
        rows, "dp", scatter_dimension=0, axis_index_groups=groups, tiled=True
    )


def four_matrices(slots, got):
    total = slots[0]
    if lax.axis_size("dp") == BLOCKS:
        rows, width = total.shape
        part = width // 4
        return call(
            finish_kernel,
            "matrices",
            [total, *got],
            (),
            (),
            [((rows, part), f32)] * 3 + [((part, rows), f32)],
            [],
        )
    for other in got:
        total = total + other.astype(f32)
    total = scatter_rest(total)
    width = total.shape[1] // 4
    parts = [total[:, i * width : (i + 1) * width] for i in range(4)]
    return parts[0], parts[1], parts[2], parts[3].T


def two_matrices(widen, narrow):
    return scatter_rest(widen), scatter_rest(narrow).T


def gather_blocks(slots):
    low = lax.axis_size("dp") // BLOCKS
    groups = [[high * low + i for high in range(BLOCKS)] for i in range(low)]
    if low == 1:
        groups = None
    return lax.all_gather(slots, "dp", axis=0, axis_index_groups=groups, tiled=False)


def sum_bits(axis, array, bit, end):
    size = lax.axis_size(axis)
    while bit < end:
        array = array + lax.ppermute(array, axis, [(i, i ^ bit) for i in range(size)])
        bit *= 2
    return array


def fetch_weights(weights, group, held, sems, order):
    copies = {}
    for i, what in enumerate(order):
        blocks = pl.ds(6, 2) if what == "merge" else pl.ds(0, 6)
        for slot in range(4):
            copies[what, slot] = pltpu.make_async_copy(
                weights.at[blocks, slot, group], held.at[slot, blocks], sems.at[slot, i]
            )
            copies[what, slot].start()
    return copies


def slot_rows(held, slot, first, last):
    part = held[slot, 2 * first : 2 * last]
    return part.reshape(part.shape[0] * part.shape[1], part.shape[2])


def wait_all(copies):
    for copy in copies:
        copy.wait()


def blocks_kernel(groups, place_ref, *refs):
    inputs = refs[: 4 * groups]
    first, others, sems = refs[4 * groups :]
    outs = [first] + [others.at[i] for i in range(groups - 1)]
    size = first.shape[0]
    place = place_ref[0]
    start = pl.multiple_of((place % 2) * size, size)
    for j in range(4):

        @pl.when(place // 2 == j)
        def _():
            copies = [
                pltpu.make_async_copy(inputs[4 * i + j].at[pl.ds(start, size)], outs[i], sems.at[i])
                for i in range(groups)
            ]
            for copy in copies:
                copy.start()
            wait_all(copies)


def inverse_rms(rows):
    return lax.rsqrt(jnp.mean(rows * rows, axis=-1, keepdims=True) + EPS)


def gain_rows(kind, gains_ref):
    at = {"encoder": (0, 1), "self": (2, 3), "cross": (3, 4)}[kind]
    return tuple(gains_ref[i : i + 1, :] for i in at)


def column_head(shape):
    return lax.broadcasted_iota(jnp.int32, shape, 1) // DH


def softmax_rows(scores):
    shifted = jnp.exp(scores - jnp.max(scores, axis=-1, keepdims=True))
    return shifted / jnp.sum(shifted, axis=-1, keepdims=True)


def masks(kind, rows, keys):
    row = lax.broadcasted_iota(jnp.int32, (rows, rows), 0)
    col = lax.broadcasted_iota(jnp.int32, (rows, rows), 1)
    same = row // SEQ == col // SEQ
    if kind == "self":
        same = jnp.logical_and(same, col <= row)
    if kind != "encoder":
        return same, None
    row = lax.broadcasted_iota(jnp.int32, (rows, keys - rows), 0)
    col = lax.broadcasted_iota(jnp.int32, (rows, keys - rows), 1)
    first = (row // SEQ) * (MEMK * PREFIX)
    valid = jnp.logical_and(col >= first, col < first + MEMK * PREFIX)
    return same, jnp.where(valid, 0.0, NEG)


def add_bias(kind, scores, rel_ref, slot, same, before):
    rows = scores.shape[0] // 3
    parts = []
    for j in range(3):
        part = scores[j * rows : (j + 1) * rows]
        own = part[:, :rows]
        if kind != "cross":
            rel = rel_ref[3 * slot + j]
            own = own + jnp.concatenate([rel] * (rows // SEQ), axis=0)
        own = jnp.where(same, own, NEG)
        if before is not None:
            own = jnp.concatenate([own, part[:, rows:] + before], axis=1)
        parts.append(own)
    return jnp.concatenate(parts, axis=0)


def stack_heads(array):
    head = column_head(array.shape)
    return jnp.concatenate([jnp.where(head == j, array, jnp.zeros_like(array)) for j in range(3)], axis=0)


def join_heads(stacked):
    rows = stacked.shape[0] // 3
    head = column_head((rows, stacked.shape[1]))
    return jnp.where(
        head == 0,
        stacked[:rows],
        jnp.where(head == 1, stacked[rows : 2 * rows], stacked[2 * rows :]),
    )


def attention_forward_kernel(kind, *refs):
    refs = list(refs)
    place_ref, x_ref = refs[:2]
    del refs[:2]
    pre_ref = refs.pop(0) if kind != "self" else None
    gains_ref = refs.pop(0)
    gain, later = gain_rows(kind, gains_ref)
    rel_ref = refs.pop(0) if kind != "cross" else None
    weights, r1_ref, next_ref, a_ref, q_ref, kv_ref, o_ref, held, sems = refs
    copies = fetch_weights(weights, int(kind == "cross"), held, sems, ("rest", "merge"))
    r = x_ref[...].astype(f32)
    rows = r.shape[0]
    a = (r * inverse_rms(r) * gain).astype(bf16)
    if kind == "encoder":
        a_ref[0:rows, :] = a
        a_ref[rows:, :] = pre_ref[...]
        a_all = a_ref[...]
    else:
        a_ref[...] = a
        a_all = a
    keys = kv_ref.shape[1]
    same, before = masks(kind, rows, keys)
    queries = []
    sources = []
    for slot in range(4):
        copies["rest", slot].wait()
        if kind == "cross":
            q = nt(a, slot_rows(held, slot, 0, 1)).astype(bf16)
            kv = nt(pre_ref[...], slot_rows(held, slot, 1, 3)).astype(bf16)
        else:
            qkv = nt(a_all, slot_rows(held, slot, 0, 3)).astype(bf16)
            q = qkv[:rows, :192]
            kv = qkv[:, 192:]
        q_ref[slot] = q
        kv_ref[slot] = kv
        queries.append(q)
        sources.append(kv)
    chances = []
    for slot in range(4):
        scores = nt(stack_heads(queries[slot]), sources[slot][:, :192])
        chances.append(softmax_rows(add_bias(kind, scores, rel_ref, slot, same, before)).astype(bf16))
    mixed = []
    for slot in range(4):
        o = join_heads(nn(chances[slot], sources[slot][:, 192:])).astype(bf16)
        o_ref[slot] = o
        mixed.append(o)
    acc = r
    for slot in range(4):
        copies["merge", slot].wait()
        acc = acc + nn(mixed[slot], slot_rows(held, slot, 3, 4))
    r1_ref[...] = acc
    next_ref[...] = (acc * inverse_rms(acc) * later).astype(bf16)


def norm_back(dn, r, gain, dgain_ref):
    t = inverse_rms(r)
    dgain_ref[...] = jnp.sum(dn * r * t, axis=0, keepdims=True)
    scaled = dn * gain
    return t * (scaled - r * (t * t) * jnp.mean(scaled * r, axis=-1, keepdims=True))


def attention_backward_kernel(kind, after_ffn, *refs):
    refs = list(refs)
    place_ref = refs.pop(0)
    place = place_ref[0]
    if after_ffn:
        dc_own, *dc_rest = refs[:4]
        up_ref, r1_ref = refs[4:6]
        refs = refs[6:]
    else:
        up_ref = refs.pop(0)
    x_ref, gains_ref, a_ref = refs[:3]
    gain, later = gain_rows(kind, gains_ref)
    refs = refs[3:]
    source_ref = refs.pop(0) if kind == "cross" else None
    q_ref, kv_ref, o_ref = refs[:3]
    weights = refs[3]
    refs = refs[4:]
    rel_ref, bucket_ref = (refs.pop(0), refs.pop(0)) if kind != "cross" else (None, None)
    if kind != "self":
        refs = refs[2:]
    dx_ref, dgain_ref = refs[:2]
    refs = refs[2:]
    keep_ref, send_ref = refs.pop(0), refs.pop(0)
    later_grad = refs.pop(0) if after_ffn else None
    if kind == "encoder":
        dpre_ref = refs.pop(0)
    elif kind == "cross":
        dsource_ref = refs.pop(0)
    bias_grad = refs.pop(0) if kind != "cross" else None
    held, sems, left, right = refs[:4]
    refs = refs[4:]
    ds_sum = refs.pop(0) if kind != "cross" else None
    stage, out_sems = refs
    copies = fetch_weights(weights, int(kind == "cross"), held, sems, ("merge", "rest"))

    d_out = up_ref[...].astype(f32)
    if after_ffn:
        dn = dc_own[...]
        for part in dc_rest:
            dn = dn + part[...].astype(f32)
        d_out = d_out + norm_back(dn, r1_ref[...], later, later_grad)
    g = d_out.astype(bf16)
    rows, width = g.shape
    keys = kv_ref.shape[1]
    stacked = [a_ref[...]] + ([source_ref[...]] if kind == "cross" else []) + [g]
    turned = jnp.concatenate(stacked, axis=0).T
    size = width // BLOCKS
    for d in range(BLOCKS):
        away = place ^ d
        at = pl.multiple_of(((away % 2) * 4 + away // 2) * size, size)
        left[pl.ds(at, size), :] = turned[d * size : (d + 1) * size]
    source_at = rows if kind == "cross" else 0
    g_at = left.shape[1] - rows
    right[...] = jnp.zeros(right.shape, bf16)
    same, before = masks(kind, rows, keys)
    grads = []
    for slot in range(4):
        copies["merge", slot].wait()
        grads.append(nt(g, slot_rows(held, slot, 3, 4)).astype(bf16))
        right[slot, g_at:, 576:768] = o_ref[slot]
    chances = []
    for slot in range(4):
        scores = nt(stack_heads(q_ref[slot]), kv_ref[slot][:, :192])
        chances.append(softmax_rows(add_bias(kind, scores, rel_ref, slot, same, before)))
    d_scores = []
    for slot in range(4):
        p = chances[slot]
        do_heads = stack_heads(grads[slot])
        dv = tn(p.astype(bf16), do_heads).astype(bf16)
        right[slot, source_at : source_at + keys, 384:576] = dv
        dp = nt(do_heads, kv_ref[slot][:, 192:])
        ds = (p * (dp - jnp.sum(dp * p, axis=-1, keepdims=True))).astype(bf16)
        d_scores.append(ds)
    for slot in range(4):
        ds = d_scores[slot]
        right[slot, 0:rows, 0:192] = join_heads(nn(ds, kv_ref[slot][:, :192])).astype(bf16)
        right[slot, source_at : source_at + keys, 192:384] = tn(ds, stack_heads(q_ref[slot])).astype(bf16)
        if kind != "cross":
            for j in range(3):
                wide = ds[j * rows : (j + 1) * rows, :rows].astype(f32)
                ds_sum[3 * slot + j] = wide[:SEQ] + wide[SEQ:]
    outgoing = []
    for slot in range(4):
        grad = nn(left[...], right[slot]).astype(bf16)
        for j in range(BLOCKS):
            to = (j // 4) * 4 + ((j % 2) * 2 + (j % 4) // 2 if slot // 2 == 0 else j % 4)
            stage[slot, to] = grad[j * size : (j + 1) * size]
        for i, out in enumerate((keep_ref, send_ref)):
            copy = pltpu.make_async_copy(
                stage.at[slot, pl.ds(4 * i, 4)], out.at[slot // 2, :, slot % 2], out_sems.at[slot, i]
            )
            copy.start()
            outgoing.append(copy)
    total = None
    source_total = None
    for slot in range(4):
        copies["rest", slot].wait()
        if kind == "cross":
            part = nn(right[slot, 0:rows, 0:192], slot_rows(held, slot, 0, 1))
            other = nn(right[slot, rows : rows + keys, 192:576], slot_rows(held, slot, 1, 3))
            source_total = other if slot == 0 else source_total + other
        else:
            part = nn(right[slot, 0:keys, 0:576], slot_rows(held, slot, 0, 3))
        total = part if slot == 0 else total + part
    if kind == "cross":
        dsource_ref[...] = source_total
    if kind == "encoder":
        dpre_ref[...] = total[rows:].astype(bf16)
    dx_ref[...] = d_out + norm_back(total[:rows], x_ref[...].astype(f32), gain, dgain_ref)
    if kind != "cross":
        bucket = bucket_ref[...]
        heads, buckets = bias_grad.shape[:2]

        @pl.loop(0, buckets)
        def _(b):
            chosen = bucket == b
            for head in range(heads):
                part = jnp.where(chosen, ds_sum[head], 0.0)
                bias_grad[head, b] = jnp.sum(part.reshape(SEQ // 8, 8, 2 * SEQ), axis=0)

    wait_all(outgoing)


def ffn_first_kernel(c0, c1, c2, c3, g0, g1, g2, g3, widen, narrow, c_all, g_all, h_ref, du_ref, dc_own, dc_rest):
    tokens = c0.shape[0]
    for i, (c, g) in enumerate(((c0, g0), (c1, g1), (c2, g2), (c3, g3))):
        c_all[i * tokens : (i + 1) * tokens, :] = c[...]
        g_all[i * tokens : (i + 1) * tokens, :] = g[...]
    inner = 0.7978845608028654
    for n in range(widen.shape[1] // 256):
        at = slice(n * 256, (n + 1) * 256)
        u = nn(c_all[...], widen[:, at])
        u2 = u * u
        th = jnp.tanh(inner * (u + 0.044715 * u * u2))
        h_ref[:, at] = (0.5 * u * (1.0 + th)).astype(bf16)
        slope = 0.5 * (1.0 + th) + (0.5 * inner) * u * (1.0 - th * th) * (1.0 + 3 * 0.044715 * u2)
        dh = nt(g_all[...], narrow[at, :])
        du_ref[:, at] = (dh * slope).astype(bf16)
    for n in range(widen.shape[0] // 256):
        at = slice(n * 256, (n + 1) * 256)
        dc = nt(du_ref[...], widen[at, :])
        dc_own[:, at] = dc[:tokens]
        for i in range(3):
            dc_rest[i, :, at] = dc[(i + 1) * tokens : (i + 2) * tokens].astype(bf16)


def ffn_second_kernel(across, place_ref, c_all, g_all, h_ref, du_ref, narrow, *refs):
    outs = refs[:-4]
    keep_ref, send_ref, stage, sems = refs[-4:]
    tokens = c_all.shape[0] // 4
    if not across:
        packed, *outs = outs
        for out in outs[1:]:
            out[tokens:, :] = packed[...]
    place = place_ref[0]
    copies = []
    for half, (left, right) in enumerate(((c_all, du_ref), (g_all, h_ref))):
        grad = tn(left[...], right[...]).astype(bf16)
        size = grad.shape[0] // BLOCKS
        for d in range(BLOCKS):
            away = place ^ d
            where = away // 2
            if half == 0:
                where = (where % 2) * 2 + where // 2
            stage[half, (away % 2) * 4 + where] = grad[d * size : (d + 1) * size]
        for i, ref in enumerate((keep_ref, send_ref)):
            copy = pltpu.make_async_copy(
                stage.at[half, pl.ds(4 * i, 4)], ref.at[half, :, 2], sems.at[half, i]
            )
            copy.start()
            copies.append(copy)
    for n in range(narrow.shape[1] // 256):
        at = slice(n * 256, (n + 1) * 256)
        out = nn(h_ref[...], narrow[:, at])
        for i in range(4):
            part = out[i * tokens : (i + 1) * tokens]
            if across:
                row = pl.multiple_of((place_ref[1] + i) % 4 * tokens, tokens)
                outs[0][pl.ds(row, tokens), at] = part.astype(bf16)
            else:
                outs[i][0:tokens, at] = part.astype(outs[i].dtype)
    wait_all(copies)


def gains_kernel(*refs):
    for i in range(5):
        refs[5][i : i + 1, :] = refs[i][...].reshape(1, -1)


def finish_kernel(total_ref, got1, got2, got3, query, key, value, merge):
    total = total_ref[...]
    for got in (got1, got2, got3):
        total = total + got[...].astype(f32)
    width = query.shape[1]
    for i, out in enumerate((query, key, value)):
        out[...] = total[:, i * width : (i + 1) * width]
    merge[...] = total[:, 3 * width :].T


def table_kernel(rows, place_ref, used_ref, out_ref):
    entries = out_ref.shape[0]
    size = used_ref.shape[1]
    first = (place_ref[2] * entries).astype(f32)
    row = lax.broadcasted_iota(jnp.int32, (PREFIX * entries, size), 0)
    column = lax.broadcasted_iota(jnp.int32, (PREFIX * entries, size), 1)
    wanted = (row % entries).astype(f32) + first
    fits = jnp.logical_and(column % PREFIX == row // entries, column < rows)
    total = jnp.zeros((PREFIX * entries, used_ref.shape[2]), f32)
    for i in range(used_ref.shape[0]):
        number = used_ref[i, :, 0:128].astype(f32)
        entry = number[rows : rows + 1, :size] * 32.0 + number[rows + 1 : rows + 2, :size]
        chosen = jnp.logical_and(entry == wanted, fits)
        total = total + nn(jnp.where(chosen, 1.0, 0.0).astype(bf16), used_ref[i])
    for p in range(PREFIX):
        out_ref[:, p, :] = total[p * entries : (p + 1) * entries]


def pack_kernel(place_ref, *refs):
    out = refs[7]
    out[...] = jnp.zeros(out.shape, f32)
    for i in range(2):
        raw = refs[5 + i]
        heads, buckets = raw.shape[:2]
        sums = jnp.sum(jnp.sum(raw[...], axis=2), axis=-1)
        here = lax.broadcasted_iota(jnp.int32, (heads, 128), 0)
        column = lax.broadcasted_iota(jnp.int32, (heads, 128), 1)
        target = (here + place_ref[1] * (heads // 4)) % heads + i * heads
        turn = jnp.where(column == target, 1.0, 0.0)
        out[0:buckets, :] += lax.dot_general(
            sums,
            turn,
            (((0,), (0,)), ((), ())),
            precision=lax.Precision.HIGHEST,
            preferred_element_type=f32,
        )
    for i in range(5):
        for j in range(6):
            out[32 + 6 * i + j : 33 + 6 * i + j, :] = refs[i][:, 128 * j : 128 * (j + 1)]


def call(kernel, name, operands, smem, hbm, outs, scratch, limit=28, hbm_outs=(), aliases=None):
    specs = []
    for i in range(len(operands)):
        if i in smem:
            specs.append(pl.BlockSpec(memory_space=pltpu.SMEM))
        elif i in hbm:
            specs.append(pl.BlockSpec(memory_space=pl.ANY))
        else:
            specs.append(pl.BlockSpec(memory_space=pltpu.VMEM))
    return pl.pallas_call(
        kernel,
        out_shape=[jax.ShapeDtypeStruct(shape, kind) for shape, kind in outs],
        in_specs=specs,
        out_specs=[
            pl.BlockSpec(memory_space=pl.ANY if i in hbm_outs else pltpu.VMEM)
            for i in range(len(outs))
        ],
        scratch_shapes=scratch,
        input_output_aliases=aliases or {},
        compiler_params=pltpu.CompilerParams(vmem_limit_bytes=limit * 1024 * 1024),
        cost_estimate=pl.CostEstimate(flops=0, bytes_accessed=1024, transcendentals=0),
        name=name,
    )(*operands)


def weight_blocks(place, groups):
    count = len(groups)
    operands = [place]
    for query, key, value, merge in groups:
        operands += [query.T, key.T, value.T, merge]
    columns, rows = operands[1].shape
    return call(
        functools.partial(blocks_kernel, count),
        "weight_blocks",
        operands,
        (0,),
        range(1, len(operands)),
        [
            ((4 * columns // BLOCKS, rows), bf16),
            ((count - 1, 4 * columns // BLOCKS, rows), bf16),
        ],
        [pltpu.SemaphoreType.DMA((count,))],
        60,
    )


def attention_forward(kind, place, x, extra, gains, rel, weights):
    rows, width = x.shape
    extra_rows = extra.shape[0] if kind == "encoder" else 0
    keys = rows + extra_rows
    operands = [place, x]
    if extra is not None:
        operands.append(extra)
    operands.append(gains)
    if rel is not None:
        operands.append(rel)
    hbm = (len(operands),)
    operands.append(weights)
    return call(
        functools.partial(attention_forward_kernel, kind),
        kind + "_forward",
        operands,
        (0,),
        hbm,
        [
            ((rows, width), f32),
            ((rows, width), bf16),
            ((keys, width), bf16),
            ((4, rows, 192), bf16),
            ((4, keys, 384), bf16),
            ((4, rows, 192), bf16),
        ],
        [pltpu.VMEM((4, BLOCKS, width // BLOCKS, width), bf16), pltpu.SemaphoreType.DMA((4, 2))],
        56,
    )


def attention_backward(
    kind, place, ffn, upstream, x, gains, stored, source, weights, rel, bucket, buckets, grads
):
    rows, width = upstream.shape
    a, q, kv, o = stored
    keys = kv.shape[1]
    operands = [place]
    if ffn is not None:
        dc_own, dc_rest, r1 = ffn
        operands += [dc_own, *dc_rest, upstream, r1]
    else:
        operands += [upstream]
    operands += [x, gains, a]
    if source is not None:
        operands.append(source)
    operands += [q, kv, o]
    hbm = (len(operands),)
    operands.append(weights)
    if kind != "cross":
        operands += [rel, bucket]
    aliases = None
    if grads is not None:
        hbm += (len(operands), len(operands) + 1)
        aliases = {len(operands): 2, len(operands) + 1: 3}
        operands += grads
    block = width // BLOCKS
    outs = [
        ((rows, width), f32),
        ((1, width), f32),
    ]
    outs += [((2, 4, 2 if grads is None else 3, block, width), bf16)] * 2
    if ffn is not None:
        outs.append(((1, width), f32))
    if kind == "encoder":
        outs.append(((keys - rows, width), bf16))
    elif kind == "cross":
        outs.append(((rows, width), f32))
    if kind != "cross":
        outs.append(((rel.shape[0], buckets, 8, 2 * SEQ), f32))
    depth = 2 * rows + (keys if kind == "cross" else keys - rows)
    scratch = [
        pltpu.VMEM((4, BLOCKS, block, width), bf16),
        pltpu.SemaphoreType.DMA((4, 2)),
        pltpu.VMEM((width, depth), bf16),
        pltpu.VMEM((4, depth, width), bf16),
    ]
    if kind != "cross":
        scratch.append(pltpu.VMEM((rel.shape[0], SEQ, 2 * SEQ), f32))
    scratch += [pltpu.VMEM((4, BLOCKS, block, width), bf16), pltpu.SemaphoreType.DMA((4, 2))]
    return call(
        functools.partial(attention_backward_kernel, kind, ffn is not None),
        kind + "_backward",
        operands,
        (0,),
        hbm,
        outs,
        scratch,
        56,
        (2, 3),
        aliases,
    )


def ffn_first(name, c_parts, g_parts, widen, narrow):
    tokens, width = c_parts[0].shape
    hidden = widen.shape[1]
    every = 4 * tokens
    return call(
        ffn_first_kernel,
        name + "_first",
        [*c_parts, *g_parts, widen, narrow],
        (),
        (),
        [
            ((every, width), bf16),
            ((every, width), bf16),
            ((every, hidden), bf16),
            ((every, hidden), bf16),
            ((tokens, width), f32),
            ((3, tokens, width), bf16),
        ],
        [],
    )


def ffn_second(name, packed, place, c_all, g_all, h, du, narrow):
    every, width = c_all.shape
    hidden = h.shape[1]
    tokens = every // 4
    block = width // BLOCKS
    across = packed is None
    operands = [place, c_all, g_all, h, du, narrow]
    if across:
        outs = [((every, width), bf16)]
    else:
        operands.append(packed)
        outs = [((tokens, width), f32)] + [((tokens + packed.shape[0], width), bf16)] * 3
    count = len(outs)
    return call(
        functools.partial(ffn_second_kernel, across),
        name + "_second",
        operands,
        (0,),
        (),
        outs + [((2, 4, 3, block, hidden), bf16)] * 2,
        [pltpu.VMEM((2, BLOCKS, block, hidden), bf16), pltpu.SemaphoreType.DMA((2, 2))],
        28,
        (count, count + 1),
    )


def gather_tokens(part):
    return [part] + [from_mp(part, step) for step in range(1, 4)]


def return_tokens(rest):
    return [to_mp(rest[step - 1], step) for step in range(1, 4)]


def relative_bias(bucket, table, heads_here):
    twice = jnp.concatenate([bucket, bucket], axis=1)
    onehot = (
        lax.broadcasted_iota(jnp.int32, (table.shape[0], 1), 0) == twice.reshape(1, -1)
    ).astype(f32)
    start = lax.axis_index("mp") * heads_here
    columns = jnp.concatenate([table.T, table.T], axis=0)
    ordered = lax.dynamic_slice_in_dim(columns, start, table.shape[1], 0)
    looked = jnp.dot(ordered, onehot, precision=lax.Precision.HIGHEST)
    return looked.reshape(table.shape[1], SEQ, 2 * SEQ), twice


def shards(
    encoder_input,
    encoder_upstream,
    memory_index,
    memory_table,
    encoder_bucket,
    encoder_bias,
    encoder_gain,
    encoder_query,
    encoder_key,
    encoder_value,
    encoder_merge,
    encoder_later_gain,
    encoder_widen,
    encoder_narrow,
    decoder_input,
    decoder_upstream,
    encoder_states,
    decoder_bucket,
    decoder_bias,
    decoder_gain,
    decoder_query,
    decoder_key,
    decoder_value,
    decoder_merge,
    cross_gain,
    cross_query,
    cross_key,
    cross_value,
    cross_merge,
    decoder_later_gain,
    decoder_widen,
    decoder_narrow,
):
    heads_here = encoder_query.shape[1] // DH
    width = encoder_input.shape[1]
    dp_at = lax.axis_index("dp")
    mp_at = lax.axis_index("mp")
    place = dp_at // (lax.axis_size("dp") // BLOCKS)
    place_in = jnp.stack([place, mp_at, dp_at * lax.axis_size("mp") + mp_at]).astype(jnp.int32)

    encoder_block, decoder_blocks = weight_blocks(
        place_in,
        [
            (encoder_query, encoder_key, encoder_value, encoder_merge),
            (decoder_query, decoder_key, decoder_value, decoder_merge),
            (cross_query, cross_key, cross_value, cross_merge),
        ],
    )
    encoder_slots = jnp.stack(gather_tokens(encoder_block))[:, None]
    encoder_weights = gather_blocks(encoder_slots)
    encoder_g = gather_tokens(after(encoder_upstream, encoder_slots))

    own_questions = memory_index.shape[0] // lax.axis_size("mp")
    entries = lax.dynamic_slice_in_dim(
        memory_index, mp_at * own_questions, own_questions, 0
    ).reshape(-1)
    prefix = jnp.take(memory_table, entries, axis=0).reshape(-1, width)
    prefix_rows = prefix.shape[0]
    prefix = jnp.pad(prefix, ((0, -prefix_rows % 64), (0, 0)))
    encoder_rel, encoder_twice = relative_bias(encoder_bucket, encoder_bias, heads_here)
    decoder_rel, decoder_twice = relative_bias(decoder_bucket, decoder_bias, heads_here)
    entry_rows = jnp.repeat(entries, PREFIX)
    numbers = jnp.stack([entry_rows // 32, entry_rows % 32]).astype(bf16)
    numbers = jnp.pad(numbers, ((0, -(prefix_rows + 2) % 16), (0, width - prefix_rows)))
    gains = call(
        gains_kernel,
        "gains",
        [encoder_gain, encoder_later_gain, decoder_gain, cross_gain, decoder_later_gain],
        (),
        (),
        [((5, width), f32)],
        [],
    )[0]
    small = (prefix, encoder_rel, encoder_twice, decoder_rel, decoder_twice, numbers, gains)
    small = after(small, encoder_block)
    prefix, encoder_rel, encoder_twice, decoder_rel, decoder_twice, numbers, gains = small
    decoder_slots = gather_tokens(after(decoder_blocks, encoder_g, small))


    encoder_r1, encoder_c, *encoder_stored = attention_forward(
        "encoder",
        after(place_in, encoder_g),
        encoder_input,
        prefix,
        gains,
        encoder_rel,
        encoder_weights,
    )
    decoder_weights = gather_blocks(jnp.stack(after(decoder_slots, encoder_r1)))
    encoder_c = gather_tokens(encoder_c)
    c_all, g_all, h, du, dc_own, dc_rest = ffn_first(
        "encoder_ffn", encoder_c, encoder_g, encoder_widen, encoder_narrow
    )
    encoder_dc = (dc_own, return_tokens(dc_rest))
    out, *grads = ffn_second(
        "encoder_ffn", None, after(place_in, encoder_dc[1][0]), c_all, g_all, h, du, encoder_narrow
    )
    encoder_out = lax.psum_scatter(out, "mp", scatter_dimension=0, tiled=True)
    decoder_g = gather_tokens(after(decoder_upstream, encoder_dc, out))
    (
        encoder_input_grad,
        encoder_gain_grad,
        keep,
        send,
        encoder_later_grad,
        prefix_grad,
        encoder_bias_raw,
    ) = attention_backward(
        "encoder",
        after(place_in, out),
        (*encoder_dc, encoder_r1),
        encoder_upstream,
        encoder_input,
        gains,
        encoder_stored,
        None,
        encoder_weights,
        encoder_rel,
        encoder_twice,
        encoder_bias.shape[0],
        grads,
    )
    encoder_got = swap_cores(after(send, decoder_g))
    packed = jnp.concatenate([prefix_grad[:prefix_rows], numbers])

    self_r1, _, *self_stored = attention_forward(
        "self", after(place_in, encoder_input_grad), decoder_input, None, gains, decoder_rel, decoder_weights
    )
    encoder_halves = fold_cores(after(keep, self_r1), encoder_got)
    encoder_once = send_once(encoder_halves)
    cross_r2, decoder_c, *cross_stored = attention_forward(
        "cross", after(place_in, encoder_halves), self_r1, encoder_states, gains, None, decoder_weights
    )
    decoder_c = gather_tokens(decoder_c)
    c_all, g_all, h, du, dc_own, dc_rest = ffn_first(
        "decoder_ffn",
        [after(decoder_c[0], encoder_out), *decoder_c[1:]],
        decoder_g,
        decoder_widen,
        decoder_narrow,
    )
    decoder_dc = (dc_own, return_tokens(dc_rest))
    encoder_last = fold_once(after(encoder_halves, decoder_dc[1][0]), encoder_once)
    encoder_twice_got = send_twice(encoder_last)
    out, *rest, keep, send = ffn_second(
        "decoder_ffn", packed, after(place_in, encoder_last), c_all, g_all, h, du, decoder_narrow
    )
    grads = [keep, send]

    encoder_sums = fold_twice(
        after(encoder_halves, out), encoder_once, encoder_twice_got
    )
    encoder_sent = send_slots(after(encoder_sums, decoder_dc))

    cross_dx, cross_gain_grad, keep, send, decoder_later_grad, states_grad = attention_backward(
        "cross",
        after(place_in, encoder_sums),
        (*decoder_dc, cross_r2),
        decoder_upstream,
        self_r1,
        gains,
        cross_stored,
        encoder_states,
        decoder_weights,
        None,
        None,
        None,
        grads,
    )
    cross_got = swap_cores(after(send, encoder_sent))
    cross_halves = fold_cores(keep, cross_got)
    cross_once = send_once(cross_halves)
    decoder_out = [to_mp(part, i + 1) for i, part in enumerate(after(rest, cross_halves))]
    tokens = cross_r2.shape[0]
    used = jnp.stack([packed] + [part[tokens:] for part in decoder_out])
    used = lax.all_gather(used, "dp", axis=0, tiled=False).reshape(-1, *packed.shape)
    decoder_input_grad, decoder_gain_grad, keep, send, decoder_bias_raw = attention_backward(
        "self",
        after(place_in, cross_halves),
        None,
        cross_dx,
        decoder_input,
        gains,
        self_stored,
        None,
        decoder_weights,
        decoder_rel,
        decoder_twice,
        decoder_bias.shape[0],
        None,
    )
    self_got = swap_cores(after(send, cross_once, decoder_out))
    cross_last = fold_once(after(cross_halves, decoder_input_grad), cross_once)
    cross_twice_got = send_twice(cross_last)
    sums = call(
        pack_kernel,
        "pack",
        [
            place_in,
            encoder_gain_grad,
            encoder_later_grad,
            decoder_gain_grad,
            cross_gain_grad,
            decoder_later_grad,
            encoder_bias_raw,
            decoder_bias_raw,
        ],
        (0,),
        (),
        [((64, 128), f32)],
        [],
    )[0]
    self_halves = fold_cores(keep, after(self_got, sums, cross_last))
    self_once = send_once(self_halves)
    cross_sums = fold_twice(after(cross_halves, self_halves), cross_once, cross_twice_got)
    cross_sent = send_slots(cross_sums)
    sums = sum_bits("mp", after(sums, cross_sent), 1, lax.axis_size("mp"))
    self_last = fold_once(after(self_halves, cross_sums), self_once)
    self_twice_got = send_twice(self_last)
    self_sums = fold_twice(after(self_halves, sums, cross_sent), self_once, self_twice_got)
    self_sent = send_slots(self_sums)
    sums = sum_bits("dp", after(sums, self_sums), 1, lax.axis_size("dp"))

    def last(value):
        return after(value, self_sums)

    cross_mats = four_matrices(last(cross_sums), cross_sent)
    encoder_mats = four_matrices(last(encoder_sums), encoder_sent)
    encoder_output = (last(encoder_r1) + encoder_out.astype(f32)).astype(bf16)
    encoder_widen_grad, encoder_narrow_grad = two_matrices(*last(encoder_sums[4:]))
    table_rows = memory_table.shape[0] // (lax.axis_size("dp") * lax.axis_size("mp"))
    table_grad = call(
        functools.partial(table_kernel, prefix_rows),
        "table",
        [last(place_in), last(used)],
        (0,),
        (),
        [((table_rows, PREFIX, width), f32)],
        [],
    )[0]
    decoder_output = (
        last(cross_r2) + out + sum(part[:tokens].astype(f32) for part in decoder_out)
    ).astype(bf16)
    decoder_widen_grad, decoder_narrow_grad = two_matrices(*last(cross_sums[4:]))
    self_mats = four_matrices(self_sums, self_sent)

    gain_sums = [sums[32 + 6 * i : 38 + 6 * i].reshape(-1) for i in range(5)]
    buckets, heads = encoder_bias.shape
    bias_grads = [sums[:buckets, i * heads : (i + 1) * heads] for i in range(2)]
    return (
        encoder_output,
        encoder_input_grad,
        table_grad,
        bias_grads[0],
        gain_sums[0],
        *encoder_mats,
        gain_sums[1],
        encoder_widen_grad,
        encoder_narrow_grad,
        decoder_output,
        decoder_input_grad,
        states_grad,
        bias_grads[1],
        gain_sums[2],
        *self_mats,
        gain_sums[3],
        *cross_mats,
        gain_sums[4],
        decoder_widen_grad,
        decoder_narrow_grad,
    )


def solution(mesh):
    rows = P(("dp", "mp"), None)
    columns = P(None, "mp")
    lines = P("mp", None)
    attention = (columns, columns, columns, lines)
    in_specs = (
        (rows, rows, P("dp", None), P(), P(), P(), P())
        + attention
        + (P(), columns, lines, rows, rows, rows, P(), P(), P())
        + attention
        + (P(),)
        + attention
        + (P(), columns, lines)
    )
    both = P("dp", "mp")
    turned = P("mp", "dp")
    grads = (both, both, both, turned)
    out_specs = (
        (rows, rows, P(("dp", "mp"), None, None), P(), P())
        + grads
        + (P(), both, turned, rows, rows, rows, P(), P())
        + grads
        + (P(),)
        + grads
        + (P(), both, turned)
    )
    return jax.shard_map(shards, mesh=mesh, in_specs=in_specs, out_specs=out_specs, check_vma=False)
```

```python
import functools

import jax
import jax.numpy as jnp
from jax import lax
from jax.experimental import pallas as pl
from jax.experimental.pallas import tpu as pltpu
from jax.sharding import PartitionSpec as P

DH = 64
SEQ = 64
MEMK = 10
PREFIX = 2
EPS = 1e-06
NEG = -1e30
BLOCKS = 8
bf16 = jnp.bfloat16
f32 = jnp.float32


def nn(left, right):
    return lax.dot_general(left, right, (((1,), (0,)), ((), ())), preferred_element_type=f32)


def nt(left, right):
    return lax.dot_general(left, right, (((1,), (1,)), ((), ())), preferred_element_type=f32)


def tn(left, right):
    return lax.dot_general(left, right, (((0,), (0,)), ((), ())), preferred_element_type=f32)


def from_mp(array, step):
    size = lax.axis_size("mp")
    return lax.ppermute(array, "mp", [(i, (i - step) % size) for i in range(size)])


def to_mp(array, step):
    size = lax.axis_size("mp")
    return lax.ppermute(array, "mp", [(i, (i + step) % size) for i in range(size)])


def swap_dp(array, bit):
    return lax.ppermute(array, "dp", [(i, i ^ bit) for i in range(lax.axis_size("dp"))])


def after(value, *earlier):
    leaves, shape = jax.tree.flatten(value)
    tied = lax.optimization_barrier((*leaves, *jax.tree.leaves(earlier)))
    return jax.tree.unflatten(shape, tied[: len(leaves)])


def high_bits():
    low = lax.axis_size("dp") // BLOCKS
    return low, 2 * low, 4 * low


def rounded_sum(left, right):
    return (left.astype(f32) + right.astype(f32)).astype(bf16)


def swap_cores(array):
    return swap_dp(array, high_bits()[0])


def fold_cores(keep, got):
    return tuple(
        (rounded_sum(keep[i, :2], got[i, :2]), rounded_sum(keep[i, 2:], got[i, 2:])) for i in range(2)
    )


def send_once(halves):
    core, along, across = high_bits()
    return swap_dp(halves[0][1], along), swap_dp(halves[1][1], across)


def fold_once(halves, got):
    return tuple(rounded_sum(halves[i][0][1], got[i][1]) for i in range(2))


def send_twice(last):
    core, along, across = high_bits()
    return swap_dp(last[0], across), swap_dp(last[1], along)


def fold_twice(halves, got, last_got):
    sums = [
        halves[i][0][0].astype(f32) + got[i][0].astype(f32) + last_got[i].astype(f32) for i in range(2)
    ]
    return [sums[0][0], sums[0][1], sums[1][0], sums[1][1]] + [part[i] for i in range(2, sums[0].shape[0]) for part in sums]


def send_slots(slots):
    return [to_mp(slots[step].astype(bf16), step) for step in range(1, 4)]


def scatter_rest(rows):
    size = lax.axis_size("dp")
    low = size // BLOCKS
    if low == 1:
        return rows
    groups = [[high * low + i for i in range(low)] for high in range(BLOCKS)]
    return lax.psum_scatter(
        rows, "dp", scatter_dimension=0, axis_index_groups=groups, tiled=True
    )


def four_matrices(slots, got):
    total = slots[0]
    if lax.axis_size("dp") == BLOCKS:
        rows, width = total.shape
        part = width // 4
        return call(
            finish_kernel,
            "matrices",
            [total, *got],
            (),
            (),
            [((rows, part), f32)] * 3 + [((part, rows), f32)],
            [],
        )
    for other in got:
        total = total + other.astype(f32)
    total = scatter_rest(total)
    width = total.shape[1] // 4
    parts = [total[:, i * width : (i + 1) * width] for i in range(4)]
    return parts[0], parts[1], parts[2], parts[3].T


def two_matrices(widen, narrow):
    return scatter_rest(widen), scatter_rest(narrow).T


def gather_blocks(slots):
    low = lax.axis_size("dp") // BLOCKS
    groups = [[high * low + i for high in range(BLOCKS)] for i in range(low)]
    if low == 1:
        groups = None
    return lax.all_gather(slots, "dp", axis=0, axis_index_groups=groups, tiled=False)


def sum_bits(axis, array, bit, end):
    size = lax.axis_size(axis)
    while bit < end:
        array = array + lax.ppermute(array, axis, [(i, i ^ bit) for i in range(size)])
        bit *= 2
    return array


def fetch_weights(weights, group, held, sems, order):
    copies = {}
    for i, what in enumerate(order):
        blocks = pl.ds(6, 2) if what == "merge" else pl.ds(0, 6)
        for slot in range(4):
            copies[what, slot] = pltpu.make_async_copy(
                weights.at[blocks, slot, group], held.at[slot, blocks], sems.at[slot, i]
            )
            copies[what, slot].start()
    return copies


def slot_rows(held, slot, first, last):
    part = held[slot, 2 * first : 2 * last]
    return part.reshape(part.shape[0] * part.shape[1], part.shape[2])


def wait_all(copies):
    for copy in copies:
        copy.wait()


def blocks_kernel(groups, place_ref, *refs):
    inputs = refs[: 4 * groups]
    first, others, sems = refs[4 * groups :]
    outs = [first] + [others.at[i] for i in range(groups - 1)]
    size = first.shape[0]
    place = place_ref[0]
    start = pl.multiple_of((place % 2) * size, size)
    for j in range(4):

        @pl.when(place // 2 == j)
        def _():
            copies = [
                pltpu.make_async_copy(inputs[4 * i + j].at[pl.ds(start, size)], outs[i], sems.at[i])
                for i in range(groups)
            ]
            for copy in copies:
                copy.start()
            wait_all(copies)


def inverse_rms(rows):
    return lax.rsqrt(jnp.mean(rows * rows, axis=-1, keepdims=True) + EPS)


def gain_rows(kind, gains_ref):
    at = {"encoder": (0, 1), "self": (2, 3), "cross": (3, 4)}[kind]
    return tuple(gains_ref[i : i + 1, :] for i in at)


def column_head(shape):
    return lax.broadcasted_iota(jnp.int32, shape, 1) // DH


def softmax_rows(scores):
    shifted = jnp.exp(scores - jnp.max(scores, axis=-1, keepdims=True))
    return shifted / jnp.sum(shifted, axis=-1, keepdims=True)


def masks(kind, rows, keys):
    row = lax.broadcasted_iota(jnp.int32, (rows, rows), 0)
    col = lax.broadcasted_iota(jnp.int32, (rows, rows), 1)
    same = row // SEQ == col // SEQ
    if kind == "self":
        same = jnp.logical_and(same, col <= row)
    if kind != "encoder":
        return same, None
    row = lax.broadcasted_iota(jnp.int32, (rows, keys - rows), 0)
    col = lax.broadcasted_iota(jnp.int32, (rows, keys - rows), 1)
    first = (row // SEQ) * (MEMK * PREFIX)
    valid = jnp.logical_and(col >= first, col < first + MEMK * PREFIX)
    return same, jnp.where(valid, 0.0, NEG)


def add_bias(kind, scores, rel_ref, slot, same, before):
    rows = scores.shape[0] // 3
    parts = []
    for j in range(3):
        part = scores[j * rows : (j + 1) * rows]
        own = part[:, :rows]
        if kind != "cross":
            rel = rel_ref[3 * slot + j]
            own = own + jnp.concatenate([rel] * (rows // SEQ), axis=0)
        own = jnp.where(same, own, NEG)
        if before is not None:
            own = jnp.concatenate([own, part[:, rows:] + before], axis=1)
        parts.append(own)
    return jnp.concatenate(parts, axis=0)


def stack_heads(array):
    head = column_head(array.shape)
    return jnp.concatenate([jnp.where(head == j, array, jnp.zeros_like(array)) for j in range(3)], axis=0)


def join_heads(stacked):
    rows = stacked.shape[0] // 3
    head = column_head((rows, stacked.shape[1]))
    return jnp.where(
        head == 0,
        stacked[:rows],
        jnp.where(head == 1, stacked[rows : 2 * rows], stacked[2 * rows :]),
    )


def attention_forward_kernel(kind, *refs):
    refs = list(refs)
    place_ref, x_ref = refs[:2]
    del refs[:2]
    pre_ref = refs.pop(0) if kind != "self" else None
    gains_ref = refs.pop(0)
    gain, later = gain_rows(kind, gains_ref)
    rel_ref = refs.pop(0) if kind != "cross" else None
    weights, r1_ref, next_ref, a_ref, q_ref, kv_ref, o_ref, held, sems = refs
    copies = fetch_weights(weights, int(kind == "cross"), held, sems, ("rest", "merge"))
    r = x_ref[...].astype(f32)
    rows = r.shape[0]
    a = (r * inverse_rms(r) * gain).astype(bf16)
    if kind == "encoder":
        a_ref[0:rows, :] = a
        a_ref[rows:, :] = pre_ref[...]
        a_all = a_ref[...]
    else:
        a_ref[...] = a
        a_all = a
    keys = kv_ref.shape[1]
    same, before = masks(kind, rows, keys)
    queries = []
    sources = []
    for slot in range(4):
        copies["rest", slot].wait()
        if kind == "cross":
            q = nt(a, slot_rows(held, slot, 0, 1)).astype(bf16)
            kv = nt(pre_ref[...], slot_rows(held, slot, 1, 3)).astype(bf16)
        else:
            qkv = nt(a_all, slot_rows(held, slot, 0, 3)).astype(bf16)
            q = qkv[:rows, :192]
            kv = qkv[:, 192:]
        q_ref[slot] = q
        kv_ref[slot] = kv
        queries.append(q)
        sources.append(kv)
    chances = []
    for slot in range(4):
        scores = nt(stack_heads(queries[slot]), sources[slot][:, :192])
        chances.append(softmax_rows(add_bias(kind, scores, rel_ref, slot, same, before)).astype(bf16))
    mixed = []
    for slot in range(4):
        o = join_heads(nn(chances[slot], sources[slot][:, 192:])).astype(bf16)
        o_ref[slot] = o
        mixed.append(o)
    acc = r
    for slot in range(4):
        copies["merge", slot].wait()
        acc = acc + nn(mixed[slot], slot_rows(held, slot, 3, 4))
    r1_ref[...] = acc
    next_ref[...] = (acc * inverse_rms(acc) * later).astype(bf16)


def norm_back(dn, r, gain, dgain_ref):
    t = inverse_rms(r)
    dgain_ref[...] = jnp.sum(dn * r * t, axis=0, keepdims=True)
    scaled = dn * gain
    return t * (scaled - r * (t * t) * jnp.mean(scaled * r, axis=-1, keepdims=True))


def attention_backward_kernel(kind, after_ffn, *refs):
    refs = list(refs)
    place_ref = refs.pop(0)
    place = place_ref[0]
    if after_ffn:
        dc_own, *dc_rest = refs[:4]
        up_ref, r1_ref = refs[4:6]
        refs = refs[6:]
    else:
        up_ref = refs.pop(0)
    x_ref, gains_ref, a_ref = refs[:3]
    gain, later = gain_rows(kind, gains_ref)
    refs = refs[3:]
    source_ref = refs.pop(0) if kind == "cross" else None
    q_ref, kv_ref, o_ref = refs[:3]
    weights = refs[3]
    refs = refs[4:]
    rel_ref, bucket_ref = (refs.pop(0), refs.pop(0)) if kind != "cross" else (None, None)
    if kind != "self":
        refs = refs[2:]
    dx_ref, dgain_ref = refs[:2]
    refs = refs[2:]
    keep_ref, send_ref = refs.pop(0), refs.pop(0)
    later_grad = refs.pop(0) if after_ffn else None
    if kind == "encoder":
        dpre_ref = refs.pop(0)
    elif kind == "cross":
        dsource_ref = refs.pop(0)
    bias_grad = refs.pop(0) if kind != "cross" else None
    held, sems, left, right = refs[:4]
    refs = refs[4:]
    ds_sum = refs.pop(0) if kind != "cross" else None
    stage, out_sems = refs
    copies = fetch_weights(weights, int(kind == "cross"), held, sems, ("merge", "rest"))

    d_out = up_ref[...].astype(f32)
    if after_ffn:
        dn = dc_own[...]
        for part in dc_rest:
            dn = dn + part[...].astype(f32)
        d_out = d_out + norm_back(dn, r1_ref[...], later, later_grad)
    g = d_out.astype(bf16)
    rows, width = g.shape
    keys = kv_ref.shape[1]
    stacked = [a_ref[...]] + ([source_ref[...]] if kind == "cross" else []) + [g]
    turned = jnp.concatenate(stacked, axis=0).T
    size = width // BLOCKS
    for d in range(BLOCKS):
        away = place ^ d
        at = pl.multiple_of(((away % 2) * 4 + away // 2) * size, size)
        left[pl.ds(at, size), :] = turned[d * size : (d + 1) * size]
    source_at = rows if kind == "cross" else 0
    g_at = left.shape[1] - rows
    right[...] = jnp.zeros(right.shape, bf16)
    same, before = masks(kind, rows, keys)
    grads = []
    for slot in range(4):
        copies["merge", slot].wait()
        grads.append(nt(g, slot_rows(held, slot, 3, 4)).astype(bf16))
        right[slot, g_at:, 576:768] = o_ref[slot]
    chances = []
    for slot in range(4):
        scores = nt(stack_heads(q_ref[slot]), kv_ref[slot][:, :192])
        chances.append(softmax_rows(add_bias(kind, scores, rel_ref, slot, same, before)))
    d_scores = []
    for slot in range(4):
        p = chances[slot]
        do_heads = stack_heads(grads[slot])
        dv = tn(p.astype(bf16), do_heads).astype(bf16)
        right[slot, source_at : source_at + keys, 384:576] = dv
        dp = nt(do_heads, kv_ref[slot][:, 192:])
        ds = (p * (dp - jnp.sum(dp * p, axis=-1, keepdims=True))).astype(bf16)
        d_scores.append(ds)
    for slot in range(4):
        ds = d_scores[slot]
        right[slot, 0:rows, 0:192] = join_heads(nn(ds, kv_ref[slot][:, :192])).astype(bf16)
        right[slot, source_at : source_at + keys, 192:384] = tn(ds, stack_heads(q_ref[slot])).astype(bf16)
        if kind != "cross":
            for j in range(3):
                wide = ds[j * rows : (j + 1) * rows, :rows].astype(f32)
                ds_sum[3 * slot + j] = wide[:SEQ] + wide[SEQ:]
    outgoing = []
    for slot in range(4):
        grad = nn(left[...], right[slot]).astype(bf16)
        for j in range(BLOCKS):
            to = (j // 4) * 4 + ((j % 2) * 2 + (j % 4) // 2 if slot // 2 == 0 else j % 4)
            stage[slot, to] = grad[j * size : (j + 1) * size]
        for i, out in enumerate((keep_ref, send_ref)):
            copy = pltpu.make_async_copy(
                stage.at[slot, pl.ds(4 * i, 4)], out.at[slot // 2, :, slot % 2], out_sems.at[slot, i]
            )
            copy.start()
            outgoing.append(copy)
    total = None
    source_total = None
    for slot in range(4):
        copies["rest", slot].wait()
        if kind == "cross":
            part = nn(right[slot, 0:rows, 0:192], slot_rows(held, slot, 0, 1))
            other = nn(right[slot, rows : rows + keys, 192:576], slot_rows(held, slot, 1, 3))
            source_total = other if slot == 0 else source_total + other
        else:
            part = nn(right[slot, 0:keys, 0:576], slot_rows(held, slot, 0, 3))
        total = part if slot == 0 else total + part
    if kind == "cross":
        dsource_ref[...] = source_total
    if kind == "encoder":
        dpre_ref[...] = total[rows:].astype(bf16)
    dx_ref[...] = d_out + norm_back(total[:rows], x_ref[...].astype(f32), gain, dgain_ref)
    if kind != "cross":
        bucket = bucket_ref[...]
        heads, buckets = bias_grad.shape[:2]

        @pl.loop(0, buckets)
        def _(b):
            chosen = bucket == b
            for head in range(heads):
                part = jnp.where(chosen, ds_sum[head], 0.0)
                bias_grad[head, b] = jnp.sum(part.reshape(SEQ // 8, 8, 2 * SEQ), axis=0)

    wait_all(outgoing)


def ffn_first_kernel(c0, c1, c2, c3, g0, g1, g2, g3, widen, narrow, c_all, g_all, h_ref, du_ref, dc_own, dc_rest):
    tokens = c0.shape[0]
    for i, (c, g) in enumerate(((c0, g0), (c1, g1), (c2, g2), (c3, g3))):
        c_all[i * tokens : (i + 1) * tokens, :] = c[...]
        g_all[i * tokens : (i + 1) * tokens, :] = g[...]
    inner = 0.7978845608028654
    for n in range(widen.shape[1] // 256):
        at = slice(n * 256, (n + 1) * 256)
        u = nn(c_all[...], widen[:, at])
        u2 = u * u
        th = jnp.tanh(inner * (u + 0.044715 * u * u2))
        h_ref[:, at] = (0.5 * u * (1.0 + th)).astype(bf16)
        slope = 0.5 * (1.0 + th) + (0.5 * inner) * u * (1.0 - th * th) * (1.0 + 3 * 0.044715 * u2)
        dh = nt(g_all[...], narrow[at, :])
        du_ref[:, at] = (dh * slope).astype(bf16)
    for n in range(widen.shape[0] // 256):
        at = slice(n * 256, (n + 1) * 256)
        dc = nt(du_ref[...], widen[at, :])
        dc_own[:, at] = dc[:tokens]
        for i in range(3):
            dc_rest[i, :, at] = dc[(i + 1) * tokens : (i + 2) * tokens].astype(bf16)


def ffn_second_kernel(across, place_ref, c_all, g_all, h_ref, du_ref, narrow, *refs):
    outs = refs[:-4]
    keep_ref, send_ref, stage, sems = refs[-4:]
    tokens = c_all.shape[0] // 4
    if not across:
        packed, *outs = outs
        for out in outs[1:]:
            out[tokens:, :] = packed[...]
    place = place_ref[0]
    copies = []
    for half, (left, right) in enumerate(((c_all, du_ref), (g_all, h_ref))):
        grad = tn(left[...], right[...]).astype(bf16)
        size = grad.shape[0] // BLOCKS
        for d in range(BLOCKS):
            away = place ^ d
            where = away // 2
            if half == 0:
                where = (where % 2) * 2 + where // 2
            stage[half, (away % 2) * 4 + where] = grad[d * size : (d + 1) * size]
        for i, ref in enumerate((keep_ref, send_ref)):
            copy = pltpu.make_async_copy(
                stage.at[half, pl.ds(4 * i, 4)], ref.at[half, :, 2], sems.at[half, i]
            )
            copy.start()
            copies.append(copy)
    for n in range(narrow.shape[1] // 256):
        at = slice(n * 256, (n + 1) * 256)
        out = nn(h_ref[...], narrow[:, at])
        for i in range(4):
            part = out[i * tokens : (i + 1) * tokens]
            if across:
                row = pl.multiple_of((place_ref[1] + i) % 4 * tokens, tokens)
                outs[0][pl.ds(row, tokens), at] = part.astype(bf16)
            else:
                outs[i][0:tokens, at] = part.astype(outs[i].dtype)
    wait_all(copies)


def gains_kernel(*refs):
    for i in range(5):
        refs[5][i : i + 1, :] = refs[i][...].reshape(1, -1)


def finish_kernel(total_ref, got1, got2, got3, query, key, value, merge):
    total = total_ref[...]
    for got in (got1, got2, got3):
        total = total + got[...].astype(f32)
    width = query.shape[1]
    for i, out in enumerate((query, key, value)):
        out[...] = total[:, i * width : (i + 1) * width]
    merge[...] = total[:, 3 * width :].T


def table_kernel(rows, place_ref, used_ref, out_ref):
    entries = out_ref.shape[0]
    size = used_ref.shape[1]
    first = (place_ref[2] * entries).astype(f32)
    row = lax.broadcasted_iota(jnp.int32, (PREFIX * entries, size), 0)
    column = lax.broadcasted_iota(jnp.int32, (PREFIX * entries, size), 1)
    wanted = (row % entries).astype(f32) + first
    fits = jnp.logical_and(column % PREFIX == row // entries, column < rows)
    total = jnp.zeros((PREFIX * entries, used_ref.shape[2]), f32)
    for i in range(used_ref.shape[0]):
        number = used_ref[i, :, 0:128].astype(f32)
        entry = number[rows : rows + 1, :size] * 32.0 + number[rows + 1 : rows + 2, :size]
        chosen = jnp.logical_and(entry == wanted, fits)
        total = total + nn(jnp.where(chosen, 1.0, 0.0).astype(bf16), used_ref[i])
    for p in range(PREFIX):
        out_ref[:, p, :] = total[p * entries : (p + 1) * entries]


def pack_kernel(place_ref, *refs):
    out = refs[7]
    out[...] = jnp.zeros(out.shape, f32)
    for i in range(2):
        raw = refs[5 + i]
        heads, buckets = raw.shape[:2]
        sums = jnp.sum(jnp.sum(raw[...], axis=2), axis=-1)
        here = lax.broadcasted_iota(jnp.int32, (heads, 128), 0)
        column = lax.broadcasted_iota(jnp.int32, (heads, 128), 1)
        target = (here + place_ref[1] * (heads // 4)) % heads + i * heads
        turn = jnp.where(column == target, 1.0, 0.0)
        out[0:buckets, :] += lax.dot_general(
            sums,
            turn,
            (((0,), (0,)), ((), ())),
            precision=lax.Precision.HIGHEST,
            preferred_element_type=f32,
        )
    for i in range(5):
        for j in range(6):
            out[32 + 6 * i + j : 33 + 6 * i + j, :] = refs[i][:, 128 * j : 128 * (j + 1)]


def call(kernel, name, operands, smem, hbm, outs, scratch, limit=28, hbm_outs=(), aliases=None):
    specs = []
    for i in range(len(operands)):
        if i in smem:
            specs.append(pl.BlockSpec(memory_space=pltpu.SMEM))
        elif i in hbm:
            specs.append(pl.BlockSpec(memory_space=pl.ANY))
        else:
            specs.append(pl.BlockSpec(memory_space=pltpu.VMEM))
    return pl.pallas_call(
        kernel,
        out_shape=[jax.ShapeDtypeStruct(shape, kind) for shape, kind in outs],
        in_specs=specs,
        out_specs=[
            pl.BlockSpec(memory_space=pl.ANY if i in hbm_outs else pltpu.VMEM)
            for i in range(len(outs))
        ],
        scratch_shapes=scratch,
        input_output_aliases=aliases or {},
        compiler_params=pltpu.CompilerParams(vmem_limit_bytes=limit * 1024 * 1024),
        cost_estimate=pl.CostEstimate(flops=0, bytes_accessed=1024, transcendentals=0),
        name=name,
    )(*operands)


def weight_blocks(place, groups):
    count = len(groups)
    operands = [place]
    for query, key, value, merge in groups:
        operands += [query.T, key.T, value.T, merge]
    columns, rows = operands[1].shape
    return call(
        functools.partial(blocks_kernel, count),
        "weight_blocks",
        operands,
        (0,),
        range(1, len(operands)),
        [
            ((4 * columns // BLOCKS, rows), bf16),
            ((count - 1, 4 * columns // BLOCKS, rows), bf16),
        ],
        [pltpu.SemaphoreType.DMA((count,))],
        60,
    )


def attention_forward(kind, place, x, extra, gains, rel, weights):
    rows, width = x.shape
    extra_rows = extra.shape[0] if kind == "encoder" else 0
    keys = rows + extra_rows
    operands = [place, x]
    if extra is not None:
        operands.append(extra)
    operands.append(gains)
    if rel is not None:
        operands.append(rel)
    hbm = (len(operands),)
    operands.append(weights)
    return call(
        functools.partial(attention_forward_kernel, kind),
        kind + "_forward",
        operands,
        (0,),
        hbm,
        [
            ((rows, width), f32),
            ((rows, width), bf16),
            ((keys, width), bf16),
            ((4, rows, 192), bf16),
            ((4, keys, 384), bf16),
            ((4, rows, 192), bf16),
        ],
        [pltpu.VMEM((4, BLOCKS, width // BLOCKS, width), bf16), pltpu.SemaphoreType.DMA((4, 2))],
        56,
    )


def attention_backward(
    kind, place, ffn, upstream, x, gains, stored, source, weights, rel, bucket, buckets, grads
):
    rows, width = upstream.shape
    a, q, kv, o = stored
    keys = kv.shape[1]
    operands = [place]
    if ffn is not None:
        dc_own, dc_rest, r1 = ffn
        operands += [dc_own, *dc_rest, upstream, r1]
    else:
        operands += [upstream]
    operands += [x, gains, a]
    if source is not None:
        operands.append(source)
    operands += [q, kv, o]
    hbm = (len(operands),)
    operands.append(weights)
    if kind != "cross":
        operands += [rel, bucket]
    aliases = None
    if grads is not None:
        hbm += (len(operands), len(operands) + 1)
        aliases = {len(operands): 2, len(operands) + 1: 3}
        operands += grads
    block = width // BLOCKS
    outs = [
        ((rows, width), f32),
        ((1, width), f32),
    ]
    outs += [((2, 4, 2 if grads is None else 3, block, width), bf16)] * 2
    if ffn is not None:
        outs.append(((1, width), f32))
    if kind == "encoder":
        outs.append(((keys - rows, width), bf16))
    elif kind == "cross":
        outs.append(((rows, width), f32))
    if kind != "cross":
        outs.append(((rel.shape[0], buckets, 8, 2 * SEQ), f32))
    depth = 2 * rows + (keys if kind == "cross" else keys - rows)
    scratch = [
        pltpu.VMEM((4, BLOCKS, block, width), bf16),
        pltpu.SemaphoreType.DMA((4, 2)),
        pltpu.VMEM((width, depth), bf16),
        pltpu.VMEM((4, depth, width), bf16),
    ]
    if kind != "cross":
        scratch.append(pltpu.VMEM((rel.shape[0], SEQ, 2 * SEQ), f32))
    scratch += [pltpu.VMEM((4, BLOCKS, block, width), bf16), pltpu.SemaphoreType.DMA((4, 2))]
    return call(
        functools.partial(attention_backward_kernel, kind, ffn is not None),
        kind + "_backward",
        operands,
        (0,),
        hbm,
        outs,
        scratch,
        56,
        (2, 3),
        aliases,
    )


def ffn_first(name, c_parts, g_parts, widen, narrow):
    tokens, width = c_parts[0].shape
    hidden = widen.shape[1]
    every = 4 * tokens
    return call(
        ffn_first_kernel,
        name + "_first",
        [*c_parts, *g_parts, widen, narrow],
        (),
        (),
        [
            ((every, width), bf16),
            ((every, width), bf16),
            ((every, hidden), bf16),
            ((every, hidden), bf16),
            ((tokens, width), f32),
            ((3, tokens, width), bf16),
        ],
        [],
    )


def ffn_second(name, packed, place, c_all, g_all, h, du, narrow):
    every, width = c_all.shape
    hidden = h.shape[1]
    tokens = every // 4
    block = width // BLOCKS
    across = packed is None
    operands = [place, c_all, g_all, h, du, narrow]
    if across:
        outs = [((every, width), bf16)]
    else:
        operands.append(packed)
        outs = [((tokens, width), f32)] + [((tokens + packed.shape[0], width), bf16)] * 3
    count = len(outs)
    return call(
        functools.partial(ffn_second_kernel, across),
        name + "_second",
        operands,
        (0,),
        (),
        outs + [((2, 4, 3, block, hidden), bf16)] * 2,
        [pltpu.VMEM((2, BLOCKS, block, hidden), bf16), pltpu.SemaphoreType.DMA((2, 2))],
        28,
        (count, count + 1),
    )


def gather_tokens(part):
    return [part] + [from_mp(part, step) for step in range(1, 4)]


def return_tokens(rest):
    return [to_mp(rest[step - 1], step) for step in range(1, 4)]


def relative_bias(bucket, table, heads_here):
    twice = jnp.concatenate([bucket, bucket], axis=1)
    onehot = (
        lax.broadcasted_iota(jnp.int32, (table.shape[0], 1), 0) == twice.reshape(1, -1)
    ).astype(f32)
    start = lax.axis_index("mp") * heads_here
    columns = jnp.concatenate([table.T, table.T], axis=0)
    ordered = lax.dynamic_slice_in_dim(columns, start, table.shape[1], 0)
    looked = jnp.dot(ordered, onehot, precision=lax.Precision.HIGHEST)
    return looked.reshape(table.shape[1], SEQ, 2 * SEQ), twice


def shards(
    encoder_input,
    encoder_upstream,
    memory_index,
    memory_table,
    encoder_bucket,
    encoder_bias,
    encoder_gain,
    encoder_query,
    encoder_key,
    encoder_value,
    encoder_merge,
    encoder_later_gain,
    encoder_widen,
    encoder_narrow,
    decoder_input,
    decoder_upstream,
    encoder_states,
    decoder_bucket,
    decoder_bias,
    decoder_gain,
    decoder_query,
    decoder_key,
    decoder_value,
    decoder_merge,
    cross_gain,
    cross_query,
    cross_key,
    cross_value,
    cross_merge,
    decoder_later_gain,
    decoder_widen,
    decoder_narrow,
):
    heads_here = encoder_query.shape[1] // DH
    width = encoder_input.shape[1]
    dp_at = lax.axis_index("dp")
    mp_at = lax.axis_index("mp")
    place = dp_at // (lax.axis_size("dp") // BLOCKS)
    place_in = jnp.stack([place, mp_at, dp_at * lax.axis_size("mp") + mp_at]).astype(jnp.int32)

    encoder_block, decoder_blocks = weight_blocks(
        place_in,
        [
            (encoder_query, encoder_key, encoder_value, encoder_merge),
            (decoder_query, decoder_key, decoder_value, decoder_merge),
            (cross_query, cross_key, cross_value, cross_merge),
        ],
    )
    encoder_slots = jnp.stack(gather_tokens(encoder_block))[:, None]
    encoder_weights = gather_blocks(encoder_slots)
    encoder_g = gather_tokens(after(encoder_upstream, encoder_slots))

    own_questions = memory_index.shape[0] // lax.axis_size("mp")
    entries = lax.dynamic_slice_in_dim(
        memory_index, mp_at * own_questions, own_questions, 0
    ).reshape(-1)
    prefix = jnp.take(memory_table, entries, axis=0).reshape(-1, width)
    prefix_rows = prefix.shape[0]
    prefix = jnp.pad(prefix, ((0, -prefix_rows % 64), (0, 0)))
    encoder_rel, encoder_twice = relative_bias(encoder_bucket, encoder_bias, heads_here)
    decoder_rel, decoder_twice = relative_bias(decoder_bucket, decoder_bias, heads_here)
    entry_rows = jnp.repeat(entries, PREFIX)
    numbers = jnp.stack([entry_rows // 32, entry_rows % 32]).astype(bf16)
    numbers = jnp.pad(numbers, ((0, -(prefix_rows + 2) % 16), (0, width - prefix_rows)))
    gains = call(
        gains_kernel,
        "gains",
        [encoder_gain, encoder_later_gain, decoder_gain, cross_gain, decoder_later_gain],
        (),
        (),
        [((5, width), f32)],
        [],
    )[0]
    small = (prefix, encoder_rel, encoder_twice, decoder_rel, decoder_twice, numbers, gains)
    small = after(small, encoder_block)
    prefix, encoder_rel, encoder_twice, decoder_rel, decoder_twice, numbers, gains = small
    decoder_slots = gather_tokens(after(decoder_blocks, encoder_g, small))


    encoder_r1, encoder_c, *encoder_stored = attention_forward(
        "encoder",
        after(place_in, encoder_g),
        encoder_input,
        prefix,
        gains,
        encoder_rel,
        encoder_weights,
    )
    decoder_weights = gather_blocks(jnp.stack(after(decoder_slots, encoder_r1)))
    encoder_c = gather_tokens(encoder_c)
    c_all, g_all, h, du, dc_own, dc_rest = ffn_first(
        "encoder_ffn", encoder_c, encoder_g, encoder_widen, encoder_narrow
    )
    encoder_dc = (dc_own, return_tokens(dc_rest))
    out, *grads = ffn_second(
        "encoder_ffn", None, after(place_in, encoder_dc[1][0]), c_all, g_all, h, du, encoder_narrow
    )
    encoder_out = lax.psum_scatter(out, "mp", scatter_dimension=0, tiled=True)
    decoder_g = gather_tokens(after(decoder_upstream, encoder_dc, out))
    (
        encoder_input_grad,
        encoder_gain_grad,
        keep,
        send,
        encoder_later_grad,
        prefix_grad,
        encoder_bias_raw,
    ) = attention_backward(
        "encoder",
        after(place_in, out),
        (*encoder_dc, encoder_r1),
        encoder_upstream,
        encoder_input,
        gains,
        encoder_stored,
        None,
        encoder_weights,
        encoder_rel,
        encoder_twice,
        encoder_bias.shape[0],
        grads,
    )
    encoder_got = swap_cores(after(send, decoder_g))
    packed = jnp.concatenate([prefix_grad[:prefix_rows], numbers])

    self_r1, _, *self_stored = attention_forward(
        "self", after(place_in, encoder_input_grad), decoder_input, None, gains, decoder_rel, decoder_weights
    )
    encoder_halves = fold_cores(after(keep, self_r1), encoder_got)
    encoder_once = send_once(encoder_halves)
    cross_r2, decoder_c, *cross_stored = attention_forward(
        "cross", after(place_in, encoder_halves), self_r1, encoder_states, gains, None, decoder_weights
    )
    decoder_c = gather_tokens(decoder_c)
    c_all, g_all, h, du, dc_own, dc_rest = ffn_first(
        "decoder_ffn",
        [after(decoder_c[0], encoder_out), *decoder_c[1:]],
        decoder_g,
        decoder_widen,
        decoder_narrow,
    )
    decoder_dc = (dc_own, return_tokens(dc_rest))
    encoder_last = fold_once(after(encoder_halves, decoder_dc[1][0]), encoder_once)
    encoder_twice_got = send_twice(encoder_last)
    out, *rest, keep, send = ffn_second(
        "decoder_ffn", packed, after(place_in, encoder_last), c_all, g_all, h, du, decoder_narrow
    )
    grads = [keep, send]

    decoder_out = [to_mp(part, i + 1) for i, part in enumerate(after(rest, decoder_dc))]

    cross_dx, cross_gain_grad, keep, send, decoder_later_grad, states_grad = attention_backward(
        "cross",
        after(place_in, encoder_twice_got),
        (*decoder_dc, cross_r2),
        decoder_upstream,
        self_r1,
        gains,
        cross_stored,
        encoder_states,
        decoder_weights,
        None,
        None,
        None,
        grads,
    )
    cross_got = swap_cores(after(send, decoder_out))
    encoder_sums = fold_twice(
        after(encoder_halves, cross_dx), encoder_once, encoder_twice_got
    )
    cross_halves = fold_cores(keep, after(cross_got, encoder_sums))
    cross_once = send_once(cross_halves)
    encoder_sent = send_slots(after(encoder_sums, cross_halves))
    tokens = cross_r2.shape[0]
    used = jnp.stack([packed] + [part[tokens:] for part in decoder_out])
    used = lax.all_gather(used, "dp", axis=0, tiled=False).reshape(-1, *packed.shape)
    decoder_input_grad, decoder_gain_grad, keep, send, decoder_bias_raw = attention_backward(
        "self",
        after(place_in, cross_halves),
        None,
        cross_dx,
        decoder_input,
        gains,
        self_stored,
        None,
        decoder_weights,
        decoder_rel,
        decoder_twice,
        decoder_bias.shape[0],
        None,
    )
    self_got = swap_cores(after(send, cross_once, encoder_sent))
    cross_last = fold_once(after(cross_halves, decoder_input_grad), cross_once)
    cross_twice_got = send_twice(cross_last)
    sums = call(
        pack_kernel,
        "pack",
        [
            place_in,
            encoder_gain_grad,
            encoder_later_grad,
            decoder_gain_grad,
            cross_gain_grad,
            decoder_later_grad,
            encoder_bias_raw,
            decoder_bias_raw,
        ],
        (0,),
        (),
        [((64, 128), f32)],
        [],
    )[0]
    self_halves = fold_cores(keep, after(self_got, sums, cross_last))
    self_once = send_once(self_halves)
    cross_sums = fold_twice(after(cross_halves, self_halves), cross_once, cross_twice_got)
    cross_sent = send_slots(cross_sums)
    sums = sum_bits("mp", after(sums, cross_sent), 1, lax.axis_size("mp"))
    self_last = fold_once(after(self_halves, cross_sums), self_once)
    self_twice_got = send_twice(self_last)
    self_sums = fold_twice(after(self_halves, sums, cross_sent), self_once, self_twice_got)
    self_sent = send_slots(self_sums)
    sums = sum_bits("dp", after(sums, self_sent[0]), 1, lax.axis_size("dp"))

    def last(value):
        return after(value, self_sums)

    cross_mats = four_matrices(last(cross_sums), cross_sent)
    encoder_mats = four_matrices(last(encoder_sums), encoder_sent)
    encoder_output = (last(encoder_r1) + encoder_out.astype(f32)).astype(bf16)
    encoder_widen_grad, encoder_narrow_grad = two_matrices(*last(encoder_sums[4:]))
    table_rows = memory_table.shape[0] // (lax.axis_size("dp") * lax.axis_size("mp"))
    table_grad = call(
        functools.partial(table_kernel, prefix_rows),
        "table",
        [last(place_in), last(used)],
        (0,),
        (),
        [((table_rows, PREFIX, width), f32)],
        [],
    )[0]
    decoder_output = (
        last(cross_r2) + out + sum(part[:tokens].astype(f32) for part in decoder_out)
    ).astype(bf16)
    decoder_widen_grad, decoder_narrow_grad = two_matrices(*last(cross_sums[4:]))
    self_mats = four_matrices(self_sums, self_sent)

    gain_sums = [sums[32 + 6 * i : 38 + 6 * i].reshape(-1) for i in range(5)]
    buckets, heads = encoder_bias.shape
    bias_grads = [sums[:buckets, i * heads : (i + 1) * heads] for i in range(2)]
    return (
        encoder_output,
        encoder_input_grad,
        table_grad,
        bias_grads[0],
        gain_sums[0],
        *encoder_mats,
        gain_sums[1],
        encoder_widen_grad,
        encoder_narrow_grad,
        decoder_output,
        decoder_input_grad,
        states_grad,
        bias_grads[1],
        gain_sums[2],
        *self_mats,
        gain_sums[3],
        *cross_mats,
        gain_sums[4],
        decoder_widen_grad,
        decoder_narrow_grad,
    )


def solution(mesh):
    rows = P(("dp", "mp"), None)
    columns = P(None, "mp")
    lines = P("mp", None)
    attention = (columns, columns, columns, lines)
    in_specs = (
        (rows, rows, P("dp", None), P(), P(), P(), P())
        + attention
        + (P(), columns, lines, rows, rows, rows, P(), P(), P())
        + attention
        + (P(),)
        + attention
        + (P(), columns, lines)
    )
    both = P("dp", "mp")
    turned = P("mp", "dp")
    grads = (both, both, both, turned)
    out_specs = (
        (rows, rows, P(("dp", "mp"), None, None), P(), P())
        + grads
        + (P(), both, turned, rows, rows, rows, P(), P())
        + grads
        + (P(),)
        + grads
        + (P(), both, turned)
    )
    return jax.shard_map(shards, mesh=mesh, in_specs=in_specs, out_specs=out_specs, check_vma=False)
```

```python
import functools

import jax
import jax.numpy as jnp
from jax import lax
from jax.experimental import pallas as pl
from jax.experimental.pallas import tpu as pltpu
from jax.sharding import PartitionSpec as P

DH = 64
SEQ = 64
MEMK = 10
PREFIX = 2
EPS = 1e-06
NEG = -1e30
BLOCKS = 8
bf16 = jnp.bfloat16
f32 = jnp.float32


def nn(left, right):
    return lax.dot_general(left, right, (((1,), (0,)), ((), ())), preferred_element_type=f32)


def nt(left, right):
    return lax.dot_general(left, right, (((1,), (1,)), ((), ())), preferred_element_type=f32)


def tn(left, right):
    return lax.dot_general(left, right, (((0,), (0,)), ((), ())), preferred_element_type=f32)


def from_mp(array, step):
    size = lax.axis_size("mp")
    return lax.ppermute(array, "mp", [(i, (i - step) % size) for i in range(size)])


def to_mp(array, step):
    size = lax.axis_size("mp")
    return lax.ppermute(array, "mp", [(i, (i + step) % size) for i in range(size)])


def swap_dp(array, bit):
    return lax.ppermute(array, "dp", [(i, i ^ bit) for i in range(lax.axis_size("dp"))])


def after(value, *earlier):
    leaves, shape = jax.tree.flatten(value)
    tied = lax.optimization_barrier((*leaves, *jax.tree.leaves(earlier)))
    return jax.tree.unflatten(shape, tied[: len(leaves)])


def high_bits():
    low = lax.axis_size("dp") // BLOCKS
    return low, 2 * low, 4 * low


def rounded_sum(left, right):
    return (left.astype(f32) + right.astype(f32)).astype(bf16)


def swap_cores(array):
    return swap_dp(array, high_bits()[0])


def fold_cores(keep, got):
    return tuple(
        (rounded_sum(keep[i, :2], got[i, :2]), rounded_sum(keep[i, 2:], got[i, 2:])) for i in range(2)
    )


def send_once(halves):
    core, along, across = high_bits()
    return swap_dp(halves[0][1], along), swap_dp(halves[1][1], across)


def fold_once(halves, got):
    return tuple(rounded_sum(halves[i][0][1], got[i][1]) for i in range(2))


def send_twice(last):
    core, along, across = high_bits()
    return swap_dp(last[0], across), swap_dp(last[1], along)


def fold_twice(halves, got, last_got):
    sums = [
        halves[i][0][0].astype(f32) + got[i][0].astype(f32) + last_got[i].astype(f32) for i in range(2)
    ]
    return [sums[0][0], sums[0][1], sums[1][0], sums[1][1]] + [part[i] for i in range(2, sums[0].shape[0]) for part in sums]


def send_slots(slots):
    return [to_mp(slots[step].astype(bf16), step) for step in range(1, 4)]


def scatter_rest(rows):
    size = lax.axis_size("dp")
    low = size // BLOCKS
    if low == 1:
        return rows
    groups = [[high * low + i for i in range(low)] for high in range(BLOCKS)]
    return lax.psum_scatter(
        rows, "dp", scatter_dimension=0, axis_index_groups=groups, tiled=True
    )


def four_matrices(slots, got):
    total = slots[0]
    if lax.axis_size("dp") == BLOCKS:
        rows, width = total.shape
        part = width // 4
        return call(
            finish_kernel,
            "matrices",
            [total, *got],
            (),
            (),
            [((rows, part), f32)] * 3 + [((part, rows), f32)],
            [],
        )
    for other in got:
        total = total + other.astype(f32)
    total = scatter_rest(total)
    width = total.shape[1] // 4
    parts = [total[:, i * width : (i + 1) * width] for i in range(4)]
    return parts[0], parts[1], parts[2], parts[3].T


def two_matrices(widen, narrow):
    return scatter_rest(widen), scatter_rest(narrow).T


def gather_blocks(slots):
    low = lax.axis_size("dp") // BLOCKS
    groups = [[high * low + i for high in range(BLOCKS)] for i in range(low)]
    if low == 1:
        groups = None
    return lax.all_gather(slots, "dp", axis=0, axis_index_groups=groups, tiled=False)


def sum_bits(axis, array, bit, end):
    size = lax.axis_size(axis)
    while bit < end:
        array = array + lax.ppermute(array, axis, [(i, i ^ bit) for i in range(size)])
        bit *= 2
    return array


def fetch_weights(weights, group, held, sems, order):
    copies = {}
    for i, what in enumerate(order):
        blocks = pl.ds(6, 2) if what == "merge" else pl.ds(0, 6)
        for slot in range(4):
            copies[what, slot] = pltpu.make_async_copy(
                weights.at[blocks, slot, group], held.at[slot, blocks], sems.at[slot, i]
            )
            copies[what, slot].start()
    return copies


def slot_rows(held, slot, first, last):
    part = held[slot, 2 * first : 2 * last]
    return part.reshape(part.shape[0] * part.shape[1], part.shape[2])


def wait_all(copies):
    for copy in copies:
        copy.wait()


def blocks_kernel(groups, place_ref, *refs):
    inputs = refs[: 4 * groups]
    first, others, sems = refs[4 * groups :]
    outs = [first] + [others.at[i] for i in range(groups - 1)]
    size = first.shape[0]
    place = place_ref[0]
    start = pl.multiple_of((place % 2) * size, size)
    for j in range(4):

        @pl.when(place // 2 == j)
        def _():
            copies = [
                pltpu.make_async_copy(inputs[4 * i + j].at[pl.ds(start, size)], outs[i], sems.at[i])
                for i in range(groups)
            ]
            for copy in copies:
                copy.start()
            wait_all(copies)


def inverse_rms(rows):
    return lax.rsqrt(jnp.mean(rows * rows, axis=-1, keepdims=True) + EPS)


def gain_rows(kind, gains_ref):
    at = {"encoder": (0, 1), "self": (2, 3), "cross": (3, 4)}[kind]
    return tuple(gains_ref[i : i + 1, :] for i in at)


def column_head(shape):
    return lax.broadcasted_iota(jnp.int32, shape, 1) // DH


def softmax_rows(scores):
    shifted = jnp.exp(scores - jnp.max(scores, axis=-1, keepdims=True))
    return shifted / jnp.sum(shifted, axis=-1, keepdims=True)


def masks(kind, rows, keys):
    row = lax.broadcasted_iota(jnp.int32, (rows, rows), 0)
    col = lax.broadcasted_iota(jnp.int32, (rows, rows), 1)
    same = row // SEQ == col // SEQ
    if kind == "self":
        same = jnp.logical_and(same, col <= row)
    if kind != "encoder":
        return same, None
    row = lax.broadcasted_iota(jnp.int32, (rows, keys - rows), 0)
    col = lax.broadcasted_iota(jnp.int32, (rows, keys - rows), 1)
    first = (row // SEQ) * (MEMK * PREFIX)
    valid = jnp.logical_and(col >= first, col < first + MEMK * PREFIX)
    return same, jnp.where(valid, 0.0, NEG)


def add_bias(kind, scores, rel_ref, slot, same, before):
    rows = scores.shape[0] // 3
    parts = []
    for j in range(3):
        part = scores[j * rows : (j + 1) * rows]
        own = part[:, :rows]
        if kind != "cross":
            rel = rel_ref[3 * slot + j]
            own = own + jnp.concatenate([rel] * (rows // SEQ), axis=0)
        own = jnp.where(same, own, NEG)
        if before is not None:
            own = jnp.concatenate([own, part[:, rows:] + before], axis=1)
        parts.append(own)
    return jnp.concatenate(parts, axis=0)


def stack_heads(array):
    head = column_head(array.shape)
    return jnp.concatenate([jnp.where(head == j, array, jnp.zeros_like(array)) for j in range(3)], axis=0)


def join_heads(stacked):
    rows = stacked.shape[0] // 3
    head = column_head((rows, stacked.shape[1]))
    return jnp.where(
        head == 0,
        stacked[:rows],
        jnp.where(head == 1, stacked[rows : 2 * rows], stacked[2 * rows :]),
    )


def attention_forward_kernel(kind, *refs):
    refs = list(refs)
    place_ref, x_ref = refs[:2]
    del refs[:2]
    pre_ref = refs.pop(0) if kind != "self" else None
    gains_ref = refs.pop(0)
    gain, later = gain_rows(kind, gains_ref)
    rel_ref = refs.pop(0) if kind != "cross" else None
    weights, r1_ref, next_ref, a_ref, q_ref, kv_ref, o_ref, held, sems = refs
    copies = fetch_weights(weights, int(kind == "cross"), held, sems, ("rest", "merge"))
    r = x_ref[...].astype(f32)
    rows = r.shape[0]
    a = (r * inverse_rms(r) * gain).astype(bf16)
    if kind == "encoder":
        a_ref[0:rows, :] = a
        a_ref[rows:, :] = pre_ref[...]
        a_all = a_ref[...]
    else:
        a_ref[...] = a
        a_all = a
    keys = kv_ref.shape[1]
    same, before = masks(kind, rows, keys)
    queries = []
    sources = []
    for slot in range(4):
        copies["rest", slot].wait()
        if kind == "cross":
            q = nt(a, slot_rows(held, slot, 0, 1)).astype(bf16)
            kv = nt(pre_ref[...], slot_rows(held, slot, 1, 3)).astype(bf16)
        else:
            qkv = nt(a_all, slot_rows(held, slot, 0, 3)).astype(bf16)
            q = qkv[:rows, :192]
            kv = qkv[:, 192:]
        q_ref[slot] = q
        kv_ref[slot] = kv
        queries.append(q)
        sources.append(kv)
    chances = []
    for slot in range(4):
        scores = nt(stack_heads(queries[slot]), sources[slot][:, :192])
        chances.append(softmax_rows(add_bias(kind, scores, rel_ref, slot, same, before)).astype(bf16))
    mixed = []
    for slot in range(4):
        o = join_heads(nn(chances[slot], sources[slot][:, 192:])).astype(bf16)
        o_ref[slot] = o
        mixed.append(o)
    acc = r
    for slot in range(4):
        copies["merge", slot].wait()
        acc = acc + nn(mixed[slot], slot_rows(held, slot, 3, 4))
    r1_ref[...] = acc
    next_ref[...] = (acc * inverse_rms(acc) * later).astype(bf16)


def norm_back(dn, r, gain, dgain_ref):
    t = inverse_rms(r)
    dgain_ref[...] = jnp.sum(dn * r * t, axis=0, keepdims=True)
    scaled = dn * gain
    return t * (scaled - r * (t * t) * jnp.mean(scaled * r, axis=-1, keepdims=True))


def attention_backward_kernel(kind, after_ffn, *refs):
    refs = list(refs)
    place_ref = refs.pop(0)
    place = place_ref[0]
    if after_ffn:
        dc_own, *dc_rest = refs[:4]
        up_ref, r1_ref = refs[4:6]
        refs = refs[6:]
    else:
        up_ref = refs.pop(0)
    x_ref, gains_ref, a_ref = refs[:3]
    gain, later = gain_rows(kind, gains_ref)
    refs = refs[3:]
    source_ref = refs.pop(0) if kind == "cross" else None
    q_ref, kv_ref, o_ref = refs[:3]
    weights = refs[3]
    refs = refs[4:]
    rel_ref, bucket_ref = (refs.pop(0), refs.pop(0)) if kind != "cross" else (None, None)
    if kind != "self":
        refs = refs[2:]
    dx_ref, dgain_ref = refs[:2]
    refs = refs[2:]
    keep_ref, send_ref = refs.pop(0), refs.pop(0)
    later_grad = refs.pop(0) if after_ffn else None
    if kind == "encoder":
        dpre_ref = refs.pop(0)
    elif kind == "cross":
        dsource_ref = refs.pop(0)
    bias_grad = refs.pop(0) if kind != "cross" else None
    held, sems, left, right = refs[:4]
    refs = refs[4:]
    ds_sum = refs.pop(0) if kind != "cross" else None
    stage, out_sems = refs
    copies = fetch_weights(weights, int(kind == "cross"), held, sems, ("merge", "rest"))

    d_out = up_ref[...].astype(f32)
    if after_ffn:
        dn = dc_own[...]
        for part in dc_rest:
            dn = dn + part[...].astype(f32)
        d_out = d_out + norm_back(dn, r1_ref[...], later, later_grad)
    g = d_out.astype(bf16)
    rows, width = g.shape
    keys = kv_ref.shape[1]
    stacked = [a_ref[...]] + ([source_ref[...]] if kind == "cross" else []) + [g]
    turned = jnp.concatenate(stacked, axis=0).T
    size = width // BLOCKS
    for d in range(BLOCKS):
        away = place ^ d
        at = pl.multiple_of(((away % 2) * 4 + away // 2) * size, size)
        left[pl.ds(at, size), :] = turned[d * size : (d + 1) * size]
    source_at = rows if kind == "cross" else 0
    g_at = left.shape[1] - rows
    right[...] = jnp.zeros(right.shape, bf16)
    same, before = masks(kind, rows, keys)
    grads = []
    for slot in range(4):
        copies["merge", slot].wait()
        grads.append(nt(g, slot_rows(held, slot, 3, 4)).astype(bf16))
        right[slot, g_at:, 576:768] = o_ref[slot]
    chances = []
    for slot in range(4):
        scores = nt(stack_heads(q_ref[slot]), kv_ref[slot][:, :192])
        chances.append(softmax_rows(add_bias(kind, scores, rel_ref, slot, same, before)))
    d_scores = []
    for slot in range(4):
        p = chances[slot]
        do_heads = stack_heads(grads[slot])
        dv = tn(p.astype(bf16), do_heads).astype(bf16)
        right[slot, source_at : source_at + keys, 384:576] = dv
        dp = nt(do_heads, kv_ref[slot][:, 192:])
        ds = (p * (dp - jnp.sum(dp * p, axis=-1, keepdims=True))).astype(bf16)
        d_scores.append(ds)
    for slot in range(4):
        ds = d_scores[slot]
        right[slot, 0:rows, 0:192] = join_heads(nn(ds, kv_ref[slot][:, :192])).astype(bf16)
        right[slot, source_at : source_at + keys, 192:384] = tn(ds, stack_heads(q_ref[slot])).astype(bf16)
        if kind != "cross":
            for j in range(3):
                wide = ds[j * rows : (j + 1) * rows, :rows].astype(f32)
                ds_sum[3 * slot + j] = wide[:SEQ] + wide[SEQ:]
    outgoing = []
    for slot in range(4):
        grad = nn(left[...], right[slot]).astype(bf16)
        for j in range(BLOCKS):
            to = (j // 4) * 4 + ((j % 2) * 2 + (j % 4) // 2 if slot // 2 == 0 else j % 4)
            stage[slot, to] = grad[j * size : (j + 1) * size]
        for i, out in enumerate((keep_ref, send_ref)):
            copy = pltpu.make_async_copy(
                stage.at[slot, pl.ds(4 * i, 4)], out.at[slot // 2, :, slot % 2], out_sems.at[slot, i]
            )
            copy.start()
            outgoing.append(copy)
    total = None
    source_total = None
    for slot in range(4):
        copies["rest", slot].wait()
        if kind == "cross":
            part = nn(right[slot, 0:rows, 0:192], slot_rows(held, slot, 0, 1))
            other = nn(right[slot, rows : rows + keys, 192:576], slot_rows(held, slot, 1, 3))
            source_total = other if slot == 0 else source_total + other
        else:
            part = nn(right[slot, 0:keys, 0:576], slot_rows(held, slot, 0, 3))
        total = part if slot == 0 else total + part
    if kind == "cross":
        dsource_ref[...] = source_total
    if kind == "encoder":
        dpre_ref[...] = total[rows:].astype(bf16)
    dx_ref[...] = d_out + norm_back(total[:rows], x_ref[...].astype(f32), gain, dgain_ref)
    if kind != "cross":
        bucket = bucket_ref[...]
        heads, buckets = bias_grad.shape[:2]

        @pl.loop(0, buckets)
        def _(b):
            chosen = bucket == b
            for head in range(heads):
                part = jnp.where(chosen, ds_sum[head], 0.0)
                bias_grad[head, b] = jnp.sum(part.reshape(SEQ // 8, 8, 2 * SEQ), axis=0)

    wait_all(outgoing)


def ffn_first_kernel(c0, c1, c2, c3, g0, g1, g2, g3, widen, narrow, c_all, g_all, h_ref, du_ref, dc_own, dc_rest):
    tokens = c0.shape[0]
    for i, (c, g) in enumerate(((c0, g0), (c1, g1), (c2, g2), (c3, g3))):
        c_all[i * tokens : (i + 1) * tokens, :] = c[...]
        g_all[i * tokens : (i + 1) * tokens, :] = g[...]
    inner = 0.7978845608028654
    for n in range(widen.shape[1] // 256):
        at = slice(n * 256, (n + 1) * 256)
        u = nn(c_all[...], widen[:, at])
        u2 = u * u
        th = jnp.tanh(inner * (u + 0.044715 * u * u2))
        h_ref[:, at] = (0.5 * u * (1.0 + th)).astype(bf16)
        slope = 0.5 * (1.0 + th) + (0.5 * inner) * u * (1.0 - th * th) * (1.0 + 3 * 0.044715 * u2)
        dh = nt(g_all[...], narrow[at, :])
        du_ref[:, at] = (dh * slope).astype(bf16)
    for n in range(widen.shape[0] // 256):
        at = slice(n * 256, (n + 1) * 256)
        dc = nt(du_ref[...], widen[at, :])
        dc_own[:, at] = dc[:tokens]
        for i in range(3):
            dc_rest[i, :, at] = dc[(i + 1) * tokens : (i + 2) * tokens].astype(bf16)


def ffn_second_kernel(across, place_ref, c_all, g_all, h_ref, du_ref, narrow, *refs):
    outs = refs[:-4]
    keep_ref, send_ref, stage, sems = refs[-4:]
    tokens = c_all.shape[0] // 4
    if not across:
        packed, *outs = outs
        for out in outs[1:]:
            out[tokens:, :] = packed[...]
    place = place_ref[0]
    copies = []
    for half, (left, right) in enumerate(((c_all, du_ref), (g_all, h_ref))):
        grad = tn(left[...], right[...]).astype(bf16)
        size = grad.shape[0] // BLOCKS
        for d in range(BLOCKS):
            away = place ^ d
            where = away // 2
            if half == 0:
                where = (where % 2) * 2 + where // 2
            stage[half, (away % 2) * 4 + where] = grad[d * size : (d + 1) * size]
        for i, ref in enumerate((keep_ref, send_ref)):
            copy = pltpu.make_async_copy(
                stage.at[half, pl.ds(4 * i, 4)], ref.at[half, :, 2], sems.at[half, i]
            )
            copy.start()
            copies.append(copy)
    for n in range(narrow.shape[1] // 256):
        at = slice(n * 256, (n + 1) * 256)
        out = nn(h_ref[...], narrow[:, at])
        for i in range(4):
            part = out[i * tokens : (i + 1) * tokens]
            if across:
                row = pl.multiple_of((place_ref[1] + i) % 4 * tokens, tokens)
                outs[0][pl.ds(row, tokens), at] = part.astype(bf16)
            else:
                outs[i][0:tokens, at] = part.astype(outs[i].dtype)
    wait_all(copies)


def gains_kernel(*refs):
    for i in range(5):
        refs[5][i : i + 1, :] = refs[i][...].reshape(1, -1)


def finish_kernel(total_ref, got1, got2, got3, query, key, value, merge):
    total = total_ref[...]
    for got in (got1, got2, got3):
        total = total + got[...].astype(f32)
    width = query.shape[1]
    for i, out in enumerate((query, key, value)):
        out[...] = total[:, i * width : (i + 1) * width]
    merge[...] = total[:, 3 * width :].T


def table_kernel(rows, place_ref, used_ref, out_ref):
    entries = out_ref.shape[0]
    size = used_ref.shape[1]
    first = (place_ref[2] * entries).astype(f32)
    row = lax.broadcasted_iota(jnp.int32, (PREFIX * entries, size), 0)
    column = lax.broadcasted_iota(jnp.int32, (PREFIX * entries, size), 1)
    wanted = (row % entries).astype(f32) + first
    fits = jnp.logical_and(column % PREFIX == row // entries, column < rows)
    total = jnp.zeros((PREFIX * entries, used_ref.shape[2]), f32)
    for i in range(used_ref.shape[0]):
        number = used_ref[i, :, 0:128].astype(f32)
        entry = number[rows : rows + 1, :size] * 32.0 + number[rows + 1 : rows + 2, :size]
        chosen = jnp.logical_and(entry == wanted, fits)
        total = total + nn(jnp.where(chosen, 1.0, 0.0).astype(bf16), used_ref[i])
    for p in range(PREFIX):
        out_ref[:, p, :] = total[p * entries : (p + 1) * entries]


def pack_kernel(place_ref, *refs):
    out = refs[7]
    out[...] = jnp.zeros(out.shape, f32)
    for i in range(2):
        raw = refs[5 + i]
        heads, buckets = raw.shape[:2]
        sums = jnp.sum(jnp.sum(raw[...], axis=2), axis=-1)
        here = lax.broadcasted_iota(jnp.int32, (heads, 128), 0)
        column = lax.broadcasted_iota(jnp.int32, (heads, 128), 1)
        target = (here + place_ref[1] * (heads // 4)) % heads + i * heads
        turn = jnp.where(column == target, 1.0, 0.0)
        out[0:buckets, :] += lax.dot_general(
            sums,
            turn,
            (((0,), (0,)), ((), ())),
            precision=lax.Precision.HIGHEST,
            preferred_element_type=f32,
        )
    for i in range(5):
        for j in range(6):
            out[32 + 6 * i + j : 33 + 6 * i + j, :] = refs[i][:, 128 * j : 128 * (j + 1)]


def call(kernel, name, operands, smem, hbm, outs, scratch, limit=28, hbm_outs=(), aliases=None):
    specs = []
    for i in range(len(operands)):
        if i in smem:
            specs.append(pl.BlockSpec(memory_space=pltpu.SMEM))
        elif i in hbm:
            specs.append(pl.BlockSpec(memory_space=pl.ANY))
        else:
            specs.append(pl.BlockSpec(memory_space=pltpu.VMEM))
    return pl.pallas_call(
        kernel,
        out_shape=[jax.ShapeDtypeStruct(shape, kind) for shape, kind in outs],
        in_specs=specs,
        out_specs=[
            pl.BlockSpec(memory_space=pl.ANY if i in hbm_outs else pltpu.VMEM)
            for i in range(len(outs))
        ],
        scratch_shapes=scratch,
        input_output_aliases=aliases or {},
        compiler_params=pltpu.CompilerParams(vmem_limit_bytes=limit * 1024 * 1024),
        cost_estimate=pl.CostEstimate(flops=0, bytes_accessed=1024, transcendentals=0),
        name=name,
    )(*operands)


def weight_blocks(place, groups):
    count = len(groups)
    operands = [place]
    for query, key, value, merge in groups:
        operands += [query.T, key.T, value.T, merge]
    columns, rows = operands[1].shape
    return call(
        functools.partial(blocks_kernel, count),
        "weight_blocks",
        operands,
        (0,),
        range(1, len(operands)),
        [
            ((4 * columns // BLOCKS, rows), bf16),
            ((count - 1, 4 * columns // BLOCKS, rows), bf16),
        ],
        [pltpu.SemaphoreType.DMA((count,))],
        60,
    )


def attention_forward(kind, place, x, extra, gains, rel, weights):
    rows, width = x.shape
    extra_rows = extra.shape[0] if kind == "encoder" else 0
    keys = rows + extra_rows
    operands = [place, x]
    if extra is not None:
        operands.append(extra)
    operands.append(gains)
    if rel is not None:
        operands.append(rel)
    hbm = (len(operands),)
    operands.append(weights)
    return call(
        functools.partial(attention_forward_kernel, kind),
        kind + "_forward",
        operands,
        (0,),
        hbm,
        [
            ((rows, width), f32),
            ((rows, width), bf16),
            ((keys, width), bf16),
            ((4, rows, 192), bf16),
            ((4, keys, 384), bf16),
            ((4, rows, 192), bf16),
        ],
        [pltpu.VMEM((4, BLOCKS, width // BLOCKS, width), bf16), pltpu.SemaphoreType.DMA((4, 2))],
        56,
    )


def attention_backward(
    kind, place, ffn, upstream, x, gains, stored, source, weights, rel, bucket, buckets, grads
):
    rows, width = upstream.shape
    a, q, kv, o = stored
    keys = kv.shape[1]
    operands = [place]
    if ffn is not None:
        dc_own, dc_rest, r1 = ffn
        operands += [dc_own, *dc_rest, upstream, r1]
    else:
        operands += [upstream]
    operands += [x, gains, a]
    if source is not None:
        operands.append(source)
    operands += [q, kv, o]
    hbm = (len(operands),)
    operands.append(weights)
    if kind != "cross":
        operands += [rel, bucket]
    aliases = None
    if grads is not None:
        hbm += (len(operands), len(operands) + 1)
        aliases = {len(operands): 2, len(operands) + 1: 3}
        operands += grads
    block = width // BLOCKS
    outs = [
        ((rows, width), f32),
        ((1, width), f32),
    ]
    outs += [((2, 4, 2 if grads is None else 3, block, width), bf16)] * 2
    if ffn is not None:
        outs.append(((1, width), f32))
    if kind == "encoder":
        outs.append(((keys - rows, width), bf16))
    elif kind == "cross":
        outs.append(((rows, width), f32))
    if kind != "cross":
        outs.append(((rel.shape[0], buckets, 8, 2 * SEQ), f32))
    depth = 2 * rows + (keys if kind == "cross" else keys - rows)
    scratch = [
        pltpu.VMEM((4, BLOCKS, block, width), bf16),
        pltpu.SemaphoreType.DMA((4, 2)),
        pltpu.VMEM((width, depth), bf16),
        pltpu.VMEM((4, depth, width), bf16),
    ]
    if kind != "cross":
        scratch.append(pltpu.VMEM((rel.shape[0], SEQ, 2 * SEQ), f32))
    scratch += [pltpu.VMEM((4, BLOCKS, block, width), bf16), pltpu.SemaphoreType.DMA((4, 2))]
    return call(
        functools.partial(attention_backward_kernel, kind, ffn is not None),
        kind + "_backward",
        operands,
        (0,),
        hbm,
        outs,
        scratch,
        56,
        (2, 3),
        aliases,
    )


def ffn_first(name, c_parts, g_parts, widen, narrow):
    tokens, width = c_parts[0].shape
    hidden = widen.shape[1]
    every = 4 * tokens
    return call(
        ffn_first_kernel,
        name + "_first",
        [*c_parts, *g_parts, widen, narrow],
        (),
        (),
        [
            ((every, width), bf16),
            ((every, width), bf16),
            ((every, hidden), bf16),
            ((every, hidden), bf16),
            ((tokens, width), f32),
            ((3, tokens, width), bf16),
        ],
        [],
    )


def ffn_second(name, packed, place, c_all, g_all, h, du, narrow):
    every, width = c_all.shape
    hidden = h.shape[1]
    tokens = every // 4
    block = width // BLOCKS
    across = packed is None
    operands = [place, c_all, g_all, h, du, narrow]
    if across:
        outs = [((every, width), bf16)]
    else:
        operands.append(packed)
        outs = [((tokens, width), f32)] + [((tokens + packed.shape[0], width), bf16)] * 3
    count = len(outs)
    return call(
        functools.partial(ffn_second_kernel, across),
        name + "_second",
        operands,
        (0,),
        (),
        outs + [((2, 4, 3, block, hidden), bf16)] * 2,
        [pltpu.VMEM((2, BLOCKS, block, hidden), bf16), pltpu.SemaphoreType.DMA((2, 2))],
        28,
        (count, count + 1),
    )


def gather_tokens(part):
    return [part] + [from_mp(part, step) for step in range(1, 4)]


def return_tokens(rest):
    return [to_mp(rest[step - 1], step) for step in range(1, 4)]


def relative_bias(bucket, table, heads_here):
    twice = jnp.concatenate([bucket, bucket], axis=1)
    onehot = (
        lax.broadcasted_iota(jnp.int32, (table.shape[0], 1), 0) == twice.reshape(1, -1)
    ).astype(f32)
    start = lax.axis_index("mp") * heads_here
    columns = jnp.concatenate([table.T, table.T], axis=0)
    ordered = lax.dynamic_slice_in_dim(columns, start, table.shape[1], 0)
    looked = jnp.dot(ordered, onehot, precision=lax.Precision.HIGHEST)
    return looked.reshape(table.shape[1], SEQ, 2 * SEQ), twice


def shards(
    encoder_input,
    encoder_upstream,
    memory_index,
    memory_table,
    encoder_bucket,
    encoder_bias,
    encoder_gain,
    encoder_query,
    encoder_key,
    encoder_value,
    encoder_merge,
    encoder_later_gain,
    encoder_widen,
    encoder_narrow,
    decoder_input,
    decoder_upstream,
    encoder_states,
    decoder_bucket,
    decoder_bias,
    decoder_gain,
    decoder_query,
    decoder_key,
    decoder_value,
    decoder_merge,
    cross_gain,
    cross_query,
    cross_key,
    cross_value,
    cross_merge,
    decoder_later_gain,
    decoder_widen,
    decoder_narrow,
):
    heads_here = encoder_query.shape[1] // DH
    width = encoder_input.shape[1]
    dp_at = lax.axis_index("dp")
    mp_at = lax.axis_index("mp")
    place = dp_at // (lax.axis_size("dp") // BLOCKS)
    place_in = jnp.stack([place, mp_at, dp_at * lax.axis_size("mp") + mp_at]).astype(jnp.int32)

    encoder_block, decoder_blocks = weight_blocks(
        place_in,
        [
            (encoder_query, encoder_key, encoder_value, encoder_merge),
            (decoder_query, decoder_key, decoder_value, decoder_merge),
            (cross_query, cross_key, cross_value, cross_merge),
        ],
    )
    encoder_slots = jnp.stack(gather_tokens(encoder_block))[:, None]
    encoder_weights = gather_blocks(encoder_slots)
    encoder_g = gather_tokens(after(encoder_upstream, encoder_slots))

    own_questions = memory_index.shape[0] // lax.axis_size("mp")
    entries = lax.dynamic_slice_in_dim(
        memory_index, mp_at * own_questions, own_questions, 0
    ).reshape(-1)
    prefix = jnp.take(memory_table, entries, axis=0).reshape(-1, width)
    prefix_rows = prefix.shape[0]
    prefix = jnp.pad(prefix, ((0, -prefix_rows % 64), (0, 0)))
    encoder_rel, encoder_twice = relative_bias(encoder_bucket, encoder_bias, heads_here)
    decoder_rel, decoder_twice = relative_bias(decoder_bucket, decoder_bias, heads_here)
    entry_rows = jnp.repeat(entries, PREFIX)
    numbers = jnp.stack([entry_rows // 32, entry_rows % 32]).astype(bf16)
    numbers = jnp.pad(numbers, ((0, -(prefix_rows + 2) % 16), (0, width - prefix_rows)))
    gains = call(
        gains_kernel,
        "gains",
        [encoder_gain, encoder_later_gain, decoder_gain, cross_gain, decoder_later_gain],
        (),
        (),
        [((5, width), f32)],
        [],
    )[0]
    small = (prefix, encoder_rel, encoder_twice, decoder_rel, decoder_twice, numbers, gains)
    small = after(small, encoder_block)
    prefix, encoder_rel, encoder_twice, decoder_rel, decoder_twice, numbers, gains = small
    decoder_slots = gather_tokens(after(decoder_blocks, encoder_g, small))


    encoder_r1, encoder_c, *encoder_stored = attention_forward(
        "encoder",
        after(place_in, encoder_g),
        encoder_input,
        prefix,
        gains,
        encoder_rel,
        encoder_weights,
    )
    decoder_weights = gather_blocks(jnp.stack(after(decoder_slots, encoder_r1)))
    encoder_c = gather_tokens(encoder_c)
    c_all, g_all, h, du, dc_own, dc_rest = ffn_first(
        "encoder_ffn", encoder_c, encoder_g, encoder_widen, encoder_narrow
    )
    encoder_dc = (dc_own, return_tokens(dc_rest))
    out, *grads = ffn_second(
        "encoder_ffn", None, after(place_in, encoder_dc[1][0]), c_all, g_all, h, du, encoder_narrow
    )
    encoder_out = lax.psum_scatter(out, "mp", scatter_dimension=0, tiled=True)
    decoder_g = gather_tokens(after(decoder_upstream, encoder_dc, out))
    (
        encoder_input_grad,
        encoder_gain_grad,
        keep,
        send,
        encoder_later_grad,
        prefix_grad,
        encoder_bias_raw,
    ) = attention_backward(
        "encoder",
        after(place_in, out),
        (*encoder_dc, encoder_r1),
        encoder_upstream,
        encoder_input,
        gains,
        encoder_stored,
        None,
        encoder_weights,
        encoder_rel,
        encoder_twice,
        encoder_bias.shape[0],
        grads,
    )
    encoder_got = swap_cores(after(send, decoder_g))
    packed = jnp.concatenate([prefix_grad[:prefix_rows], numbers])

    self_r1, _, *self_stored = attention_forward(
        "self", after(place_in, encoder_input_grad), decoder_input, None, gains, decoder_rel, decoder_weights
    )
    encoder_halves = fold_cores(after(keep, self_r1), encoder_got)
    encoder_once = send_once(encoder_halves)
    cross_r2, decoder_c, *cross_stored = attention_forward(
        "cross", after(place_in, encoder_halves), self_r1, encoder_states, gains, None, decoder_weights
    )
    decoder_c = gather_tokens(decoder_c)
    c_all, g_all, h, du, dc_own, dc_rest = ffn_first(
        "decoder_ffn",
        [after(decoder_c[0], encoder_out), *decoder_c[1:]],
        decoder_g,
        decoder_widen,
        decoder_narrow,
    )
    decoder_dc = (dc_own, return_tokens(dc_rest))
    encoder_last = fold_once(after(encoder_halves, decoder_dc[1][0]), encoder_once)
    encoder_twice_got = send_twice(encoder_last)
    out, *rest, keep, send = ffn_second(
        "decoder_ffn", packed, after(place_in, encoder_last), c_all, g_all, h, du, decoder_narrow
    )
    grads = [keep, send]

    decoder_out = [to_mp(part, i + 1) for i, part in enumerate(after(rest, decoder_dc))]

    cross_dx, cross_gain_grad, keep, send, decoder_later_grad, states_grad = attention_backward(
        "cross",
        after(place_in, encoder_twice_got),
        (*decoder_dc, cross_r2),
        decoder_upstream,
        self_r1,
        gains,
        cross_stored,
        encoder_states,
        decoder_weights,
        None,
        None,
        None,
        grads,
    )
    cross_got = swap_cores(after(send, decoder_out))
    encoder_sums = fold_twice(
        after(encoder_halves, cross_dx), encoder_once, encoder_twice_got
    )
    cross_halves = fold_cores(keep, after(cross_got, encoder_sums))
    cross_once = send_once(cross_halves)
    encoder_sent = send_slots(after(encoder_sums, cross_halves))
    tokens = cross_r2.shape[0]
    used = jnp.stack([packed] + [part[tokens:] for part in decoder_out])
    used = lax.all_gather(used, "dp", axis=0, tiled=False).reshape(-1, *packed.shape)
    decoder_input_grad, decoder_gain_grad, keep, send, decoder_bias_raw = attention_backward(
        "self",
        after(place_in, cross_halves),
        None,
        cross_dx,
        decoder_input,
        gains,
        self_stored,
        None,
        decoder_weights,
        decoder_rel,
        decoder_twice,
        decoder_bias.shape[0],
        None,
    )
    self_got = swap_cores(after(send, cross_once, encoder_sent))
    cross_last = fold_once(after(cross_halves, decoder_input_grad), cross_once)
    cross_twice_got = send_twice(cross_last)
    sums = call(
        pack_kernel,
        "pack",
        [
            place_in,
            encoder_gain_grad,
            encoder_later_grad,
            decoder_gain_grad,
            cross_gain_grad,
            decoder_later_grad,
            encoder_bias_raw,
            decoder_bias_raw,
        ],
        (0,),
        (),
        [((64, 128), f32)],
        [],
    )[0]
    self_halves = fold_cores(keep, after(self_got, sums, cross_last))
    self_once = send_once(self_halves)
    encoder_mats = four_matrices(after(encoder_sums, self_halves), encoder_sent)
    encoder_output = (after(encoder_r1, self_halves) + encoder_out.astype(f32)).astype(bf16)
    cross_sums = fold_twice(
        after(cross_halves, encoder_mats, encoder_output), cross_once, cross_twice_got
    )
    cross_sent = send_slots(cross_sums)
    sums = sum_bits("mp", after(sums, cross_sent), 1, lax.axis_size("mp"))
    self_last = fold_once(after(self_halves, cross_sums), self_once)
    self_twice_got = send_twice(self_last)
    self_sums = fold_twice(after(self_halves, sums, cross_sent), self_once, self_twice_got)
    self_sent = send_slots(self_sums)
    sums = sum_bits("dp", after(sums, self_sent[0]), 1, lax.axis_size("dp"))

    def last(value):
        return after(value, self_sums)

    cross_mats = four_matrices(last(cross_sums), cross_sent)
    encoder_widen_grad, encoder_narrow_grad = two_matrices(*last(encoder_sums[4:]))
    table_rows = memory_table.shape[0] // (lax.axis_size("dp") * lax.axis_size("mp"))
    table_grad = call(
        functools.partial(table_kernel, prefix_rows),
        "table",
        [last(place_in), last(used)],
        (0,),
        (),
        [((table_rows, PREFIX, width), f32)],
        [],
    )[0]
    decoder_output = (
        last(cross_r2) + out + sum(part[:tokens].astype(f32) for part in decoder_out)
    ).astype(bf16)
    decoder_widen_grad, decoder_narrow_grad = two_matrices(*last(cross_sums[4:]))
    self_mats = four_matrices(self_sums, self_sent)

    gain_sums = [sums[32 + 6 * i : 38 + 6 * i].reshape(-1) for i in range(5)]
    buckets, heads = encoder_bias.shape
    bias_grads = [sums[:buckets, i * heads : (i + 1) * heads] for i in range(2)]
    return (
        encoder_output,
        encoder_input_grad,
        table_grad,
        bias_grads[0],
        gain_sums[0],
        *encoder_mats,
        gain_sums[1],
        encoder_widen_grad,
        encoder_narrow_grad,
        decoder_output,
        decoder_input_grad,
        states_grad,
        bias_grads[1],
        gain_sums[2],
        *self_mats,
        gain_sums[3],
        *cross_mats,
        gain_sums[4],
        decoder_widen_grad,
        decoder_narrow_grad,
    )


def solution(mesh):
    rows = P(("dp", "mp"), None)
    columns = P(None, "mp")
    lines = P("mp", None)
    attention = (columns, columns, columns, lines)
    in_specs = (
        (rows, rows, P("dp", None), P(), P(), P(), P())
        + attention
        + (P(), columns, lines, rows, rows, rows, P(), P(), P())
        + attention
        + (P(),)
        + attention
        + (P(), columns, lines)
    )
    both = P("dp", "mp")
    turned = P("mp", "dp")
    grads = (both, both, both, turned)
    out_specs = (
        (rows, rows, P(("dp", "mp"), None, None), P(), P())
        + grads
        + (P(), both, turned, rows, rows, rows, P(), P())
        + grads
        + (P(),)
        + grads
        + (P(), both, turned)
    )
    return jax.shard_map(shards, mesh=mesh, in_specs=in_specs, out_specs=out_specs, check_vma=False)
```
